128 devices in a mesh: fsdp: 64 (over z_lo, x, y, core), ctx: 2 (over z_hi).
Axes of the slice: x: 4, y: 4, z: 4 (z_hi: 2, z_lo: 2; z = z_hi * 2 + z_lo), core: 2. Of those that a mesh axis runs over, the one named last changes fastest.
Arguments:
- tokens: bfloat16 [64, 256, 1024], P('fsdp', 'ctx'), may hold values from -16 to 16
- labels: int32 [64], P('fsdp'), may hold values from 0 to 999
- timesteps: int32 [64], P('fsdp'), may hold values from 0 to 999
- cotangent: bfloat16 [64, 256, 1024], P('fsdp', 'ctx'), may hold values from -6 to 6
- class_table: bfloat16 [1000, 1024], P(None, 'fsdp'), may hold values from -6 to 6
- time_weight: bfloat16 [256, 1024], P(None, 'fsdp'), may hold values from -0.375 to 0.375
- modulate_weight: bfloat16 [1, 1024, 6144], P(None, 'fsdp'), may hold values from -0.1875 to 0.1875
- modulate_offset: bfloat16 [1, 6144], P(None, 'fsdp'), may hold values from -3 to 3
- attend_weight: bfloat16 [1, 1024, 3072], P(None, 'fsdp'), may hold values from -0.1875 to 0.1875
- output_weight: bfloat16 [1, 1024, 1024], P(None, 'fsdp'), may hold values from -3 to 3
- expand_weight: bfloat16 [1, 1024, 4096], P(None, 'fsdp'), may hold values from -0.1875 to 0.1875
- hidden_offset: bfloat16 [1, 4096], P(None, 'fsdp'), may hold values from -3 to 3
- contract_weight: bfloat16 [1, 4096, 1024], P(None, 'fsdp'), may hold values from -0.09375 to 0.09375
Outputs:
- result: bfloat16 [64, 256, 1024], P('fsdp', 'ctx')
- tokens_grad: float32 [64, 256, 1024], P('fsdp', 'ctx')
- table_grad: float32 [1000, 1024], P(None, 'fsdp')
- time_grad: float32 [256, 1024], P(None, 'fsdp')
- modulate_grad: float32 [1, 1024, 6144], P(None, 'fsdp')
- offset_grad: float32 [1, 6144], P(None, 'fsdp')
- attend_grad: float32 [1, 1024, 3072], P(None, 'fsdp')
- output_grad: float32 [1, 1024, 1024], P(None, 'fsdp')
- expand_grad: float32 [1, 1024, 4096], P(None, 'fsdp')
- hidden_grad: float32 [1, 4096], P(None, 'fsdp')
- contract_grad: float32 [1, 4096, 1024], P(None, 'fsdp')
The draws below stay inside these ranges and needn't reach their ends.
All inputs are finite; a program needn't handle non-finite values.
Results may differ from the reference program's by a relative error of at most 0.025.
Values may be sent and summed in bfloat16 or wider, within the bound.
A program may use at most 192 MiB of HBM per device.

```python
import math
import jax
import jax.numpy as jnp
from jax import lax

D = 1024
HEADS = 16
HEAD = 64
FF = 4096
CLASSES = 1000
FREQ = 256
LAYERS = 1
SEQ = 256
LATENTS = 64


def set_ends(drawn, own_key, smallest, high):
    dims = drawn.shape
    place = [jax.random.randint(jax.random.fold_in(own_key, axis), (), 0, dims[axis]) for axis in range(len(dims))]
    drawn = drawn.at[tuple(place)].set(smallest)
    longest = dims.index(max(dims))
    place[longest] = (place[longest] + 1) % dims[longest]
    return drawn.at[tuple(place)].set(high)


def raised(values, stream_key, source, target, shards_of, factor):
    owner, partner = [(jnp.arange(values.shape[position]) // (values.shape[position] // shards_of)).reshape([-1 if axis == position else 1 for axis in range(values.ndim)]) for position in (source, target)]
    chosen = jax.random.permutation(stream_key, shards_of)[partner]
    strong = (owner == chosen) | (owner == (partner + shards_of // 2) % shards_of)
    return jnp.where(strong, factor * values, values)


def block_levels(key, extent, cuts, smallest, high):
    loudness, own = 1.0, jax.random.fold_in(key, 6)
    for dim, parts in cuts:
        steps = jnp.exp(jax.random.uniform(jax.random.fold_in(own, dim), (parts,), jnp.float32, smallest / len(cuts), high / len(cuts)))
        loudness = loudness * jnp.repeat(steps, extent[dim] // parts).reshape([-1 if axis == dim else 1 for axis in range(len(extent))])
    return loudness


def centred(rng, extent, deviation, bound, cuts=(), kind=jnp.bfloat16):
    gain = block_levels(rng, extent, cuts, -0.22, 0.18) if cuts else 1.0
    entries = jax.random.normal(rng, extent, jnp.float32) * deviation * gain
    return jnp.minimum(jnp.maximum(entries, -bound), bound).astype(kind)


def noise_with(key, dims, scale, most, cuts, heavy, held_as=jnp.bfloat16):
    values = scale * jax.random.normal(key, dims, jnp.float32)
    if cuts:
        values = values * block_levels(key, dims, cuts, -0.22, 0.18)
    return jnp.clip(raised(values, jax.random.fold_in(key, 3), *heavy), -most, most).astype(held_as)


def setup_inputs(seed: int = 0) -> dict:
    splits = jax.random.split(jax.random.key(seed), 14)
    tokens = noise_with(splits[0], (LATENTS, SEQ, D), 1.0, 16.0, ((0, 64), (1, 2)), (0, 2, 64, 4.0))
    labels = set_ends(jax.random.randint(splits[1], (LATENTS,), 0, CLASSES), jax.random.fold_in(splits[1], 1), 0, CLASSES - 1).astype(jnp.int32)
    timesteps = set_ends(jax.random.randint(splits[2], (LATENTS,), 0, 1000), jax.random.fold_in(splits[2], 1), 0, 999).astype(jnp.int32)
    cotangent = centred(splits[3], (LATENTS, SEQ, D), 1.0, 6.0, ((0, 64), (1, 2)))
    class_table = centred(splits[4], (CLASSES, D), 1.0, 6.0, ((1, 64),))
    time_weight = centred(splits[5], (FREQ, D), FREQ ** -0.5, 0.375, ((1, 64),))
    modulate_weight = centred(splits[6], (LAYERS, D, 6 * D), D ** -0.5, 0.1875, ((1, 64),))
    modulate_offset = centred(splits[7], (LAYERS, 6 * D), 0.5, 3.0, ((1, 64),))
    attend_weight = centred(splits[8], (LAYERS, D, 3 * D), D ** -0.5, 0.1875, ((1, 64),))
    output_weight = centred(splits[9], (LAYERS, D, D), (max(1, D // SEQ)) ** -0.5, 3.0, ((1, 64),))
    expand_weight = centred(splits[10], (LAYERS, D, FF), D ** -0.5, 0.1875, ((1, 64),))
    hidden_offset = centred(splits[11], (LAYERS, FF), 0.5, 3.0, ((1, 64),))
    contract_weight = centred(splits[12], (LAYERS, FF, D), FF ** -0.5, 0.09375, ((1, 64),))
    return {"tokens": tokens, "labels": labels, "timesteps": timesteps, "cotangent": cotangent, "class_table": class_table, "time_weight": time_weight, "modulate_weight": modulate_weight, "modulate_offset": modulate_offset, "attend_weight": attend_weight, "output_weight": output_weight, "expand_weight": expand_weight, "hidden_offset": hidden_offset, "contract_weight": contract_weight}


@jax.custom_vjp
def low(v):
    return lax.optimization_barrier(v.astype(jnp.bfloat16)).astype(jnp.float32)

@jax.custom_vjp
def low_back(v):
    return v

def low_keep(v):
    return (low(v), None)

def low_pass(kept, grad):
    return (grad,)

def back_keep(v):
    return (v, None)

def back_low(kept, grad):
    return (low(grad),)
low.defvjp(low_keep, low_pass)
low_back.defvjp(back_keep, back_low)
HIGHEST = lax.Precision.HIGHEST
EPSILON = 1e-06

def layer_norm(values):
    centre = values - lax.optimization_barrier(jnp.mean(values, -1, keepdims=True))
    spread = lax.optimization_barrier(jnp.mean(centre * centre, -1, keepdims=True))
    return centre * lax.rsqrt(spread + EPSILON)

def sinusoid(step_ids):
    half_width = FREQ // 2
    freq_rates = jnp.exp(-math.log(10000.0) * jnp.arange(half_width, dtype=jnp.float32) / half_width)
    angles = step_ids.astype(jnp.float32)[:, None] * freq_rates[None, :]
    return jnp.concatenate([jnp.cos(angles), jnp.sin(angles)], axis=-1)

def attention(query_heads, key_heads, value_heads):
    scores = low_back(jnp.einsum('bqhd,bkhd->bhqk', query_heads, key_heads, precision=HIGHEST) * HEAD ** (-0.5))
    softmaxed = jax.nn.softmax(scores, axis=-1)
    return jnp.einsum('bhqk,bkhd->bqhd', low(softmaxed), value_heads, precision=HIGHEST)

def forward(group_tokens, group_labels, group_steps, class_table, time_weight, modulate_weight, modulate_offset, attend_weight, output_weight, expand_weight, hidden_offset, contract_weight):
    cond = class_table[group_labels] + jnp.dot(low(sinusoid(group_steps)), time_weight, precision=HIGHEST)
    modulation = low_back(jnp.einsum('bd,ldk->blk', low(jax.nn.silu(cond)), modulate_weight, precision=HIGHEST) + modulate_offset[None])
    hidden = group_tokens
    batch_size, length = (hidden.shape[0], hidden.shape[1])
    for which_layer in range(LAYERS):
        pieces = [modulation[:, which_layer, None, portion * D:(portion + 1) * D] for portion in range(6)]
        shift_one, scale_one, gate_one, shift_two, scale_two, gate_two = pieces
        first_in = low(layer_norm(hidden) * (1.0 + scale_one) + shift_one)
        projected = low(low_back(jnp.einsum('bsd,de->bse', first_in, attend_weight[which_layer], precision=HIGHEST)))
        query_heads = projected[..., :D].reshape(batch_size, length, HEADS, HEAD)
        key_heads = projected[..., D:2 * D].reshape(batch_size, length, HEADS, HEAD)
        value_heads = projected[..., 2 * D:].reshape(batch_size, length, HEADS, HEAD)
        attended = low(low_back(jax.checkpoint(attention)(query_heads, key_heads, value_heads))).reshape(batch_size, length, D)
        branch_one = low_back(jnp.einsum('bsd,de->bse', attended, output_weight[which_layer], precision=HIGHEST))
        middle = hidden + gate_one * branch_one
        second_in = low(layer_norm(middle) * (1.0 + scale_two) + shift_two)
        pre_act = low_back(jnp.einsum('bsd,df->bsf', second_in, expand_weight[which_layer], precision=HIGHEST) + hidden_offset[which_layer])
        activated = low(jax.nn.gelu(pre_act, approximate=True))
        branch_two = low_back(jnp.einsum('bsf,fd->bsd', activated, contract_weight[which_layer], precision=HIGHEST))
        hidden = middle + gate_two * branch_two
    return hidden

def reference(tokens, labels, timesteps, cotangent, class_table, time_weight, modulate_weight, modulate_offset, attend_weight, output_weight, expand_weight, hidden_offset, contract_weight):
    weights = tuple((weight_array.astype(jnp.float32) for weight_array in (class_table, time_weight, modulate_weight, modulate_offset, attend_weight, output_weight, expand_weight, hidden_offset, contract_weight)))
    group_size = math.gcd(LATENTS, max(1, 4096 // SEQ))
    group_count = LATENTS // group_size
    shaped = (group_count, group_size, SEQ, D)
    token_groups = tokens.astype(jnp.float32).reshape(shaped)
    cot_groups = cotangent.astype(jnp.float32).reshape(shaped)
    label_groups = labels.reshape(group_count, group_size)
    step_groups = timesteps.reshape(group_count, group_size)

    def one_group(grad_sums, group_item):
        group_tokens, group_labels, group_steps, group_cot = group_item

        def run_forward(tokens_in, *params):
            return forward(tokens_in, group_labels, group_steps, *params)
        outputs, pull_back = jax.vjp(run_forward, group_tokens, *weights)
        back_terms = pull_back(group_cot)
        grad_sums = tuple((running + addend for running, addend in zip(grad_sums, back_terms[1:])))
        return (grad_sums, (outputs.astype(jnp.bfloat16), back_terms[0]))
    initial = tuple((jnp.zeros(weight_array.shape, jnp.float32) for weight_array in weights))
    grad_sums, (outputs, token_grads) = lax.scan(one_group, initial, (token_groups, label_groups, step_groups, cot_groups))
    table_grad, time_grad, modulate_grad, offset_grad, attend_grad, output_grad, expand_grad, hidden_grad, contract_grad = grad_sums
    result = outputs.reshape(LATENTS, SEQ, D)
    tokens_grad = token_grads.reshape(LATENTS, SEQ, D)
    return (result, tokens_grad, table_grad, time_grad, modulate_grad, offset_grad, attend_grad, output_grad, expand_grad, hidden_grad, contract_grad)
```

```python
import functools
import math

import jax
import jax.numpy as jnp
from jax import lax
from jax.experimental import pallas as pl
from jax.experimental.pallas import tpu as pltpu
from jax.sharding import PartitionSpec as P

D = 1024
HEADS = 16
HEAD = 64
FF = 4096
CLASSES = 1000
FREQ = 256
SEQ = 256
HALF = SEQ // 2

ATTEND = (16, 3 * D, "zyx")
OUTPUT = (16, D, "zyx")
EXPAND = (16, FF, "xzy")
CONTRACT = (64, D, "yxz")
WEIGHTS = (ATTEND, OUTPUT, EXPAND, CONTRACT)

HIGHEST = lax.Precision.HIGHEST
EPSILON = 1e-06
MESH = pl.DeviceIdType.MESH
BF16 = jnp.bfloat16
F32 = jnp.float32


class Place:
    def __init__(self):
        shard = lax.axis_index("fsdp")
        self.z_hi = lax.axis_index("ctx")
        self.core = lax.rem(shard, 2)
        self.z_lo = lax.div(shard, 32)
        self.at = {
            "x": lax.rem(lax.div(shard, 8), 4),
            "y": lax.rem(lax.div(shard, 2), 4),
            "z": 2 * self.z_hi + self.z_lo,
        }

    def step(self, axis, distance):
        return lax.rem(self.at[axis] + distance + 4, 4)

    def device(self, core=None, **moved):
        at = {**self.at, **moved}
        core = self.core if core is None else core
        shard = ((lax.rem(at["z"], 2) * 4 + at["x"]) * 4 + at["y"]) * 2 + core
        return (shard, lax.div(at["z"], 2))

    def along(self, axis, distance):
        return self.device(**{axis: self.step(axis, distance)})

    def other_core(self):
        return self.device(core=1 - self.core)

    def other_z_lo(self):
        return self.device(z=2 * self.z_hi + 1 - self.z_lo)

    def everyone(self):
        ids = [self.other_core()]
        for axis in "xyz":
            ids += [self.along(axis, distance) for distance in (1, 2, 3)]
        return ids


def greet(ids):
    barrier = pltpu.get_barrier_semaphore()
    for device in ids:
        pl.semaphore_signal(barrier, inc=1, device_id=device, device_id_type=MESH)
    pl.semaphore_wait(barrier, len(ids))


class Copies:
    def __init__(self, send_sems, recv_sems, local_sems):
        self.send_sems, self.recv_sems, self.local_sems = send_sems, recv_sems, local_sems
        self.remote, self.local = [], []

    def send(self, source, target, device):
        slot = len(self.remote)
        copy = pltpu.make_async_remote_copy(
            src_ref=source,
            dst_ref=target,
            send_sem=self.send_sems.at[slot],
            recv_sem=self.recv_sems.at[slot],
            device_id=device,
            device_id_type=MESH,
        )
        copy.start()
        self.remote.append(copy)
        return copy

    def move(self, source, target):
        slot = len(self.local)
        copy = pltpu.make_async_copy(source, target, self.local_sems.at[slot])
        copy.start()
        self.local.append(copy)
        return copy

    def drain(self):
        for copy in self.remote:
            copy.wait_send()


def copy_scratch(remote, local):
    return [
        pltpu.SemaphoreType.DMA((remote,)),
        pltpu.SemaphoreType.DMA((remote,)),
        pltpu.SemaphoreType.DMA((max(local, 1),)),
    ]


class Gather:
    def __init__(self, place, copies, source, out, columns, order):
        self.place, self.copies, self.source, self.out = place, copies, source, out
        self.half, self.order = columns // 2, order
        self.done = []
        self.to_core = []

    def region(self, half_index, core, **sel):
        lead = [sel.get(axis) for axis in "xy"]
        lead = [slice(None) if index is None else index for index in lead]
        z = sel.get("z")
        start, width = half_index * self.half, self.half
        z_lo = slice(None)
        if z is not None:
            width = self.half // 2
            start = start + lax.div(z, 2) * width
            z_lo = lax.rem(z, 2)
        core = slice(None) if core is None else core
        return self.out.at[z_lo, lead[0], lead[1], core, :, pl.ds(pl.multiple_of(start, 128), width)]

    def begin(self):
        place = self.place
        quarter = self.half // 2
        mine = place.core * self.half + place.z_hi * quarter
        theirs = (1 - place.core) * self.half + place.z_hi * quarter
        mine, theirs = pl.multiple_of(mine, 128), pl.multiple_of(theirs, 128)
        self.first = self.copies.send(
            self.source.at[:, pl.ds(theirs, quarter)],
            self.region(1 - place.core, place.core, **place.at),
            place.other_core(),
        )
        self.own = self.copies.move(
            self.source.at[:, pl.ds(mine, quarter)], self.region(place.core, place.core, **place.at)
        )

    def ready(self):
        self.first.wait_recv()
        self.own.wait()

    def block(self, axis, index, core):
        sel = {a: self.place.at[a] for a in "xyz" if a not in self.done}
        return self.region(self.place.core, core, **{**sel, axis: index})

    def pass_on(self, phase, index, core):
        if phase == 2:
            piece = self.block(self.order[2], index, core)
            self.to_core.append(self.copies.send(piece, piece, self.place.other_core()))

    def start(self, phase):
        axis, place = self.order[phase], self.place
        self.arriving = {}
        for way, core in ((1, 0), (-1, 1), (1, 1), (-1, 0)):
            piece = self.block(axis, place.at[axis], core)
            self.arriving[way, core] = self.copies.send(piece, piece, place.along(axis, way))
        self.pass_on(phase, place.at[axis], None)

    def forward(self, phase):
        axis, place = self.order[phase], self.place
        self.last = {}
        for way, core in ((1, 0), (-1, 1)):
            self.arriving[way, core].wait_recv()
            piece = self.block(axis, place.step(axis, -way), core)
            self.last[way, core] = self.copies.send(piece, piece, place.along(axis, way))
            self.pass_on(phase, place.step(axis, -way), core)

    def finish(self, phase):
        axis, place = self.order[phase], self.place
        for way, core in ((1, 1), (-1, 0)):
            self.arriving[way, core].wait_recv()
            self.pass_on(phase, place.step(axis, -way), core)
        for way, core in ((1, 0), (-1, 1)):
            self.last[way, core].wait_recv()
            self.pass_on(phase, place.step(axis, 2), core)
        self.done.append(axis)


def add_rows(out, left, right, count):
    def body(i, _):
        out[i] = (left[i].astype(F32) + right[i].astype(F32)).astype(out.dtype)
        return 0

    lax.fori_loop(0, count, body, 0)


def enter_kernel(
    w0, w1, w2, w3, tokens, partial_mod,
    o0, o1, o2, o3, other_tokens, modulation,
    got_core, sum_core, got_z, sum_z, got_x, sum_x, got_y,
    send_sems, recv_sems, local_sems,
):
    place = Place()
    copies = Copies(send_sems, recv_sems, local_sems)
    greet(place.everyone())
    gathers = [
        Gather(place, copies, source, out, spec[1], spec[2])
        for source, out, spec in zip((w0, w1, w2, w3), (o0, o1, o2, o3), WEIGHTS)
    ]
    for gather in gathers:
        gather.begin()
    mod_core = copies.send(
        partial_mod.at[:, :, :, 1 - place.core], got_core, place.other_core()
    )
    for gather in gathers:
        gather.ready()
        gather.start(0)
    tokens_copy = copies.send(tokens, other_tokens, place.along("z", 2))

    mod_core.wait_recv()
    for z_lo in range(2):
        for x in range(4):
            for y in range(4):
                sum_core[z_lo, x, y] = (
                    partial_mod[z_lo, x, y, place.core].astype(F32) + got_core[z_lo, x, y].astype(F32)
                ).astype(BF16)
    mod_z = copies.send(sum_core.at[1 - place.z_lo], got_z, place.other_z_lo())
    for gather in gathers:
        gather.forward(0)
    mod_z.wait_recv()
    for x in range(4):
        for y in range(4):
            sum_z[x, y] = (
                sum_core[place.z_lo, x, y].astype(F32) + got_z[x, y].astype(F32)
            ).astype(BF16)
    mod_x = [
        copies.send(sum_z.at[place.step("x", distance)], got_x.at[distance - 1], place.along("x", distance))
        for distance in (1, 2, 3)
    ]
    for gather in gathers:
        gather.finish(0)
        gather.start(1)
    for copy in mod_x:
        copy.wait_recv()
    for y in range(4):
        total = sum_z[place.at["x"], y].astype(F32)
        for slot in range(3):
            total += got_x[slot, y].astype(F32)
        sum_x[y] = total.astype(BF16)
    mod_y = [
        copies.send(sum_x.at[place.step("y", distance)], got_y.at[distance - 1], place.along("y", distance))
        for distance in (1, 2, 3)
    ]
    for gather in gathers:
        gather.forward(1)
    for copy in mod_y:
        copy.wait_recv()
    total = sum_x[place.at["y"]].astype(F32)
    for slot in range(3):
        total += got_y[slot].astype(F32)
    modulation[...] = total
    for gather in gathers:
        gather.finish(1)
        gather.start(2)
    for gather in gathers:
        gather.forward(2)
    for gather in gathers:
        gather.finish(2)
    tokens_copy.wait_recv()
    for gather in gathers:
        for copy in gather.to_core:
            copy.wait_recv()
    copies.drain()


def enter(weights, tokens, partial_mod):
    anywhere = pl.BlockSpec(memory_space=pl.ANY)
    inside = pl.BlockSpec(memory_space=pltpu.VMEM)
    slab = (48, 128)
    shapes = [jax.ShapeDtypeStruct((2, 4, 4, 2, rows, columns), BF16) for rows, columns, _ in WEIGHTS]
    shapes += [jax.ShapeDtypeStruct((HALF, D), BF16), jax.ShapeDtypeStruct(slab, F32)]
    out = pl.pallas_call(
        enter_kernel,
        out_shape=shapes,
        in_specs=[anywhere] * 5 + [inside],
        out_specs=[anywhere] * 5 + [inside],
        scratch_shapes=[
            pltpu.VMEM((2, 4, 4) + slab, BF16),
            pltpu.VMEM((2, 4, 4) + slab, BF16),
            pltpu.VMEM((4, 4) + slab, BF16),
            pltpu.VMEM((4, 4) + slab, BF16),
            pltpu.VMEM((3, 4) + slab, BF16),
            pltpu.VMEM((4,) + slab, BF16),
            pltpu.VMEM((3,) + slab, BF16),
        ]
        + copy_scratch(4 * 26 + 9, 4),
        compiler_params=pltpu.CompilerParams(
            collective_id=0, has_side_effects=True, vmem_limit_bytes=32 * 2**20
        ),
        name="enter",
    )(*weights, tokens, partial_mod)
    full = [
        whole.reshape(64 * rows, columns) for whole, (rows, columns, _) in zip(out[:4], WEIGHTS)
    ]
    return full, out[4], out[5].reshape(6, D)


class SmallGather:
    def __init__(self, place, copies, whole):
        self.place, self.copies, self.whole = place, copies, whole
        self.waiting = []

    def arrive(self):
        for copy in self.waiting:
            copy.wait_recv()
        self.waiting = []

    def stage(self, which):
        self.arrive()
        place, whole, send = self.place, self.whole, self.copies.send
        at, core = place.at, place.core
        if which == 0:
            piece = whole.at[place.z_lo, at["x"], at["y"], core]
            self.waiting = [send(piece, piece, place.along("y", d)) for d in (1, 2, 3)]
        elif which == 1:
            piece = whole.at[place.z_lo, at["x"], :, core]
            self.waiting = [send(piece, piece, place.along("x", d)) for d in (1, 2, 3)]
        elif which == 2:
            piece = whole.at[place.z_lo, :, :, core]
            self.waiting = [send(piece, piece, place.other_z_lo())]
        else:
            piece = whole.at[:, :, :, core]
            self.waiting = [send(piece, piece, place.other_core())]


def ids_kernel(own, whole, send_sems, recv_sems, local_sems):
    place = Place()
    copies = Copies(send_sems, recv_sems, local_sems)
    whole[place.z_lo, place.at["x"], place.at["y"], place.core] = own[...]
    greet(place.everyone())
    gather = SmallGather(place, copies, whole)
    for which in range(4):
        gather.stage(which)
    gather.arrive()
    copies.drain()


def gather_ids(labels, timesteps):
    inside = pl.BlockSpec(memory_space=pltpu.VMEM)
    lane = lax.broadcasted_iota(jnp.int32, (8, 128), 1)
    own = jnp.where(lane == 0, labels[0], timesteps[0])
    whole = pl.pallas_call(
        ids_kernel,
        out_shape=jax.ShapeDtypeStruct((2, 4, 4, 2, 8, 128), jnp.int32),
        in_specs=[inside],
        out_specs=inside,
        scratch_shapes=copy_scratch(8, 0),
        compiler_params=pltpu.CompilerParams(collective_id=1, has_side_effects=True),
        name="gather_ids",
    )(own).reshape(64, 8, 128)
    return whole[:, 0, 0], whole[:, 0, 1]


def swap_kernel(own, other, send_sems, recv_sems, local_sems):
    place = Place()
    copies = Copies(send_sems, recv_sems, local_sems)
    partner = place.along("z", 2)
    greet([partner])
    copies.send(own, other, partner).wait_recv()
    copies.drain()


def swap(own):
    inside = pl.BlockSpec(memory_space=pltpu.VMEM)
    return pl.pallas_call(
        swap_kernel,
        out_shape=jax.ShapeDtypeStruct(own.shape, own.dtype),
        in_specs=[inside],
        out_specs=inside,
        scratch_shapes=copy_scratch(1, 0),
        compiler_params=pltpu.CompilerParams(collective_id=2, has_side_effects=True),
        name="swap",
    )(own)


class Scatter:
    def __init__(self, place, copies, spec, left, right, lefts, rights, parts, bufs, final, out):
        self.place, self.copies = place, copies
        self.rows, self.columns, self.order = spec[0], spec[1], spec[2][::-1]
        self.left, self.right, self.lefts, self.rights = left, right, lefts, rights
        self.parts, self.bufs, self.final, self.out = parts, bufs, final, out
        self.done = []

    def begin(self):
        place, copies, quarter = self.place, self.copies, self.columns // 4
        self.inputs = [copies.send(self.left, self.lefts.at[pl.ds(HALF, HALF)], place.other_core())]
        for q in range(2):
            start = pl.multiple_of((1 - place.core) * 2 * quarter + q * quarter, 128)
            self.inputs.append(
                copies.send(
                    self.right.at[:, pl.ds(start, quarter)],
                    self.rights.at[q, pl.ds(HALF, HALF)],
                    place.other_core(),
                )
            )
        self.own = [copies.move(self.left, self.lefts.at[pl.ds(0, HALF)])]
        for q in range(2):
            start = pl.multiple_of(place.core * 2 * quarter + q * quarter, 128)
            self.own.append(
                copies.move(self.right.at[:, pl.ds(start, quarter)], self.rights.at[q, pl.ds(0, HALF)])
            )

    def make(self):
        for copy in self.inputs:
            copy.wait_recv()
        for copy in self.own:
            copy.wait()
        rows, quarter = self.rows, self.columns // 4
        chunk = 8 * rows

        def body(i, _):
            q, z_lo, x = lax.div(i, 8), lax.rem(lax.div(i, 4), 2), lax.rem(i, 4)
            start = pl.multiple_of(lax.rem(i, 8) * chunk, 128)
            made = lax.dot_general(
                self.lefts[:, pl.ds(start, chunk)],
                self.rights[q],
                (((0,), (0,)), ((), ())),
                preferred_element_type=F32,
            )
            self.parts[2 * q + z_lo, x] = made.astype(BF16).reshape(4, 2, rows, quarter)
            return 0

        lax.fori_loop(0, 16, body, 0)

    def sel(self, axis, index):
        at = {a: self.place.at[a] if a in self.done else None for a in "xyz"}
        at[axis] = index
        return [at[a] for a in "zxy"]

    def block(self, axis, index, core):
        lead = [slice(None) if i is None else i for i in self.sel(axis, index)]
        return self.parts.at[(*lead, core)]

    def add(self, axis, index, core, bufs):
        sel = self.sel(axis, index)
        free = [i for i, s in enumerate(sel) if s is None]

        def body(step, _):
            where, inner = list(sel), []
            for i in reversed(free):
                where[i] = lax.rem(step, 4)
                inner.insert(0, where[i])
                step = lax.div(step, 4)
            total = self.parts[(*where, core)].astype(F32)
            for buf in bufs:
                total += buf[tuple(inner)].astype(F32)
            self.parts[(*where, core)] = total.astype(BF16)
            return 0

        if free:
            lax.fori_loop(0, 4 ** len(free), body, 0)
        else:
            body(jnp.int32(0), 0)

    def start(self, phase):
        axis, place = self.order[phase], self.place
        buf = self.bufs[phase]
        send = self.copies.send
        up, down = place.along(axis, 1), place.along(axis, -1)
        far = place.step(axis, 2)
        self.far = {
            1: send(self.block(axis, far, 0), buf.at[0], up),
            -1: send(self.block(axis, far, 1), buf.at[1], down),
        }
        self.raw = {
            1: send(self.block(axis, place.step(axis, 1), 1), buf.at[3], up),
            -1: send(self.block(axis, place.step(axis, -1), 0), buf.at[2], down),
        }

    def forward(self, phase):
        axis, place = self.order[phase], self.place
        buf = self.bufs[phase]
        self.near = {}
        for way, core in ((1, 0), (-1, 1)):
            self.far[way].wait_recv()
            index = place.step(axis, way)
            self.add(axis, index, core, [buf.at[core]])
            self.near[way] = self.copies.send(
                self.block(axis, index, core), buf.at[4 + core], place.along(axis, way)
            )

    def finish(self, phase):
        axis, place = self.order[phase], self.place
        buf = self.bufs[phase]
        for way, core in ((1, 0), (-1, 1)):
            self.raw[-way].wait_recv()
            self.near[way].wait_recv()
            self.add(axis, place.at[axis], core, [buf.at[2 + core], buf.at[4 + core]])
        self.done.append(axis)

    def share(self):
        place, at = self.place, self.place.at
        slot = place.core * 2 + place.z_hi
        mine = self.parts.at[at["z"], at["x"], at["y"], place.core]
        theirs = self.parts.at[at["z"], at["x"], at["y"], 1 - place.core]
        far = place.step("z", 2)
        target = self.final.at[slot]
        self.shared = [
            self.copies.send(theirs, target, place.other_core()),
            self.copies.send(mine, target, place.device(z=far)),
            self.copies.send(theirs, target, place.device(z=far, core=1 - place.core)),
        ]
        self.kept = self.copies.move(mine, target)

    def store(self):
        for copy in self.shared:
            copy.wait_recv()
        self.kept.wait()
        quarter = self.columns // 4
        for slot in range(4):
            self.out[:, slot * quarter : (slot + 1) * quarter] = self.final[slot].astype(F32)


LEFTS = (D, D, D, FF)


def leave_kernel(*refs):
    refs = list(refs)

    def take(count):
        taken, refs[:count] = refs[:count], []
        return taken

    lefts_in, rights_in = take(4), take(4)
    (vector,) = take(1)
    outs = take(4)
    (whole,) = take(1)
    lefts, rights, parts = take(4), take(4), take(4)
    bufs = [take(3) for _ in range(4)]
    finals = take(4)
    (vector_got,) = take(1)
    send_sems, recv_sems, local_sems = refs
    place = Place()
    copies = Copies(send_sems, recv_sems, local_sems)
    far = place.step("z", 2)
    greet(place.everyone() + [place.device(z=far, core=1 - place.core)])
    scatters = [
        Scatter(place, copies, WEIGHTS[i], lefts_in[i], rights_in[i], lefts[i], rights[i], parts[i], bufs[i], finals[i], outs[i])
        for i in (3, 2, 0, 1)
    ]
    for scatter in scatters:
        scatter.begin()
    vector_copy = copies.send(vector, vector_got, place.along("z", 2))
    for scatter in scatters:
        scatter.make()
        scatter.start(0)
    vector_copy.wait_recv()
    whole[place.z_lo, place.at["x"], place.at["y"], place.core] = (
        vector[...].astype(F32) + vector_got[...].astype(F32)
    ).astype(BF16)
    gather = SmallGather(place, copies, whole)
    gather.stage(0)
    for scatter in scatters:
        scatter.forward(0)
    gather.stage(1)
    for scatter in scatters:
        scatter.finish(0)
        scatter.start(1)
    gather.stage(2)
    for scatter in scatters:
        scatter.forward(1)
    gather.stage(3)
    for scatter in scatters:
        scatter.finish(1)
        scatter.start(2)
    for scatter in scatters:
        scatter.forward(2)
    for scatter in scatters:
        scatter.finish(2)
        scatter.share()
    gather.arrive()
    for scatter in scatters:
        scatter.store()
    copies.drain()


def buffer_shapes(rows, columns, order):
    shapes = []
    for left in (2, 1, 0):
        shapes.append(pltpu.VMEM((6,) + (4,) * left + (rows, columns // 4), BF16))
    return shapes


def leave(lefts, rights, vector):
    anywhere = pl.BlockSpec(memory_space=pl.ANY)
    inside = pl.BlockSpec(memory_space=pltpu.VMEM)
    scratch = [pltpu.VMEM((SEQ, width), BF16) for width in LEFTS]
    scratch += [pltpu.VMEM((2, SEQ, columns // 4), BF16) for _, columns, _ in WEIGHTS]
    scratch += [pltpu.VMEM((4, 4, 4, 2, rows, columns // 4), BF16) for rows, columns, _ in WEIGHTS]
    for spec in WEIGHTS:
        scratch += buffer_shapes(*spec)
    scratch += [pltpu.VMEM((4, rows, columns // 4), BF16) for rows, columns, _ in WEIGHTS]
    scratch += [pltpu.VMEM(vector.shape, BF16)]
    scratch += copy_scratch(4 * 24 + 9, 16)
    return pl.pallas_call(
        leave_kernel,
        out_shape=[jax.ShapeDtypeStruct((rows, columns), F32) for rows, columns, _ in WEIGHTS]
        + [jax.ShapeDtypeStruct((2, 4, 4, 2) + vector.shape, BF16)],
        in_specs=[anywhere] * 8 + [inside],
        out_specs=[inside] * 5,
        scratch_shapes=scratch,
        compiler_params=pltpu.CompilerParams(
            collective_id=3, has_side_effects=True, vmem_limit_bytes=56 * 2**20
        ),
        name="leave",
    )(*lefts, *rights, vector)


def normalize(values):
    centre = values - jnp.mean(values, -1, keepdims=True)
    spread = jnp.mean(centre * centre, -1, keepdims=True)
    return centre * lax.rsqrt(spread + EPSILON)


def modulated(values, shift_vec, scale_vec):
    return normalize(values) * (1.0 + scale_vec) + shift_vec


def gelu_tanh(values):
    return jax.nn.gelu(values, approximate=True)


def sinusoid(step_ids):
    half_width = FREQ // 2
    freq_rates = jnp.exp(
        -math.log(10000.0) * jnp.arange(half_width, dtype=jnp.float32) / half_width
    )
    angles = step_ids.astype(jnp.float32)[:, None] * freq_rates[None, :]
    return jnp.concatenate([jnp.cos(angles), jnp.sin(angles)], axis=-1)


def head_split(rows_in):
    return rows_in.reshape(rows_in.shape[0], HEADS, HEAD)


def attend_scores(query_rows, key_rows):
    return jnp.einsum(
        "qhd,khd->hqk",
        head_split(query_rows),
        head_split(key_rows),
        preferred_element_type=F32,
    ) * HEAD ** (-0.5)


def per_device(
    tokens,
    labels,
    timesteps,
    cotangent,
    class_table,
    time_weight,
    modulate_weight,
    modulate_offset,
    attend_weight,
    output_weight,
    expand_weight,
    hidden_offset,
    contract_weight,
):
    shard_index = lax.axis_index("fsdp")
    token_half = lax.axis_index("ctx")
    all_labels, all_steps = gather_ids(labels, timesteps)
    onehot = all_labels[:, None] == jnp.arange(CLASSES, dtype=jnp.int32)[None, :]
    sinus_rows = sinusoid(all_steps).astype(BF16)
    cond_cols = jnp.dot(
        onehot.astype(BF16), class_table, preferred_element_type=F32
    ) + jnp.dot(sinus_rows, time_weight, preferred_element_type=F32)
    offset_width = modulate_offset.shape[1]
    act_cols = jax.nn.silu(cond_cols).astype(BF16)
    partial_mod = jnp.dot(act_cols, modulate_weight[0], preferred_element_type=F32)
    placed = lax.dynamic_update_slice(
        jnp.zeros((1, 6 * D), F32),
        modulate_offset.astype(F32),
        (jnp.int32(0), shard_index * offset_width),
    )
    partial_mod = (partial_mod + placed).astype(BF16).reshape(2, 4, 4, 2, 48, 128)
    (w_attend, w_output, w_expand, w_contract), other_tokens, modulation = enter(
        (attend_weight[0], output_weight[0], expand_weight[0], contract_weight[0]),
        tokens[0],
        partial_mod,
    )
    b_hidden = lax.all_gather(hidden_offset[0], "fsdp", axis=0, tiled=True)
    shift_one, scale_one, gate_one, shift_two, scale_two, gate_two = [modulation[i] for i in range(6)]

    hidden = tokens[0].astype(F32)
    both_hidden = jnp.concatenate([tokens[0], other_tokens], 0).astype(F32)
    both_first = modulated(both_hidden, shift_one, scale_one).astype(BF16)
    first_in = both_first[:HALF]
    projected = jnp.dot(both_first, w_attend, preferred_element_type=F32).astype(BF16)
    query_rows, key_rows, value_rows = projected[:, :D], projected[:, D : 2 * D], projected[:, 2 * D :]
    scores = attend_scores(query_rows, key_rows)
    top_score = jnp.max(scores, -1, keepdims=True)
    exp_terms = jnp.exp(scores - top_score)
    totals = jnp.sum(exp_terms, -1, keepdims=True)
    softmaxed = exp_terms / totals
    rounded_probs = softmaxed.astype(BF16)
    attended = (
        jnp.einsum(
            "hqk,khd->qhd", rounded_probs[:, :HALF], head_split(value_rows), preferred_element_type=F32
        )
        .reshape(-1, D)
        .astype(BF16)
    )
    branch_one = jnp.dot(attended, w_output, preferred_element_type=F32)
    middle = hidden + gate_one * branch_one
    second_in = modulated(middle, shift_two, scale_two).astype(BF16)
    pre_act = jnp.dot(second_in, w_expand, preferred_element_type=F32) + b_hidden.astype(F32)
    activated = gelu_tanh(pre_act).astype(BF16)
    branch_two = jnp.dot(activated, w_contract, preferred_element_type=F32)
    result = (middle + gate_two * branch_two).astype(BF16)[None]

    grad_hidden = cotangent[0].astype(F32)
    grad_two = (grad_hidden * gate_two).astype(BF16)
    gate_two_grad = jnp.sum(grad_hidden * branch_two, 0)
    grad_act = jnp.einsum("td,fd->tf", grad_two, w_contract, preferred_element_type=F32)
    _, gelu_pull = jax.vjp(gelu_tanh, pre_act)
    grad_pre = gelu_pull(grad_act)[0].astype(BF16)
    hidden_term = jnp.sum(grad_pre.astype(F32), 0)
    grad_second = jnp.einsum("tf,df->td", grad_pre, w_expand, preferred_element_type=F32)
    _, second_pull = jax.vjp(modulated, middle, shift_two, scale_two)
    grad_middle, shift_two_grad, scale_two_grad = second_pull(grad_second)
    grad_middle = grad_hidden + grad_middle
    grad_one = (grad_middle * gate_one).astype(BF16)
    gate_one_grad = jnp.sum(grad_middle * branch_one, 0)
    grad_att = jnp.einsum("te,de->td", grad_one, w_output, preferred_element_type=F32).astype(BF16)
    both_att = jnp.concatenate([grad_att, swap(grad_att)], 0)
    grad_heads = head_split(both_att)
    grad_probs = jnp.einsum(
        "qhd,khd->hqk", grad_heads, head_split(value_rows), preferred_element_type=F32
    )
    grad_scores = (
        softmaxed * (grad_probs - jnp.sum(softmaxed * grad_probs, -1, keepdims=True))
    ).astype(BF16)
    grad_query = jnp.einsum(
        "hqk,khd->qhd", grad_scores[:, :HALF], head_split(key_rows), preferred_element_type=F32
    ) * HEAD ** (-0.5)
    grad_key = jnp.einsum(
        "hqk,qhd->khd", grad_scores[:, :, :HALF], head_split(query_rows), preferred_element_type=F32
    ) * HEAD ** (-0.5)
    grad_value = jnp.einsum(
        "hqk,qhd->khd", rounded_probs[:, :, :HALF], grad_heads, preferred_element_type=F32
    )
    grad_proj = jnp.concatenate(
        [part.reshape(-1, D).astype(BF16) for part in (grad_query, grad_key, grad_value)], 1
    )
    grad_first = jnp.einsum("te,de->td", grad_proj, w_attend, preferred_element_type=F32)
    _, first_pull = jax.vjp(modulated, hidden, shift_one, scale_one)
    grad_input, shift_one_grad, scale_one_grad = first_pull(grad_first)
    tokens_grad = (grad_middle + grad_input)[None]

    vector = jnp.concatenate(
        [
            shift_one_grad,
            scale_one_grad,
            gate_one_grad,
            shift_two_grad,
            scale_two_grad,
            gate_two_grad,
            hidden_term,
        ]
    )
    vector = vector.astype(BF16).reshape(80, 128)
    attend_grad, output_grad, expand_grad, contract_grad, all_vectors = leave(
        (first_in, attended, second_in, activated), (grad_proj, grad_one, grad_pre, grad_two), vector
    )
    all_vectors = all_vectors.reshape(64, 80 * 128)
    all_mod = all_vectors[:, : 6 * D]
    own_hidden = lax.dynamic_slice_in_dim(all_vectors, 6 * D + shard_index * (FF // 64), FF // 64, 1)
    hidden_grad = jnp.sum(own_hidden.astype(F32), 0)
    grad_act_cols = jnp.einsum("bk,dk->bd", all_mod, modulate_weight[0], preferred_element_type=F32)
    modulate_grad = jnp.einsum("bd,bk->dk", act_cols, all_mod, preferred_element_type=F32)
    own_cols = lax.dynamic_slice_in_dim(all_mod, shard_index * offset_width, offset_width, 1)
    offset_grad = jnp.sum(own_cols.astype(F32), 0)
    _, silu_pull = jax.vjp(jax.nn.silu, cond_cols)
    grad_cond = silu_pull(grad_act_cols)[0]
    table_grad = jnp.einsum("bc,bd->cd", onehot.astype(F32), grad_cond, precision=HIGHEST)
    time_grad = jnp.einsum("bf,bd->fd", sinus_rows.astype(F32), grad_cond, precision=HIGHEST)
    return (
        result,
        tokens_grad,
        table_grad,
        time_grad,
        modulate_grad[None],
        offset_grad[None],
        attend_grad[None],
        output_grad[None],
        expand_grad[None],
        hidden_grad[None],
        contract_grad[None],
    )


def solution(mesh):
    rows = P(None, "fsdp", None)
    columns = P(None, "fsdp")
    halves = P("fsdp", "ctx", None)
    each = P("fsdp")
    in_specs = (
        halves, each, each, halves, columns, columns, rows, columns, rows, rows, rows, columns, rows,
    )
    out_specs = (
        halves, halves, columns, columns, rows, columns, rows, rows, rows, columns, rows,
    )
    return jax.shard_map(
        per_device, mesh=mesh, in_specs=in_specs, out_specs=out_specs, check_vma=False
    )
```

```python
import functools
import math

import jax
import jax.numpy as jnp
from jax import lax
from jax.experimental import pallas as pl
from jax.experimental.pallas import tpu as pltpu
from jax.sharding import PartitionSpec as P

D = 1024
HEADS = 16
HEAD = 64
FF = 4096
CLASSES = 1000
FREQ = 256
SEQ = 256
HALF = SEQ // 2

WEIGHTS = ((16, 3 * D), (16, D), (16, FF), (64, D))
ORDERS = ("zyx", "xzy", "yxz")
WAVES = tuple(
    tuple((weight, row, column, order) for (weight, row, column), order in zip(wave, ORDERS))
    for wave in (
        ((0, 0, 0), (0, 0, D), (0, 0, 2 * D)),
        ((1, 0, 0), (2, 0, 0), (2, 0, D)),
        ((2, 0, 2 * D), (2, 0, 3 * D), (3, 0, 0)),
        ((3, 16, 0), (3, 32, 0), (3, 48, 0)),
    )
)
UNITS = tuple(unit for wave in WAVES for unit in wave)
QUARTER = D // 4

HIGHEST = lax.Precision.HIGHEST
EPSILON = 1e-06
MESH = pl.DeviceIdType.MESH
BF16 = jnp.bfloat16
F32 = jnp.float32
NT = (((1,), (1,)), ((), ()))
TN = (((0,), (0,)), ((), ()))


class Place:
    def __init__(self):
        shard = lax.axis_index("fsdp")
        self.z_hi = lax.axis_index("ctx")
        self.core = lax.rem(shard, 2)
        self.z_lo = lax.div(shard, 32)
        self.at = {
            "x": lax.rem(lax.div(shard, 8), 4),
            "y": lax.rem(lax.div(shard, 2), 4),
            "z": 2 * self.z_hi + self.z_lo,
        }

    def step(self, axis, distance):
        return lax.rem(self.at[axis] + distance + 4, 4)

    def device(self, core=None, **moved):
        at = {**self.at, **moved}
        core = self.core if core is None else core
        shard = ((lax.rem(at["z"], 2) * 4 + at["x"]) * 4 + at["y"]) * 2 + core
        return (shard, lax.div(at["z"], 2))

    def along(self, axis, distance):
        return self.device(**{axis: self.step(axis, distance)})

    def other_core(self):
        return self.device(core=1 - self.core)

    def other_z_lo(self):
        return self.device(z=2 * self.z_hi + 1 - self.z_lo)

    def everyone(self):
        ids = [self.other_core()]
        for axis in "xyz":
            ids += [self.along(axis, distance) for distance in (1, 2, 3)]
        return ids


def greet(ids):
    barrier = pltpu.get_barrier_semaphore()
    for device in ids:
        pl.semaphore_signal(barrier, inc=1, device_id=device, device_id_type=MESH)
    pl.semaphore_wait(barrier, len(ids))


class Copies:
    def __init__(self, send_sems, recv_sems, local_sems):
        self.send_sems, self.recv_sems, self.local_sems = send_sems, recv_sems, local_sems
        self.remote, self.local = [], []

    def send(self, source, target, device):
        slot = len(self.remote)
        copy = pltpu.make_async_remote_copy(
            src_ref=source,
            dst_ref=target,
            send_sem=self.send_sems.at[slot],
            recv_sem=self.recv_sems.at[slot],
            device_id=device,
            device_id_type=MESH,
        )
        copy.start()
        self.remote.append(copy)
        return copy

    def move(self, source, target):
        slot = len(self.local)
        copy = pltpu.make_async_copy(source, target, self.local_sems.at[slot])
        copy.start()
        self.local.append(copy)
        return copy

    def drain(self):
        for copy in self.remote:
            copy.wait_send()


def copy_scratch(remote, local):
    return [
        pltpu.SemaphoreType.DMA((remote,)),
        pltpu.SemaphoreType.DMA((remote,)),
        pltpu.SemaphoreType.DMA((max(local, 1),)),
    ]


class Gather:
    def __init__(self, place, copies, source, out, unit, direct):
        self.place, self.copies, self.source, self.out = place, copies, source, out
        self.direct = direct
        _, self.row, self.column, self.order = unit
        self.done = []
        self.to_core = []

    def region(self, half_index, core, **sel):
        lead = [sel.get(axis) for axis in "xy"]
        lead = [slice(None) if index is None else index for index in lead]
        z = sel.get("z")
        start, width = self.column + half_index * 2 * QUARTER, 2 * QUARTER
        z_lo = slice(None)
        if z is not None:
            width = QUARTER
            start = start + lax.div(z, 2) * QUARTER
            z_lo = lax.rem(z, 2)
        core = slice(None) if core is None else core
        rows = pl.ds(self.row, 16)
        return self.out.at[z_lo, lead[0], lead[1], core, rows, pl.ds(pl.multiple_of(start, 128), width)]

    def begin(self):
        place = self.place
        mine = self.column + (place.core * 2 + place.z_hi) * QUARTER
        theirs = self.column + ((1 - place.core) * 2 + place.z_hi) * QUARTER
        mine, theirs = pl.multiple_of(mine, 128), pl.multiple_of(theirs, 128)
        rows = pl.ds(self.row, 16)
        self.first = self.copies.send(
            self.source.at[rows, pl.ds(theirs, QUARTER)],
            self.region(1 - place.core, place.core, **place.at),
            place.other_core(),
        )
        self.own = self.copies.move(
            self.source.at[rows, pl.ds(mine, QUARTER)], self.region(place.core, place.core, **place.at)
        )

    def ready(self):
        self.first.wait_recv()
        self.own.wait()

    def block(self, axis, index, core):
        sel = {a: self.place.at[a] for a in "xyz" if a not in self.done}
        return self.region(self.place.core, core, **{**sel, axis: index})

    def pass_on(self, phase, index, core):
        if phase == 2:
            piece = self.block(self.order[2], index, core)
            self.to_core.append(self.copies.send(piece, piece, self.place.other_core()))

    def start(self, phase):
        axis, place = self.order[phase], self.place
        self.arriving = {}
        if phase in self.direct:
            piece = self.block(axis, place.at[axis], None)
            for distance in (1, 3, 2):
                self.arriving[distance] = self.copies.send(piece, piece, place.along(axis, distance))
            return
        for way, core in ((1, 0), (-1, 1), (1, 1), (-1, 0)):
            piece = self.block(axis, place.at[axis], core)
            self.arriving[way, core] = self.copies.send(piece, piece, place.along(axis, way))
        self.pass_on(phase, place.at[axis], None)

    def forward(self, phase):
        axis, place = self.order[phase], self.place
        self.last = {}
        for way, core in ((1, 0), (-1, 1)):
            self.arriving[way, core].wait_recv()
            piece = self.block(axis, place.step(axis, -way), core)
            self.last[way, core] = self.copies.send(piece, piece, place.along(axis, way))
            self.pass_on(phase, place.step(axis, -way), core)

    def finish(self, phase):
        axis, place = self.order[phase], self.place
        self.done.append(axis)
        if phase in self.direct:
            for copy in self.arriving.values():
                copy.wait_recv()
            return
        self.done.pop()
        for way, core in ((1, 1), (-1, 0)):
            self.arriving[way, core].wait_recv()
            self.pass_on(phase, place.step(axis, -way), core)
        for way, core in ((1, 0), (-1, 1)):
            self.last[way, core].wait_recv()
            self.pass_on(phase, place.step(axis, 2), core)
        self.done.append(axis)


def enter_kernel(
    w0, w1, w2, w3, tokens, partial_mod,
    o0, o1, o2, o3, other_tokens, modulation,
    got_core, sum_core, got_z, sum_z, got_x, sum_x, got_y,
    send_sems, recv_sems, local_sems,
):
    place = Place()
    copies = Copies(send_sems, recv_sems, local_sems)
    greet(place.everyone())
    sources, wholes = (w0, w1, w2, w3), (o0, o1, o2, o3)
    waves = [
        [
            Gather(place, copies, sources[unit[0]], wholes[unit[0]], unit, (0, 1) if index == 0 else (0,))
            for unit in wave
        ]
        for index, wave in enumerate(WAVES)
    ]
    gathers = [gather for wave in waves for gather in wave]

    def start(wave, phase):
        for gather in waves[wave]:
            gather.start(phase)

    def forward(wave, phase):
        for gather in waves[wave]:
            gather.forward(phase)

    def finish(wave, phase):
        for gather in waves[wave]:
            gather.finish(phase)

    tokens_copy = copies.send(tokens, other_tokens, place.along("z", 2))
    for gather in gathers:
        gather.begin()
    mod_core = copies.send(
        partial_mod.at[:, :, :, 1 - place.core], got_core, place.other_core()
    )
    for gather in gathers:
        gather.ready()
        gather.start(0)
    mod_core.wait_recv()
    for z_lo in range(2):
        for x in range(4):
            for y in range(4):
                sum_core[z_lo, x, y] = (
                    partial_mod[z_lo, x, y, place.core].astype(F32) + got_core[z_lo, x, y].astype(F32)
                ).astype(BF16)
    mod_z = copies.send(sum_core.at[1 - place.z_lo], got_z, place.other_z_lo())
    for wave in range(4):
        finish(wave, 0)
        start(wave, 1)
    mod_z.wait_recv()
    for x in range(4):
        for y in range(4):
            sum_z[x, y] = (
                sum_core[place.z_lo, x, y].astype(F32) + got_z[x, y].astype(F32)
            ).astype(BF16)
    mod_x = [
        copies.send(sum_z.at[place.step("x", distance)], got_x.at[distance - 1], place.along("x", distance))
        for distance in (1, 2, 3)
    ]
    finish(0, 1)
    start(0, 2)
    for wave in (1, 2, 3):
        forward(wave, 1)
    for copy in mod_x:
        copy.wait_recv()
    for y in range(4):
        total = sum_z[place.at["x"], y].astype(F32)
        for slot in range(3):
            total += got_x[slot, y].astype(F32)
        sum_x[y] = total.astype(BF16)
    mod_y = [
        copies.send(sum_x.at[place.step("y", distance)], got_y.at[distance - 1], place.along("y", distance))
        for distance in (1, 2, 3)
    ]
    finish(1, 1)
    start(1, 2)
    finish(2, 1)
    forward(0, 2)
    start(2, 2)
    for copy in mod_y:
        copy.wait_recv()
    total = sum_x[place.at["y"]].astype(F32)
    for slot in range(3):
        total += got_y[slot].astype(F32)
    modulation[...] = total
    finish(3, 1)
    forward(1, 2)
    start(3, 2)
    finish(0, 2)
    forward(2, 2)
    finish(1, 2)
    forward(3, 2)
    finish(2, 2)
    finish(3, 2)
    tokens_copy.wait_recv()
    for gather in gathers:
        for copy in gather.to_core:
            copy.wait_recv()
    copies.drain()


def enter(weights, tokens, partial_mod):
    anywhere = pl.BlockSpec(memory_space=pl.ANY)
    inside = pl.BlockSpec(memory_space=pltpu.VMEM)
    slab = (48, 128)
    shapes = [jax.ShapeDtypeStruct((2, 4, 4, 2, rows, columns), BF16) for rows, columns in WEIGHTS]
    shapes += [jax.ShapeDtypeStruct((HALF, D), BF16), jax.ShapeDtypeStruct(slab, F32)]
    out = pl.pallas_call(
        enter_kernel,
        out_shape=shapes,
        in_specs=[anywhere] * 5 + [inside],
        out_specs=[anywhere] * 5 + [inside],
        scratch_shapes=[
            pltpu.VMEM((2, 4, 4) + slab, BF16),
            pltpu.VMEM((2, 4, 4) + slab, BF16),
            pltpu.VMEM((4, 4) + slab, BF16),
            pltpu.VMEM((4, 4) + slab, BF16),
            pltpu.VMEM((3, 4) + slab, BF16),
            pltpu.VMEM((4,) + slab, BF16),
            pltpu.VMEM((3,) + slab, BF16),
        ]
        + copy_scratch(12 * 23 + 9, 12),
        compiler_params=pltpu.CompilerParams(
            collective_id=0, has_side_effects=True, vmem_limit_bytes=32 * 2**20
        ),
        name="enter",
    )(*weights, tokens, partial_mod)
    full = [
        whole.reshape(64 * rows, columns) for whole, (rows, columns) in zip(out[:4], WEIGHTS)
    ]
    return full, out[4], out[5].reshape(6, D)


class SmallGather:
    def __init__(self, place, copies, whole):
        self.place, self.copies, self.whole = place, copies, whole
        self.waiting = []

    def arrive(self):
        for copy in self.waiting:
            copy.wait_recv()
        self.waiting = []

    def stage(self, which):
        self.arrive()
        place, whole, send = self.place, self.whole, self.copies.send
        at, core = place.at, place.core
        if which == 0:
            piece = whole.at[place.z_lo, at["x"], at["y"], core]
            self.waiting = [send(piece, piece, place.along("y", d)) for d in (1, 2, 3)]
        elif which == 1:
            piece = whole.at[place.z_lo, at["x"], :, core]
            self.waiting = [send(piece, piece, place.along("x", d)) for d in (1, 2, 3)]
        elif which == 2:
            piece = whole.at[place.z_lo, :, :, core]
            self.waiting = [send(piece, piece, place.other_z_lo())]
        else:
            piece = whole.at[:, :, :, core]
            self.waiting = [send(piece, piece, place.other_core())]


def ids_kernel(own, whole, send_sems, recv_sems, local_sems):
    place = Place()
    copies = Copies(send_sems, recv_sems, local_sems)
    whole[place.z_lo, place.at["x"], place.at["y"], place.core] = own[...]
    greet(place.everyone())
    gather = SmallGather(place, copies, whole)
    for which in range(4):
        gather.stage(which)
    gather.arrive()
    copies.drain()


def gather_ids(labels, timesteps, offsets):
    inside = pl.BlockSpec(memory_space=pltpu.VMEM)
    lane = lax.broadcasted_iota(jnp.int32, (7, 128), 1)
    ids = jnp.where(lane == 0, labels[0], timesteps[0]).astype(F32)
    own = jnp.concatenate([jnp.pad(offsets.astype(F32)[None], ((0, 0), (0, 64))), ids], 0)
    whole = pl.pallas_call(
        ids_kernel,
        out_shape=jax.ShapeDtypeStruct((2, 4, 4, 2, 8, 128), F32),
        in_specs=[inside],
        out_specs=inside,
        scratch_shapes=copy_scratch(8, 0),
        compiler_params=pltpu.CompilerParams(collective_id=1, has_side_effects=True),
        name="gather_ids",
    )(own).reshape(64, 8, 128)
    ids = whole[:, 1, :2].astype(jnp.int32)
    return ids[:, 0], ids[:, 1], whole[:, 0, :64].reshape(FF)


class Pair:
    def __init__(self, place, copies, source, both, blocks=None):
        self.copies = []
        other = place.other_core()
        if blocks is None:
            self.copies.append(copies.send(source, both.at[pl.ds(HALF, HALF)], other))
            self.copies.append(copies.move(source, both.at[pl.ds(0, HALF)]))
            return
        for block in range(blocks):
            mine = pl.multiple_of(block * D + place.core * 2 * QUARTER, 128)
            theirs = pl.multiple_of(block * D + (1 - place.core) * 2 * QUARTER, 128)
            width = 2 * QUARTER
            self.copies.append(
                copies.send(source.at[:, pl.ds(theirs, width)], both.at[block, pl.ds(HALF, HALF)], other)
            )
            self.copies.append(
                copies.move(source.at[:, pl.ds(mine, width)], both.at[block, pl.ds(0, HALF)])
            )

    def wait(self):
        for index, copy in enumerate(self.copies):
            if index % 2:
                copy.wait()
            else:
                copy.wait_recv()


def make_parts(left, right, scatters):
    def body(i, _):
        z_lo, x = lax.div(i, 4), lax.rem(i, 4)
        chosen = left[:, pl.ds(pl.multiple_of(i * 128, 128), 128)]
        for scatter in scatters:
            made = lax.dot_general(
                chosen, right[scatter.column // D], TN, preferred_element_type=F32
            ).astype(BF16)
            for q in range(2):
                scatter.parts[2 * q + z_lo, x] = made[:, q * QUARTER : (q + 1) * QUARTER].reshape(
                    4, 2, 16, QUARTER
                )
        return 0

    lax.fori_loop(0, 8, body, 0)


def make_tall_parts(left, right, scatters):
    def body(i, _):
        z_lo, x = lax.div(i, 4), lax.rem(i, 4)
        chosen = left[:, pl.ds(pl.multiple_of(i * 512, 128), 512)]
        made = lax.dot_general(chosen, right[0], TN, preferred_element_type=F32).astype(BF16)
        made = made.reshape(4, 2, 64, 2 * QUARTER)
        for scatter in scatters:
            rows = made[:, :, scatter.row : scatter.row + 16]
            for q in range(2):
                scatter.parts[2 * q + z_lo, x] = rows[..., q * QUARTER : (q + 1) * QUARTER]
        return 0

    lax.fori_loop(0, 8, body, 0)


class Scatter:
    def __init__(self, place, copies, unit, parts, bufs, final, out):
        self.place, self.copies = place, copies
        _, self.row, self.column, order = unit
        self.order = order[::-1]
        self.parts, self.bufs, self.final, self.out = parts, bufs, final, out
        self.done = []

    def sel(self, axis, index):
        at = {a: self.place.at[a] if a in self.done else None for a in "xyz"}
        at[axis] = index
        return [at[a] for a in "zxy"]

    def block(self, axis, index, core):
        lead = [slice(None) if i is None else i for i in self.sel(axis, index)]
        return self.parts.at[(*lead, core)]

    def add(self, axis, index, core, bufs):
        sel = self.sel(axis, index)
        free = [i for i, s in enumerate(sel) if s is None]

        def body(step, _):
            where = [slice(None) if s is None else s for s in sel]
            inner = (slice(None),) * len(free)
            if len(free) == 2:
                where[free[0]], inner = step, (step, slice(None))
            if core is not None:
                where.append(core)
            total = self.parts[tuple(where)].astype(F32)
            for buf in bufs:
                total += buf[inner].astype(F32)
            self.parts[tuple(where)] = total.astype(BF16)
            return 0

        if len(free) == 2:
            lax.fori_loop(0, 4, body, 0)
        else:
            body(0, 0)

    def start(self, phase):
        axis, place = self.order[phase], self.place
        buf = self.bufs[phase]
        send = self.copies.send
        if phase > 0:
            self.direct = [
                send(
                    self.block(axis, place.step(axis, distance), slice(None)),
                    buf.at[distance - 1],
                    place.along(axis, distance),
                )
                for distance in (1, 3, 2)
            ]
            return
        up, down = place.along(axis, 1), place.along(axis, -1)
        far = place.step(axis, 2)
        self.far = {
            1: send(self.block(axis, far, 0), buf.at[0], up),
            -1: send(self.block(axis, far, 1), buf.at[1], down),
        }
        self.raw = {
            1: send(self.block(axis, place.step(axis, 1), 1), buf.at[3], up),
            -1: send(self.block(axis, place.step(axis, -1), 0), buf.at[2], down),
        }

    def forward(self):
        axis, place = self.order[0], self.place
        buf = self.bufs[0]
        self.near = {}
        for way, core in ((1, 0), (-1, 1)):
            self.far[way].wait_recv()
            index = place.step(axis, way)
            self.add(axis, index, core, [buf.at[core]])
            self.near[way] = self.copies.send(
                self.block(axis, index, core), buf.at[4 + core], place.along(axis, way)
            )

    def finish(self, phase):
        axis, place = self.order[phase], self.place
        buf = self.bufs[phase]
        if phase > 0:
            for copy in self.direct:
                copy.wait_recv()
            self.add(axis, place.at[axis], None, [buf.at[slot] for slot in range(3)])
        else:
            for way, core in ((1, 0), (-1, 1)):
                self.raw[-way].wait_recv()
                self.near[way].wait_recv()
                self.add(axis, place.at[axis], core, [buf.at[2 + core], buf.at[4 + core]])
        self.done.append(axis)

    def share(self):
        place, at = self.place, self.place.at
        slot = place.core * 2 + place.z_hi
        mine = self.parts.at[at["z"], at["x"], at["y"], place.core]
        theirs = self.parts.at[at["z"], at["x"], at["y"], 1 - place.core]
        far = place.step("z", 2)
        target = self.final.at[slot]
        self.shared = [
            self.copies.send(theirs, target, place.other_core()),
            self.copies.send(mine, target, place.device(z=far)),
            self.copies.send(theirs, target, place.device(z=far, core=1 - place.core)),
        ]
        self.kept = self.copies.move(mine, target)

    def store(self):
        for copy in self.shared:
            copy.wait_recv()
        self.kept.wait()
        for slot in range(4):
            start = self.column + slot * QUARTER
            self.out[self.row : self.row + 16, start : start + QUARTER] = self.final[slot].astype(F32)


LEFTS = (D, D, D, FF)
BLOCKS = (3, 1, 4, 1)


def attention_back(projected, grad_att, grad_proj, pairs):
    low = lax.broadcasted_iota(jnp.int32, (1, 128), 1) < HEAD

    def body(pair, _):
        def columns(part):
            return pl.ds(pl.multiple_of(part * D + pair * 128, 128), 128)

        query = projected[:, columns(0)] * jnp.asarray(HEAD ** (-0.5), BF16)
        key = projected[:, columns(1)]
        value = projected[:, columns(2)]
        grad = grad_att[:, columns(0)]
        zero = jnp.zeros((), BF16)
        pieces = []
        for mine in (low, jnp.logical_not(low)):
            scores = lax.dot_general(
                jnp.where(mine, query, zero), key, NT, preferred_element_type=F32
            )
            terms = jnp.exp(scores - jnp.max(scores, -1, keepdims=True))
            probs = terms * (1.0 / jnp.sum(terms, -1, keepdims=True))
            grad_probs = lax.dot_general(
                jnp.where(mine, grad, zero), value, NT, preferred_element_type=F32
            )
            inner = jnp.sum(probs * grad_probs, -1, keepdims=True)
            grad_scores = (probs * (grad_probs - inner)).astype(BF16)
            rounded = probs.astype(BF16)
            pieces.append(
                (
                    jnp.dot(grad_scores[:HALF], key, preferred_element_type=F32) * HEAD ** (-0.5),
                    lax.dot_general(grad_scores[:, :HALF], query, TN, preferred_element_type=F32),
                    lax.dot_general(rounded[:, :HALF], grad, TN, preferred_element_type=F32),
                )
            )
        for part in range(3):
            both = jnp.where(low, pieces[0][part], pieces[1][part])
            grad_proj[:, columns(part)] = both.astype(BF16)
        return 0

    lax.fori_loop(*pairs, body, 0)


def normal_parts(values):
    centre = values - jnp.mean(values, -1, keepdims=True)
    scale = lax.rsqrt(jnp.mean(centre * centre, -1, keepdims=True) + EPSILON)
    return centre * scale, scale


def leave_kernel(*refs):
    refs = list(refs)

    def take(count):
        taken, refs[:count] = refs[:count], []
        return taken

    lefts_in, rights_in = take(4), take(3)
    w_attend, projected, own_att, tokens, grad_middle, scale_one, sums = take(7)
    outs = take(4)
    whole, tokens_grad = take(2)
    lefts, rights, parts = take(4), take(4), take(12)
    bufs = [take(3) for _ in range(12)]
    finals = take(12)
    weight, both_att, grad_proj, vector, vector_sent, vector_got = take(6)
    send_sems, recv_sems, local_sems = refs
    place = Place()
    copies = Copies(send_sems, recv_sems, local_sems)
    far = place.step("z", 2)
    rights_in = [grad_proj] + rights_in
    greet(place.everyone() + [place.device(z=far, core=1 - place.core)])
    scatters = [
        Scatter(place, copies, UNITS[i], parts[i], bufs[i], finals[i], outs[UNITS[i][0]]) for i in range(12)
    ]

    def of(weight_index, wave=None):
        return [
            scatters[i]
            for i in range(12)
            if UNITS[i][0] == weight_index and wave in (None, i // 3)
        ]

    def start(wave, phase):
        for scatter in scatters[3 * wave : 3 * wave + 3]:
            scatter.start(phase)

    def forward(wave):
        for scatter in scatters[3 * wave : 3 * wave + 3]:
            scatter.forward()

    def finish(wave, phase):
        for scatter in scatters[3 * wave : 3 * wave + 3]:
            scatter.finish(phase)

    def share(wave):
        for scatter in scatters[3 * wave : 3 * wave + 3]:
            scatter.share()

    def store(wave):
        for scatter in scatters[3 * wave : 3 * wave + 3]:
            scatter.store()

    pairs = {}
    for i in (3, 2, 1):
        pairs[i] = [
            Pair(place, copies, lefts_in[i], lefts[i]),
            Pair(place, copies, rights_in[i], rights[i], BLOCKS[i]),
        ]
    att_copy = copies.send(own_att, both_att.at[pl.ds(HALF, HALF)], place.along("z", 2))
    late = [Pair(place, copies, lefts_in[0], lefts[0])]
    weight_copy = copies.move(w_attend, weight)
    both_att[:HALF] = own_att[...]

    def meet(pair):
        for half in pair:
            half.wait()

    meet(pairs[3])
    make_tall_parts(lefts[3], rights[3], of(3))
    start(3, 0)
    meet(pairs[2])
    make_parts(lefts[2], rights[2], of(2, 2))
    start(2, 0)
    meet(pairs[1])
    make_parts(lefts[2], rights[2], of(2, 1))
    make_parts(lefts[1], rights[1], of(1))
    start(1, 0)

    att_copy.wait_recv()
    attention_back(projected, both_att, grad_proj, (0, HEADS // 4))
    forward(3)
    attention_back(projected, both_att, grad_proj, (HEADS // 4, HEADS // 2))
    late.append(Pair(place, copies, grad_proj, rights[0], BLOCKS[0]))
    forward(2)
    forward(1)
    finish(3, 0)
    start(3, 1)
    meet(late)
    make_parts(lefts[0], rights[0], of(0))
    start(0, 0)

    weight_copy.wait()
    normal, scale = normal_parts(tokens[...].astype(F32))
    grad_first = jnp.concatenate(
        [
            lax.dot_general(
                grad_proj[...], weight[start : start + 256], NT, preferred_element_type=F32
            )
            for start in range(0, D, 256)
        ],
        1,
    )
    back = grad_first * (1.0 + scale_one[...])
    tokens_grad[...] = grad_middle[...] + scale * (
        back
        - jnp.mean(back, -1, keepdims=True)
        - normal * jnp.mean(back * normal, -1, keepdims=True)
    )
    vector[...] = sums[...]
    for place_of, total in ((0, grad_first), (8, grad_first * normal)):
        total = jnp.sum(total, 0, keepdims=True)
        for row in range(8):
            vector[place_of + row : place_of + row + 1, :] = total[:, row * 128 : (row + 1) * 128]
    vector_sent[...] = vector[...].astype(BF16)
    vector_copy = copies.send(vector_sent, vector_got, place.along("z", 2))

    finish(2, 0)
    start(2, 1)
    finish(3, 1)
    start(3, 2)
    forward(0)
    finish(1, 0)
    start(1, 1)
    vector_copy.wait_recv()
    whole[place.z_lo, place.at["x"], place.at["y"], place.core] = (
        vector_sent[...].astype(F32) + vector_got[...].astype(F32)
    ).astype(BF16)
    gather = SmallGather(place, copies, whole)
    gather.stage(0)
    finish(2, 1)
    start(2, 2)
    finish(3, 2)
    share(3)
    gather.stage(1)
    finish(1, 1)
    start(1, 2)
    finish(0, 0)
    start(0, 1)
    gather.stage(2)
    finish(2, 2)
    share(2)
    finish(1, 2)
    share(1)
    store(3)
    finish(0, 1)
    start(0, 2)
    gather.stage(3)
    store(2)
    finish(0, 2)
    share(0)
    store(1)
    gather.arrive()
    store(0)
    copies.drain()


def buffer_shapes():
    shapes = [(6, 4, 4, 16, QUARTER), (3, 4, 2, 16, QUARTER), (3, 2, 16, QUARTER)]
    return [pltpu.VMEM(shape, BF16) for shape in shapes]


def leave(lefts, rights, w_attend, projected, grad_att, tokens, grad_middle, scale_one, sums):
    anywhere = pl.BlockSpec(memory_space=pl.ANY)
    inside = pl.BlockSpec(memory_space=pltpu.VMEM)
    scratch = [pltpu.VMEM((SEQ, width), BF16) for width in LEFTS]
    scratch += [pltpu.VMEM((blocks, SEQ, 2 * QUARTER), BF16) for blocks in BLOCKS]
    scratch += [pltpu.VMEM((4, 4, 4, 2, 16, QUARTER), BF16)] * 12
    scratch += buffer_shapes() * 12
    scratch += [pltpu.VMEM((4, 16, QUARTER), BF16)] * 12
    scratch += [
        pltpu.VMEM((D, 3 * D), BF16),
        pltpu.VMEM((SEQ, D), BF16),
        pltpu.VMEM((HALF, 3 * D), BF16),
        pltpu.VMEM(sums.shape, F32),
        pltpu.VMEM(sums.shape, BF16),
        pltpu.VMEM(sums.shape, BF16),
    ]
    scratch += copy_scratch(12 * 15 + 4 + 9 + 10, 4 + 9 + 1 + 12)
    return pl.pallas_call(
        leave_kernel,
        out_shape=[jax.ShapeDtypeStruct((rows, columns), F32) for rows, columns in WEIGHTS]
        + [jax.ShapeDtypeStruct((2, 4, 4, 2) + sums.shape, BF16), jax.ShapeDtypeStruct((HALF, D), F32)],
        in_specs=[anywhere] * 8 + [inside] * 6,
        out_specs=[inside] * 6,
        scratch_shapes=scratch,
        compiler_params=pltpu.CompilerParams(
            collective_id=3, has_side_effects=True, vmem_limit_bytes=58 * 2**20
        ),
        name="leave",
    )(*lefts, *rights, w_attend, projected, grad_att, tokens, grad_middle, scale_one, sums)


def normalize(values):
    centre = values - jnp.mean(values, -1, keepdims=True)
    spread = jnp.mean(centre * centre, -1, keepdims=True)
    return centre * lax.rsqrt(spread + EPSILON)


def modulated(values, shift_vec, scale_vec):
    return normalize(values) * (1.0 + scale_vec) + shift_vec


def gelu_tanh(values):
    return jax.nn.gelu(values, approximate=True)


def sinusoid(step_ids):
    half_width = FREQ // 2
    freq_rates = jnp.exp(
        -math.log(10000.0) * jnp.arange(half_width, dtype=jnp.float32) / half_width
    )
    angles = step_ids.astype(jnp.float32)[:, None] * freq_rates[None, :]
    return jnp.concatenate([jnp.cos(angles), jnp.sin(angles)], axis=-1)


def head_split(rows_in):
    return rows_in.reshape(rows_in.shape[0], HEADS, HEAD)


def attend_scores(query_rows, key_rows):
    return jnp.einsum(
        "qhd,khd->hqk",
        head_split(query_rows),
        head_split(key_rows),
        preferred_element_type=F32,
    ) * HEAD ** (-0.5)


def per_device(
    tokens,
    labels,
    timesteps,
    cotangent,
    class_table,
    time_weight,
    modulate_weight,
    modulate_offset,
    attend_weight,
    output_weight,
    expand_weight,
    hidden_offset,
    contract_weight,
):
    shard_index = lax.axis_index("fsdp")
    token_half = lax.axis_index("ctx")
    all_labels, all_steps, b_hidden = gather_ids(labels, timesteps, hidden_offset[0])
    onehot = all_labels[:, None] == jnp.arange(CLASSES, dtype=jnp.int32)[None, :]
    sinus_rows = sinusoid(all_steps).astype(BF16)
    cond_cols = jnp.dot(
        onehot.astype(BF16), class_table, preferred_element_type=F32
    ) + jnp.dot(sinus_rows, time_weight, preferred_element_type=F32)
    offset_width = modulate_offset.shape[1]
    act_cols = jax.nn.silu(cond_cols).astype(BF16)
    partial_mod = jnp.dot(act_cols, modulate_weight[0], preferred_element_type=F32)
    placed = lax.dynamic_update_slice(
        jnp.zeros((1, 6 * D), F32),
        modulate_offset.astype(F32),
        (jnp.int32(0), shard_index * offset_width),
    )
    partial_mod = (partial_mod + placed).astype(BF16).reshape(2, 4, 4, 2, 48, 128)
    (w_attend, w_output, w_expand, w_contract), other_tokens, modulation = enter(
        (attend_weight[0], output_weight[0], expand_weight[0], contract_weight[0]),
        tokens[0],
        partial_mod,
    )
    shift_one, scale_one, gate_one, shift_two, scale_two, gate_two = [modulation[i] for i in range(6)]

    hidden = tokens[0].astype(F32)
    both_hidden = jnp.concatenate([tokens[0], other_tokens], 0).astype(F32)
    both_first = modulated(both_hidden, shift_one, scale_one).astype(BF16)
    first_in = both_first[:HALF]
    projected = jnp.dot(both_first, w_attend, preferred_element_type=F32).astype(BF16)
    query_rows, key_rows, value_rows = projected[:, :D], projected[:, D : 2 * D], projected[:, 2 * D :]
    scores = attend_scores(query_rows[:HALF], key_rows)
    top_score = jnp.max(scores, -1, keepdims=True)
    exp_terms = jnp.exp(scores - top_score)
    totals = jnp.sum(exp_terms, -1, keepdims=True)
    rounded_probs = (exp_terms / totals).astype(BF16)
    attended = (
        jnp.einsum(
            "hqk,khd->qhd", rounded_probs, head_split(value_rows), preferred_element_type=F32
        )
        .reshape(-1, D)
        .astype(BF16)
    )
    branch_one = jnp.dot(attended, w_output, preferred_element_type=F32)
    middle = hidden + gate_one * branch_one
    second_in = modulated(middle, shift_two, scale_two).astype(BF16)
    pre_act = jnp.dot(second_in, w_expand, preferred_element_type=F32) + b_hidden
    activated = gelu_tanh(pre_act).astype(BF16)
    branch_two = jnp.dot(activated, w_contract, preferred_element_type=F32)
    result = (middle + gate_two * branch_two).astype(BF16)[None]

    grad_hidden = cotangent[0].astype(F32)
    grad_two = (grad_hidden * gate_two).astype(BF16)
    gate_two_grad = jnp.sum(grad_hidden * branch_two, 0)
    grad_act = jnp.einsum("td,fd->tf", grad_two, w_contract, preferred_element_type=F32)
    _, gelu_pull = jax.vjp(gelu_tanh, pre_act)
    grad_pre = gelu_pull(grad_act)[0].astype(BF16)
    hidden_term = jnp.sum(grad_pre.astype(F32), 0)
    grad_second = jnp.einsum("tf,df->td", grad_pre, w_expand, preferred_element_type=F32)
    _, second_pull = jax.vjp(modulated, middle, shift_two, scale_two)
    grad_middle, shift_two_grad, scale_two_grad = second_pull(grad_second)
    grad_middle = grad_hidden + grad_middle
    grad_one = (grad_middle * gate_one).astype(BF16)
    gate_one_grad = jnp.sum(grad_middle * branch_one, 0)
    grad_att = jnp.einsum("te,de->td", grad_one, w_output, preferred_element_type=F32).astype(BF16)
    sums = jnp.concatenate(
        [
            jnp.zeros((2 * D,), F32),
            gate_one_grad,
            shift_two_grad,
            scale_two_grad,
            gate_two_grad,
            hidden_term,
        ]
    ).reshape(80, 128)
    attend_grad, output_grad, expand_grad, contract_grad, all_vectors, tokens_grad = leave(
        (first_in, attended, second_in, activated),
        (grad_one, grad_pre, grad_two),
        w_attend,
        projected,
        grad_att,
        tokens[0],
        grad_middle,
        scale_one[None],
        sums,
    )
    all_vectors = all_vectors.reshape(64, 80 * 128)
    all_mod = all_vectors[:, : 6 * D]
    own_hidden = lax.dynamic_slice_in_dim(all_vectors, 6 * D + shard_index * (FF // 64), FF // 64, 1)
    hidden_grad = jnp.sum(own_hidden.astype(F32), 0)
    grad_act_cols = jnp.einsum("bk,dk->bd", all_mod, modulate_weight[0], preferred_element_type=F32)
    modulate_grad = jnp.einsum("bd,bk->dk", act_cols, all_mod, preferred_element_type=F32)
    own_cols = lax.dynamic_slice_in_dim(all_mod, shard_index * offset_width, offset_width, 1)
    offset_grad = jnp.sum(own_cols.astype(F32), 0)
    _, silu_pull = jax.vjp(jax.nn.silu, cond_cols)
    grad_cond = silu_pull(grad_act_cols)[0]
    table_grad = jnp.einsum("bc,bd->cd", onehot.astype(F32), grad_cond, precision=HIGHEST)
    time_grad = jnp.einsum("bf,bd->fd", sinus_rows.astype(F32), grad_cond, precision=HIGHEST)
    return (
        result,
        tokens_grad[None],
        table_grad,
        time_grad,
        modulate_grad[None],
        offset_grad[None],
        attend_grad[None],
        output_grad[None],
        expand_grad[None],
        hidden_grad[None],
        contract_grad[None],
    )


def solution(mesh):
    rows = P(None, "fsdp", None)
    columns = P(None, "fsdp")
    halves = P("fsdp", "ctx", None)
    each = P("fsdp")
    in_specs = (
        halves, each, each, halves, columns, columns, rows, columns, rows, rows, rows, columns, rows,
    )
    out_specs = (
        halves, halves, columns, columns, rows, columns, rows, rows, rows, columns, rows,
    )
    return jax.shard_map(
        per_device, mesh=mesh, in_specs=in_specs, out_specs=out_specs, check_vma=False
    )
```

```python
import functools
import math

import jax
import jax.numpy as jnp
from jax import lax
from jax.experimental import pallas as pl
from jax.experimental.pallas import tpu as pltpu
from jax.sharding import PartitionSpec as P

D = 1024
HEADS = 16
HEAD = 64
FF = 4096
CLASSES = 1000
FREQ = 256
SEQ = 256
HALF = SEQ // 2

WEIGHTS = ((16, 3 * D), (16, D), (16, FF), (64, D))
ORDERS = ("zyx", "xzy", "yxz")
WAVES = tuple(
    tuple((weight, row, column, order) for (weight, row, column), order in zip(wave, ORDERS))
    for wave in (
        ((0, 0, 0), (0, 0, D), (0, 0, 2 * D)),
        ((1, 0, 0), (2, 0, 0), (2, 0, D)),
        ((2, 0, 2 * D), (2, 0, 3 * D), (3, 0, 0)),
        ((3, 16, 0), (3, 32, 0), (3, 48, 0)),
    )
)
UNITS = tuple(unit for wave in WAVES for unit in wave)
QUARTER = D // 4

HIGHEST = lax.Precision.HIGHEST
EPSILON = 1e-06
MESH = pl.DeviceIdType.MESH
BF16 = jnp.bfloat16
F32 = jnp.float32
NT = (((1,), (1,)), ((), ()))
TN = (((0,), (0,)), ((), ()))


class Place:
    def __init__(self):
        shard = lax.axis_index("fsdp")
        self.z_hi = lax.axis_index("ctx")
        self.core = lax.rem(shard, 2)
        self.z_lo = lax.div(shard, 32)
        self.at = {
            "x": lax.rem(lax.div(shard, 8), 4),
            "y": lax.rem(lax.div(shard, 2), 4),
            "z": 2 * self.z_hi + self.z_lo,
        }

    def step(self, axis, distance):
        return lax.rem(self.at[axis] + distance + 4, 4)

    def device(self, core=None, **moved):
        at = {**self.at, **moved}
        core = self.core if core is None else core
        shard = ((lax.rem(at["z"], 2) * 4 + at["x"]) * 4 + at["y"]) * 2 + core
        return (shard, lax.div(at["z"], 2))

    def along(self, axis, distance):
        return self.device(**{axis: self.step(axis, distance)})

    def other_core(self):
        return self.device(core=1 - self.core)

    def other_z_lo(self):
        return self.device(z=2 * self.z_hi + 1 - self.z_lo)

    def everyone(self):
        ids = [self.other_core()]
        for axis in "xyz":
            ids += [self.along(axis, distance) for distance in (1, 2, 3)]
        return ids


def greet(ids):
    barrier = pltpu.get_barrier_semaphore()
    for device in ids:
        pl.semaphore_signal(barrier, inc=1, device_id=device, device_id_type=MESH)
    pl.semaphore_wait(barrier, len(ids))


class Copies:
    def __init__(self, send_sems, recv_sems, local_sems):
        self.send_sems, self.recv_sems, self.local_sems = send_sems, recv_sems, local_sems
        self.remote, self.local = [], []

    def send(self, source, target, device):
        slot = len(self.remote)
        copy = pltpu.make_async_remote_copy(
            src_ref=source,
            dst_ref=target,
            send_sem=self.send_sems.at[slot],
            recv_sem=self.recv_sems.at[slot],
            device_id=device,
            device_id_type=MESH,
        )
        copy.start()
        self.remote.append(copy)
        return copy

    def move(self, source, target):
        slot = len(self.local)
        copy = pltpu.make_async_copy(source, target, self.local_sems.at[slot])
        copy.start()
        self.local.append(copy)
        return copy

    def drain(self):
        for copy in self.remote:
            copy.wait_send()


def copy_scratch(remote, local):
    return [
        pltpu.SemaphoreType.DMA((remote,)),
        pltpu.SemaphoreType.DMA((remote,)),
        pltpu.SemaphoreType.DMA((max(local, 1),)),
    ]


class Gather:
    def __init__(self, place, copies, source, out, unit, direct):
        self.place, self.copies, self.source, self.out = place, copies, source, out
        self.direct = direct
        _, self.row, self.column, self.order = unit
        self.done = []
        self.to_core = []

    def region(self, half_index, core, **sel):
        lead = [sel.get(axis) for axis in "xy"]
        lead = [slice(None) if index is None else index for index in lead]
        z = sel.get("z")
        start, width = self.column + half_index * 2 * QUARTER, 2 * QUARTER
        z_lo = slice(None)
        if z is not None:
            width = QUARTER
            start = start + lax.div(z, 2) * QUARTER
            z_lo = lax.rem(z, 2)
        core = slice(None) if core is None else core
        rows = pl.ds(self.row, 16)
        return self.out.at[z_lo, lead[0], lead[1], core, rows, pl.ds(pl.multiple_of(start, 128), width)]

    def begin(self):
        place = self.place
        mine = self.column + (place.core * 2 + place.z_hi) * QUARTER
        theirs = self.column + ((1 - place.core) * 2 + place.z_hi) * QUARTER
        mine, theirs = pl.multiple_of(mine, 128), pl.multiple_of(theirs, 128)
        rows = pl.ds(self.row, 16)
        self.first = self.copies.send(
            self.source.at[rows, pl.ds(theirs, QUARTER)],
            self.region(1 - place.core, place.core, **place.at),
            place.other_core(),
        )
        self.own = self.copies.move(
            self.source.at[rows, pl.ds(mine, QUARTER)], self.region(place.core, place.core, **place.at)
        )

    def ready(self):
        self.first.wait_recv()
        self.own.wait()

    def block(self, axis, index, core):
        sel = {a: self.place.at[a] for a in "xyz" if a not in self.done}
        return self.region(self.place.core, core, **{**sel, axis: index})

    def pass_on(self, phase, index, core):
        if phase == 2:
            piece = self.block(self.order[2], index, core)
            self.to_core.append(self.copies.send(piece, piece, self.place.other_core()))

    def start(self, phase):
        axis, place = self.order[phase], self.place
        self.arriving = {}
        if phase in self.direct:
            piece = self.block(axis, place.at[axis], None)
            for distance in (1, 3, 2):
                self.arriving[distance] = self.copies.send(piece, piece, place.along(axis, distance))
            return
        for way, core in ((1, 0), (-1, 1), (1, 1), (-1, 0)):
            piece = self.block(axis, place.at[axis], core)
            self.arriving[way, core] = self.copies.send(piece, piece, place.along(axis, way))
        self.pass_on(phase, place.at[axis], None)

    def forward(self, phase):
        axis, place = self.order[phase], self.place
        self.last = {}
        for way, core in ((1, 0), (-1, 1)):
            self.arriving[way, core].wait_recv()
            piece = self.block(axis, place.step(axis, -way), core)
            self.last[way, core] = self.copies.send(piece, piece, place.along(axis, way))
            self.pass_on(phase, place.step(axis, -way), core)

    def finish(self, phase):
        axis, place = self.order[phase], self.place
        self.done.append(axis)
        if phase in self.direct:
            for copy in self.arriving.values():
                copy.wait_recv()
            return
        self.done.pop()
        for way, core in ((1, 1), (-1, 0)):
            self.arriving[way, core].wait_recv()
            self.pass_on(phase, place.step(axis, -way), core)
        for way, core in ((1, 0), (-1, 1)):
            self.last[way, core].wait_recv()
            self.pass_on(phase, place.step(axis, 2), core)
        self.done.append(axis)


class SmallGather:
    def __init__(self, place, copies, whole):
        self.place, self.copies, self.whole = place, copies, whole
        self.waiting = []

    def arrive(self):
        for copy in self.waiting:
            copy.wait_recv()
        self.waiting = []

    def stage(self, which):
        self.arrive()
        place, whole, send = self.place, self.whole, self.copies.send
        at, core = place.at, place.core
        if which == 0:
            piece = whole.at[core, place.z_lo, at["x"], at["y"]]
            self.waiting = [send(piece, piece, place.along("y", d)) for d in (1, 2, 3)]
        elif which == 1:
            piece = whole.at[core, place.z_lo, at["x"]]
            self.waiting = [send(piece, piece, place.along("x", d)) for d in (1, 2, 3)]
        elif which == 2:
            piece = whole.at[core, place.z_lo]
            self.waiting = [send(piece, piece, place.other_z_lo())]
        else:
            piece = whole.at[core]
            self.waiting = [send(piece, piece, place.other_core())]


def conditioned(ids, class_table, time_weight, labels, sinus, bias):
    def body(row, _):
        core, z_lo = lax.div(row, 32), lax.rem(lax.div(row, 16), 2)
        x, y = lax.rem(lax.div(row, 4), 4), lax.rem(row, 4)
        labels[pl.ds(row, 1), :] = ids[core, z_lo, x, y, 1:2, :]
        for half in range(2):
            sinus[half, pl.ds(row, 1), :] = ids[core, z_lo, x, y, 2 + half : 3 + half, :]
        return 0

    def join(row, _):
        z_lo, x, y = lax.div(row, 16), lax.rem(lax.div(row, 4), 4), lax.rem(row, 4)
        bias[pl.ds(row, 1), :] = ids[0, z_lo, x, y, 0:1, :] + ids[1, z_lo, x, y, 0:1, :]
        return 0

    lax.fori_loop(0, 32, join, 0)

    lax.fori_loop(0, 64, body, 0)
    cond = jnp.zeros((64, 16), F32)
    lane = lax.broadcasted_iota(jnp.int32, (64, 128), 1).astype(F32)
    for start in range(0, CLASSES, 128):
        width = min(128, CLASSES - start)
        chosen = jnp.where(labels[...] == lane + float(start), 1.0, 0.0).astype(BF16)
        cond += lax.dot_general(
            chosen[:, :width], class_table[:, start : start + width], NT, preferred_element_type=F32
        )
    for half in range(2):
        cond += lax.dot_general(
            sinus[half].astype(BF16),
            time_weight[:, half * 128 : half * 128 + 128],
            NT,
            preferred_element_type=F32,
        )
    return cond


def attention_forward(projected, attended, pairs):
    low = lax.broadcasted_iota(jnp.int32, (1, 128), 1) < HEAD

    def body(pair, _):
        def columns(part):
            return pl.ds(pl.multiple_of(part * D + pair * 128, 128), 128)

        query = projected[:HALF, columns(0)] * jnp.asarray(HEAD ** (-0.5), BF16)
        key = projected[:, columns(1)]
        value = projected[:, columns(2)]
        pieces = []
        for mine in (low, jnp.logical_not(low)):
            scores = lax.dot_general(
                jnp.where(mine, query, jnp.zeros((), BF16)), key, NT, preferred_element_type=F32
            )
            terms = jnp.exp(scores - jnp.max(scores, -1, keepdims=True))
            probs = terms * (1.0 / jnp.sum(terms, -1, keepdims=True))
            pieces.append(jnp.dot(probs.astype(BF16), value, preferred_element_type=F32))
        attended[:, columns(0)] = jnp.where(low, *pieces).astype(BF16)
        return 0

    lax.fori_loop(*pairs, body, 0)


def normal_parts(values):
    centre = values - jnp.mean(values, -1, keepdims=True)
    scale = lax.rsqrt(jnp.mean(centre * centre, -1, keepdims=True) + EPSILON)
    return centre * scale, scale


def enter_kernel(
    w0, w1, w2, w3, tokens_in, class_in, time_in, modulate_in, own_ids, placed,
    o0, o1, o2, o3, modulation, labels, sinus, bias, cond, first_in, projected, attended,
    ids, other_tokens, w_attend,
    partial_mod, got_core, sum_core, got_z, slabs, sum_z, got_x, sum_x, got_y, both_first,
    tokens, class_table, time_weight, modulate_weight,
    send_sems, recv_sems, local_sems,
):
    place = Place()
    copies = Copies(send_sems, recv_sems, local_sems)
    sources, wholes = (w0, w1, w2, w3), (o0, o1, o2, o3)
    waves = [
        [
            Gather(place, copies, sources[unit[0]], wholes[unit[0]], unit, (0, 1) if index == 0 else (0,))
            for unit in wave
        ]
        for index, wave in enumerate(WAVES)
    ]
    gathers = [gather for wave in waves for gather in wave]

    def start(wave, phase):
        for gather in waves[wave]:
            gather.start(phase)

    def forward(wave, phase):
        for gather in waves[wave]:
            gather.forward(phase)

    def finish(wave, phase):
        for gather in waves[wave]:
            gather.finish(phase)

    operands = [
        copies.move(source, target)
        for source, target in (
            (class_in, class_table),
            (time_in, time_weight),
            (modulate_in, modulate_weight),
            (tokens_in, tokens),
        )
    ]
    ids[place.core, place.z_lo, place.at["x"], place.at["y"]] = own_ids[...]
    greet(place.everyone())
    id_gather = SmallGather(place, copies, ids)
    id_gather.stage(0)
    for gather in gathers:
        gather.begin()
    tokens_copy = copies.send(tokens_in, other_tokens, place.along("z", 2))
    id_gather.stage(1)
    for gather in gathers:
        gather.ready()
        gather.start(0)
    id_gather.stage(2)
    for wave in range(2):
        finish(wave, 0)
        start(wave, 1)
    id_gather.stage(3)
    for wave in range(2, 4):
        finish(wave, 0)
        start(wave, 1)
    id_gather.arrive()
    finish(0, 1)
    start(0, 2)

    for copy in operands:
        copy.wait()
    cond[...] = conditioned(ids, class_table, time_weight, labels, sinus, bias)
    act = (cond[...] / (1.0 + jnp.exp(-cond[...]))).astype(BF16)
    for column in range(0, 6 * D, D):
        columns = slice(column, column + D)
        partial_mod[:, columns] = (
            jnp.dot(act, modulate_weight[:, columns], preferred_element_type=F32) + placed[:, columns]
        ).astype(BF16)

    def share(index, count):
        return pl.ds(pl.multiple_of(index * count, count), count)

    mod_core = copies.send(partial_mod.at[share(1 - place.core, 32)], got_core, place.other_core())
    for wave in (1, 2, 3):
        forward(wave, 1)
    mod_core.wait_recv()
    sum_core[...] = (
        partial_mod[share(place.core, 32)].astype(F32) + got_core[...].astype(F32)
    ).astype(BF16)
    mod_z = copies.send(sum_core.at[share(1 - place.z_lo, 16)], got_z, place.other_z_lo())
    finish(1, 1)
    start(1, 2)
    mod_z.wait_recv()
    for row in range(48):
        columns = slice(row * 128, row * 128 + 128)
        slabs[:, row, :] = sum_core[share(place.z_lo, 16), columns].astype(F32) + got_z[
            :, columns
        ].astype(F32)
    sum_z[...] = slabs[...].astype(BF16).reshape(4, 4, 48, 128)
    mod_x = [
        copies.send(sum_z.at[place.step("x", distance)], got_x.at[distance - 1], place.along("x", distance))
        for distance in (1, 2, 3)
    ]
    finish(2, 1)
    forward(0, 2)
    start(2, 2)
    for copy in mod_x:
        copy.wait_recv()
    for y in range(4):
        total = sum_z[place.at["x"], y].astype(F32)
        for slot in range(3):
            total += got_x[slot, y].astype(F32)
        sum_x[y] = total.astype(BF16)
    mod_y = [
        copies.send(sum_x.at[place.step("y", distance)], got_y.at[distance - 1], place.along("y", distance))
        for distance in (1, 2, 3)
    ]
    finish(3, 1)
    finish(0, 2)
    for gather in waves[0]:
        for copy in gather.to_core:
            copy.wait_recv()
    weight_copy = copies.move(o0, w_attend)
    forward(1, 2)
    start(3, 2)
    for copy in mod_y:
        copy.wait_recv()
    total = sum_x[place.at["y"]].astype(F32)
    for slot in range(3):
        total += got_y[slot].astype(F32)
    for row in range(48):
        vector, lane = divmod(row, 8)
        modulation[vector : vector + 1, lane * 128 : lane * 128 + 128] = total[row : row + 1]
    tokens_copy.wait_recv()
    for row, source in enumerate((tokens, other_tokens)):
        normal, _ = normal_parts(source[...].astype(F32))
        both_first[row * HALF : row * HALF + HALF] = (
            normal * (1.0 + modulation[1:2]) + modulation[0:1]
        ).astype(BF16)
    first_in[...] = both_first[:HALF]
    forward(2, 2)
    weight_copy.wait()
    for column in range(0, 3 * D, 512):
        columns = slice(column, column + 512)
        projected[:, columns] = jnp.dot(
            both_first[...],
            w_attend[:, :, :, :, :, columns].reshape(D, 512),
            preferred_element_type=F32,
        ).astype(BF16)
    finish(1, 2)
    forward(3, 2)
    attention_forward(projected, attended, (0, HEADS // 4))
    finish(2, 2)
    attention_forward(projected, attended, (HEADS // 4, HEADS // 2))
    finish(3, 2)
    for wave in waves[1:]:
        for gather in wave:
            for copy in gather.to_core:
                copy.wait_recv()
    copies.drain()


def enter(weights, tokens, class_table, time_weight, modulate_weight, own_ids, placed):
    outside = pl.BlockSpec(memory_space=pl.ANY)
    inside = pl.BlockSpec(memory_space=pltpu.VMEM)
    slab = (48, 128)
    shapes = [jax.ShapeDtypeStruct((2, 4, 4, 2, rows, columns), BF16) for rows, columns in WEIGHTS]
    shapes += [
        jax.ShapeDtypeStruct((6, D), F32),
        jax.ShapeDtypeStruct((64, 128), F32),
        jax.ShapeDtypeStruct((2, 64, 128), F32),
        jax.ShapeDtypeStruct((32, 128), F32),
        jax.ShapeDtypeStruct((64, 16), F32),
        jax.ShapeDtypeStruct((HALF, D), BF16),
        jax.ShapeDtypeStruct((SEQ, 3 * D), BF16),
        jax.ShapeDtypeStruct((HALF, D), BF16),
    ]
    out = pl.pallas_call(
        enter_kernel,
        out_shape=shapes,
        in_specs=[outside] * 8 + [inside] * 2,
        out_specs=[outside] * 4 + [inside] * 8,
        scratch_shapes=[
            pltpu.VMEM((2, 2, 4, 4, 8, 128), F32),
            pltpu.VMEM((HALF, D), BF16),
            pltpu.VMEM((2, 4, 4, 2, 16, 3 * D), BF16),
            pltpu.VMEM((64, 6 * D), BF16),
            pltpu.VMEM((32, 6 * D), BF16),
            pltpu.VMEM((32, 6 * D), BF16),
            pltpu.VMEM((16, 6 * D), BF16),
            pltpu.VMEM((16,) + slab, F32),
            pltpu.VMEM((4, 4) + slab, BF16),
            pltpu.VMEM((3, 4) + slab, BF16),
            pltpu.VMEM((4,) + slab, BF16),
            pltpu.VMEM((3,) + slab, BF16),
            pltpu.VMEM((SEQ, D), BF16),
            pltpu.VMEM((HALF, D), BF16),
            pltpu.VMEM((16, CLASSES), BF16),
            pltpu.VMEM((16, FREQ), BF16),
            pltpu.VMEM((16, 6 * D), BF16),
        ]
        + copy_scratch(12 * 23 + 9 + 8, 17),
        compiler_params=pltpu.CompilerParams(
            collective_id=0, has_side_effects=True, vmem_limit_bytes=60 * 2**20
        ),
        name="enter",
    )(*weights, tokens, class_table, time_weight, modulate_weight, own_ids, placed)
    full = [whole.reshape(64 * rows, columns) for whole, (rows, columns) in zip(out[:4], WEIGHTS)]
    return full, out[4:]


class Pair:
    def __init__(self, place, copies, source, both, blocks=None):
        self.copies = []
        other = place.other_core()
        if blocks is None:
            self.copies.append(copies.send(source, both.at[pl.ds(HALF, HALF)], other))
            self.copies.append(copies.move(source, both.at[pl.ds(0, HALF)]))
            return
        for block in range(blocks):
            mine = pl.multiple_of(block * D + place.core * 2 * QUARTER, 128)
            theirs = pl.multiple_of(block * D + (1 - place.core) * 2 * QUARTER, 128)
            width = 2 * QUARTER
            self.copies.append(
                copies.send(source.at[:, pl.ds(theirs, width)], both.at[block, pl.ds(HALF, HALF)], other)
            )
            self.copies.append(
                copies.move(source.at[:, pl.ds(mine, width)], both.at[block, pl.ds(0, HALF)])
            )

    def wait(self):
        for index, copy in enumerate(self.copies):
            if index % 2:
                copy.wait()
            else:
                copy.wait_recv()


def make_parts(left, right, scatters):
    def body(i, _):
        z_lo, x = lax.div(i, 4), lax.rem(i, 4)
        chosen = left[:, pl.ds(pl.multiple_of(i * 128, 128), 128)]
        for scatter in scatters:
            made = lax.dot_general(
                chosen, right[scatter.column // D], TN, preferred_element_type=F32
            ).astype(BF16)
            for q in range(2):
                scatter.parts[2 * q + z_lo, x] = made[:, q * QUARTER : (q + 1) * QUARTER].reshape(
                    4, 2, 16, QUARTER
                )
        return 0

    lax.fori_loop(0, 8, body, 0)


def make_tall_parts(left, right, scatters):
    def body(i, _):
        z_lo, x = lax.div(i, 4), lax.rem(i, 4)
        chosen = left[:, pl.ds(pl.multiple_of(i * 512, 128), 512)]
        made = lax.dot_general(chosen, right[0], TN, preferred_element_type=F32).astype(BF16)
        made = made.reshape(4, 2, 64, 2 * QUARTER)
        for scatter in scatters:
            rows = made[:, :, scatter.row : scatter.row + 16]
            for q in range(2):
                scatter.parts[2 * q + z_lo, x] = rows[..., q * QUARTER : (q + 1) * QUARTER]
        return 0

    lax.fori_loop(0, 8, body, 0)


class Scatter:
    def __init__(self, place, copies, unit, parts, bufs, final, out):
        self.place, self.copies = place, copies
        _, self.row, self.column, order = unit
        self.order = order[::-1]
        self.parts, self.bufs, self.final, self.out = parts, bufs, final, out
        self.done = []

    def sel(self, axis, index):
        at = {a: self.place.at[a] if a in self.done else None for a in "xyz"}
        at[axis] = index
        return [at[a] for a in "zxy"]

    def block(self, axis, index, core):
        lead = [slice(None) if i is None else i for i in self.sel(axis, index)]
        return self.parts.at[(*lead, core)]

    def add(self, axis, index, core, bufs):
        sel = self.sel(axis, index)
        free = [i for i, s in enumerate(sel) if s is None]

        def body(step, _):
            where = [slice(None) if s is None else s for s in sel]
            inner = (slice(None),) * len(free)
            if len(free) == 2:
                where[free[0]], inner = step, (step, slice(None))
            if core is not None:
                where.append(core)
            total = self.parts[tuple(where)].astype(F32)
            for buf in bufs:
                total += buf[inner].astype(F32)
            self.parts[tuple(where)] = total.astype(BF16)
            return 0

        if len(free) == 2:
            lax.fori_loop(0, 4, body, 0)
        else:
            body(0, 0)

    def start(self, phase):
        axis, place = self.order[phase], self.place
        buf = self.bufs[phase]
        send = self.copies.send
        if phase > 0:
            self.direct = [
                send(
                    self.block(axis, place.step(axis, distance), slice(None)),
                    buf.at[distance - 1],
                    place.along(axis, distance),
                )
                for distance in (1, 3, 2)
            ]
            return
        up, down = place.along(axis, 1), place.along(axis, -1)
        far = place.step(axis, 2)
        self.far = {
            1: send(self.block(axis, far, 0), buf.at[0], up),
            -1: send(self.block(axis, far, 1), buf.at[1], down),
        }
        self.raw = {
            1: send(self.block(axis, place.step(axis, 1), 1), buf.at[3], up),
            -1: send(self.block(axis, place.step(axis, -1), 0), buf.at[2], down),
        }

    def forward(self):
        axis, place = self.order[0], self.place
        buf = self.bufs[0]
        self.near = {}
        for way, core in ((1, 0), (-1, 1)):
            self.far[way].wait_recv()
            index = place.step(axis, way)
            self.add(axis, index, core, [buf.at[core]])
            self.near[way] = self.copies.send(
                self.block(axis, index, core), buf.at[4 + core], place.along(axis, way)
            )

    def finish(self, phase):
        axis, place = self.order[phase], self.place
        buf = self.bufs[phase]
        if phase > 0:
            for copy in self.direct:
                copy.wait_recv()
            self.add(axis, place.at[axis], None, [buf.at[slot] for slot in range(3)])
        else:
            for way, core in ((1, 0), (-1, 1)):
                self.raw[-way].wait_recv()
                self.near[way].wait_recv()
                self.add(axis, place.at[axis], core, [buf.at[2 + core], buf.at[4 + core]])
        self.done.append(axis)

    def share(self):
        place, at = self.place, self.place.at
        slot = place.core * 2 + place.z_hi
        mine = self.parts.at[at["z"], at["x"], at["y"], place.core]
        theirs = self.parts.at[at["z"], at["x"], at["y"], 1 - place.core]
        far = place.step("z", 2)
        target = self.final.at[slot]
        self.shared = [
            self.copies.send(theirs, target, place.other_core()),
            self.copies.send(mine, target, place.device(z=far)),
            self.copies.send(theirs, target, place.device(z=far, core=1 - place.core)),
        ]
        self.kept = self.copies.move(mine, target)

    def store(self):
        for copy in self.shared:
            copy.wait_recv()
        self.kept.wait()
        for slot in range(4):
            start = self.column + slot * QUARTER
            self.out[self.row : self.row + 16, start : start + QUARTER] = self.final[slot].astype(F32)


LEFTS = (D, D, D, FF)
BLOCKS = (3, 1, 4, 1)


def attention_back(projected, grad_att, grad_proj, pairs):
    low = lax.broadcasted_iota(jnp.int32, (1, 128), 1) < HEAD

    def body(pair, _):
        def columns(part):
            return pl.ds(pl.multiple_of(part * D + pair * 128, 128), 128)

        query = projected[:, columns(0)] * jnp.asarray(HEAD ** (-0.5), BF16)
        key = projected[:, columns(1)]
        value = projected[:, columns(2)]
        grad = grad_att[:, columns(0)]
        zero = jnp.zeros((), BF16)
        pieces = []
        for mine in (low, jnp.logical_not(low)):
            scores = lax.dot_general(
                jnp.where(mine, query, zero), key, NT, preferred_element_type=F32
            )
            terms = jnp.exp(scores - jnp.max(scores, -1, keepdims=True))
            probs = terms * (1.0 / jnp.sum(terms, -1, keepdims=True))
            grad_probs = lax.dot_general(
                jnp.where(mine, grad, zero), value, NT, preferred_element_type=F32
            )
            inner = jnp.sum(probs * grad_probs, -1, keepdims=True)
            grad_scores = (probs * (grad_probs - inner)).astype(BF16)
            rounded = probs.astype(BF16)
            pieces.append(
                (
                    jnp.dot(grad_scores[:HALF], key, preferred_element_type=F32) * HEAD ** (-0.5),
                    lax.dot_general(grad_scores[:, :HALF], query, TN, preferred_element_type=F32),
                    lax.dot_general(rounded[:, :HALF], grad, TN, preferred_element_type=F32),
                )
            )
        for part in range(3):
            both = jnp.where(low, pieces[0][part], pieces[1][part])
            grad_proj[:, columns(part)] = both.astype(BF16)
        return 0

    lax.fori_loop(*pairs, body, 0)


LEAVE_STEPS = (
    "M3", "S30", "M2", "S20", "M1", "S10", "A0", "F3", "A1", "F2",
    "F1", "M0", "S00", "L", "N30", "S31", "N20", "S21", "F0", "G0",
    "N10", "S11", "N31", "S32", "N21", "S22", "G1", "N00", "S01", "N11",
    "S12", "G2", "N32", "H3", "N22", "H2", "N01", "S02", "G3", "N12",
    "H1", "T3", "T2", "N02", "H0", "T1", "G4", "T0",
)


def leave_kernel(*refs):
    refs = list(refs)

    def take(count):
        taken, refs[:count] = refs[:count], []
        return taken

    lefts_in, rights_in = take(4), take(3)
    w_attend, projected, own_att, tokens, grad_middle, scale_one, sums = take(7)
    outs = take(4)
    whole, tokens_grad = take(2)
    lefts, rights, parts = take(4), take(4), take(12)
    bufs = [take(3) for _ in range(12)]
    finals = take(12)
    weight, both_att, grad_proj, vector, vector_sent, vector_got = take(6)
    send_sems, recv_sems, local_sems = refs
    place = Place()
    copies = Copies(send_sems, recv_sems, local_sems)
    far = place.step("z", 2)
    rights_in = [grad_proj] + rights_in
    greet(place.everyone() + [place.device(z=far, core=1 - place.core)])
    scatters = [
        Scatter(place, copies, UNITS[i], parts[i], bufs[i], finals[i], outs[UNITS[i][0]]) for i in range(12)
    ]

    def of(weight_index, wave=None):
        return [
            scatters[i]
            for i in range(12)
            if UNITS[i][0] == weight_index and wave in (None, i // 3)
        ]

    def start(wave, phase):
        for scatter in scatters[3 * wave : 3 * wave + 3]:
            scatter.start(phase)

    def forward(wave):
        for scatter in scatters[3 * wave : 3 * wave + 3]:
            scatter.forward()

    def finish(wave, phase):
        for scatter in scatters[3 * wave : 3 * wave + 3]:
            scatter.finish(phase)

    def share(wave):
        for scatter in scatters[3 * wave : 3 * wave + 3]:
            scatter.share()

    def store(wave):
        for scatter in scatters[3 * wave : 3 * wave + 3]:
            scatter.store()

    pairs = {}
    for i in (3, 2, 1):
        pairs[i] = [
            Pair(place, copies, lefts_in[i], lefts[i]),
            Pair(place, copies, rights_in[i], rights[i], BLOCKS[i]),
        ]
    att_copy = copies.send(own_att, both_att.at[pl.ds(HALF, HALF)], place.along("z", 2))
    late = [Pair(place, copies, lefts_in[0], lefts[0])]
    weight_copy = copies.move(w_attend, weight)
    both_att[:HALF] = own_att[...]

    def meet(pair):
        for half in pair:
            half.wait()

    later = []

    def make(which):
        if which == 0:
            meet(late)
            make_parts(lefts[0], rights[0], of(0))
        elif which == 3:
            meet(pairs[3])
            make_tall_parts(lefts[3], rights[3], of(3))
        elif which == 2:
            meet(pairs[2])
            make_parts(lefts[2], rights[2], of(2, 2))
        else:
            meet(pairs[1])
            make_parts(lefts[2], rights[2], of(2, 1))
            make_parts(lefts[1], rights[1], of(1))

    def attention(which):
        if which == 0:
            att_copy.wait_recv()
            attention_back(projected, both_att, grad_proj, (0, HEADS // 4))
        else:
            attention_back(projected, both_att, grad_proj, (HEADS // 4, HEADS // 2))
            late.append(Pair(place, copies, grad_proj, rights[0], BLOCKS[0]))

    def input_gradient():
        weight_copy.wait()
        normal, scale = normal_parts(tokens[...].astype(F32))
        grad_first = jnp.concatenate(
            [
                lax.dot_general(
                    grad_proj[...], weight[start : start + 256], NT, preferred_element_type=F32
                )
                for start in range(0, D, 256)
            ],
            1,
        )
        back = grad_first * (1.0 + scale_one[...])
        tokens_grad[...] = grad_middle[...] + scale * (
            back
            - jnp.mean(back, -1, keepdims=True)
            - normal * jnp.mean(back * normal, -1, keepdims=True)
        )
        vector[...] = sums[...]
        for place_of, total in ((0, grad_first), (8, grad_first * normal)):
            total = jnp.sum(total, 0, keepdims=True)
            for row in range(8):
                vector[place_of + row : place_of + row + 1, :] = total[:, row * 128 : (row + 1) * 128]
        vector_sent[...] = vector[...].astype(BF16)
        later.append(copies.send(vector_sent, vector_got, place.along("z", 2)))

    gather = SmallGather(place, copies, whole)

    def vectors(which):
        if which == 0:
            later[0].wait_recv()
            whole[place.core, place.z_lo, place.at["x"], place.at["y"]] = (
                vector_sent[...].astype(F32) + vector_got[...].astype(F32)
            ).astype(BF16)
        if which < 4:
            gather.stage(which)
        else:
            gather.arrive()

    steps = {
        "M": make,
        "A": attention,
        "L": input_gradient,
        "G": vectors,
        "S": start,
        "F": forward,
        "N": finish,
        "H": share,
        "T": store,
    }
    for step in LEAVE_STEPS:
        steps[step[0]](*(int(number) for number in step[1:]))
    copies.drain()


def buffer_shapes():
    shapes = [(6, 4, 4, 16, QUARTER), (3, 4, 2, 16, QUARTER), (3, 2, 16, QUARTER)]
    return [pltpu.VMEM(shape, BF16) for shape in shapes]


def leave(lefts, rights, w_attend, projected, grad_att, tokens, grad_middle, scale_one, sums):
    outside = pl.BlockSpec(memory_space=pl.ANY)
    inside = pl.BlockSpec(memory_space=pltpu.VMEM)
    scratch = [pltpu.VMEM((SEQ, width), BF16) for width in LEFTS]
    scratch += [pltpu.VMEM((blocks, SEQ, 2 * QUARTER), BF16) for blocks in BLOCKS]
    scratch += [pltpu.VMEM((4, 4, 4, 2, 16, QUARTER), BF16)] * 12
    scratch += buffer_shapes() * 12
    scratch += [pltpu.VMEM((4, 16, QUARTER), BF16)] * 12
    scratch += [
        pltpu.VMEM((D, 3 * D), BF16),
        pltpu.VMEM((SEQ, D), BF16),
        pltpu.VMEM((HALF, 3 * D), BF16),
        pltpu.VMEM(sums.shape, F32),
        pltpu.VMEM(sums.shape, BF16),
        pltpu.VMEM(sums.shape, BF16),
    ]
    scratch += copy_scratch(12 * 15 + 4 + 9 + 10, 4 + 9 + 1 + 12)
    return pl.pallas_call(
        leave_kernel,
        out_shape=[jax.ShapeDtypeStruct((rows, columns), F32) for rows, columns in WEIGHTS]
        + [jax.ShapeDtypeStruct((2, 2, 4, 4) + sums.shape, BF16), jax.ShapeDtypeStruct((HALF, D), F32)],
        in_specs=[outside] * 8 + [inside] * 6,
        out_specs=[inside] * 6,
        scratch_shapes=scratch,
        compiler_params=pltpu.CompilerParams(
            collective_id=3, has_side_effects=True, vmem_limit_bytes=60 * 2**20
        ),
        name="leave",
    )(*lefts, *rights, w_attend, projected, grad_att, tokens, grad_middle, scale_one, sums)


def normalize(values):
    centre = values - jnp.mean(values, -1, keepdims=True)
    spread = jnp.mean(centre * centre, -1, keepdims=True)
    return centre * lax.rsqrt(spread + EPSILON)


def modulated(values, shift_vec, scale_vec):
    return normalize(values) * (1.0 + scale_vec) + shift_vec


def gelu_tanh(values):
    return jax.nn.gelu(values, approximate=True)


def sinusoid(step_ids):
    half_width = FREQ // 2
    freq_rates = jnp.exp(
        -math.log(10000.0) * jnp.arange(half_width, dtype=jnp.float32) / half_width
    )
    angles = step_ids.astype(jnp.float32)[:, None] * freq_rates[None, :]
    return jnp.concatenate([jnp.cos(angles), jnp.sin(angles)], axis=-1)


def per_device(
    tokens,
    labels,
    timesteps,
    cotangent,
    class_table,
    time_weight,
    modulate_weight,
    modulate_offset,
    attend_weight,
    output_weight,
    expand_weight,
    hidden_offset,
    contract_weight,
):
    shard_index = lax.axis_index("fsdp")
    offset_width = modulate_offset.shape[1]
    placed = lax.dynamic_update_slice(
        jnp.zeros((1, 6 * D), F32),
        modulate_offset.astype(F32),
        (jnp.int32(0), shard_index * offset_width),
    )
    lane = lax.broadcasted_iota(jnp.int32, (1, 128), 1)
    own_bias = jnp.where(
        lax.div(lane, 64) == lax.rem(shard_index, 2), jnp.tile(hidden_offset.astype(F32), (1, 2)), 0.0
    )
    own_ids = jnp.concatenate(
        [
            own_bias,
            jnp.broadcast_to(labels[0].astype(F32), (1, 128)),
            sinusoid(timesteps).astype(BF16).astype(F32).reshape(2, 128),
            jnp.zeros((4, 128), F32),
        ],
        0,
    )
    full, (modulation, labels, sinus, bias, cond_cols, first_in, projected, attended) = enter(
        (attend_weight[0], output_weight[0], expand_weight[0], contract_weight[0]),
        tokens[0],
        class_table.T,
        time_weight.T,
        modulate_weight[0],
        own_ids,
        placed,
    )
    w_attend, w_output, w_expand, w_contract = full
    b_hidden = bias.reshape(FF)
    onehot = labels[:, :1].astype(jnp.int32) == jnp.arange(CLASSES, dtype=jnp.int32)[None, :]
    sinus_rows = jnp.concatenate([sinus[0], sinus[1]], 1)
    act_cols = jax.nn.silu(cond_cols).astype(BF16)
    _, scale_one, gate_one, shift_two, scale_two, gate_two = [modulation[i] for i in range(6)]

    hidden = tokens[0].astype(F32)
    branch_one = jnp.dot(attended, w_output, preferred_element_type=F32)
    middle = hidden + gate_one * branch_one
    second_in = modulated(middle, shift_two, scale_two).astype(BF16)
    pre_act = jnp.dot(second_in, w_expand, preferred_element_type=F32) + b_hidden
    activated = gelu_tanh(pre_act).astype(BF16)
    branch_two = jnp.dot(activated, w_contract, preferred_element_type=F32)
    result = (middle + gate_two * branch_two).astype(BF16)[None]

    grad_hidden = cotangent[0].astype(F32)
    grad_two = (grad_hidden * gate_two).astype(BF16)
    gate_two_grad = jnp.sum(grad_hidden * branch_two, 0)
    grad_act = jnp.einsum("td,fd->tf", grad_two, w_contract, preferred_element_type=F32)
    _, gelu_pull = jax.vjp(gelu_tanh, pre_act)
    grad_pre = gelu_pull(grad_act)[0].astype(BF16)
    hidden_term = jnp.sum(grad_pre.astype(F32), 0)
    grad_second = jnp.einsum("tf,df->td", grad_pre, w_expand, preferred_element_type=F32)
    _, second_pull = jax.vjp(modulated, middle, shift_two, scale_two)
    grad_middle, shift_two_grad, scale_two_grad = second_pull(grad_second)
    grad_middle = grad_hidden + grad_middle
    grad_one = (grad_middle * gate_one).astype(BF16)
    gate_one_grad = jnp.sum(grad_middle * branch_one, 0)
    grad_att = jnp.einsum("te,de->td", grad_one, w_output, preferred_element_type=F32).astype(BF16)
    sums = jnp.concatenate(
        [
            jnp.zeros((2 * D,), F32),
            gate_one_grad,
            shift_two_grad,
            scale_two_grad,
            gate_two_grad,
            hidden_term,
        ]
    ).reshape(80, 128)
    attend_grad, output_grad, expand_grad, contract_grad, all_vectors, tokens_grad = leave(
        (first_in, attended, second_in, activated),
        (grad_one, grad_pre, grad_two),
        w_attend,
        projected,
        grad_att,
        tokens[0],
        grad_middle,
        scale_one[None],
        sums,
    )
    all_vectors = all_vectors.reshape(64, 80 * 128)
    all_mod = all_vectors[:, : 6 * D]
    own_hidden = lax.dynamic_slice_in_dim(all_vectors, 6 * D + shard_index * (FF // 64), FF // 64, 1)
    hidden_grad = jnp.sum(own_hidden.astype(F32), 0)
    grad_act_cols = jnp.einsum("bk,dk->bd", all_mod, modulate_weight[0], preferred_element_type=F32)
    modulate_grad = jnp.einsum("bd,bk->dk", act_cols, all_mod, preferred_element_type=F32)
    own_cols = lax.dynamic_slice_in_dim(all_mod, shard_index * offset_width, offset_width, 1)
    offset_grad = jnp.sum(own_cols.astype(F32), 0)
    _, silu_pull = jax.vjp(jax.nn.silu, cond_cols)
    grad_cond = silu_pull(grad_act_cols)[0]
    table_grad = jnp.einsum("bc,bd->cd", onehot.astype(F32), grad_cond, precision=HIGHEST)
    time_grad = jnp.einsum("bf,bd->fd", sinus_rows, grad_cond, precision=HIGHEST)
    return (
        result,
        tokens_grad[None],
        table_grad,
        time_grad,
        modulate_grad[None],
        offset_grad[None],
        attend_grad[None],
        output_grad[None],
        expand_grad[None],
        hidden_grad[None],
        contract_grad[None],
    )


def solution(mesh):
    rows = P(None, "fsdp", None)
    columns = P(None, "fsdp")
    halves = P("fsdp", "ctx", None)
    each = P("fsdp")
    in_specs = (
        halves, each, each, halves, columns, columns, rows, columns, rows, rows, rows, columns, rows,
    )
    out_specs = (
        halves, halves, columns, columns, rows, columns, rows, rows, rows, columns, rows,
    )
    return jax.shard_map(
        per_device, mesh=mesh, in_specs=in_specs, out_specs=out_specs, check_vma=False
    )
```

```python
import functools
import math

import jax
import jax.numpy as jnp
from jax import lax
from jax.experimental import pallas as pl
from jax.experimental.pallas import tpu as pltpu
from jax.sharding import PartitionSpec as P

D = 1024
HEADS = 16
HEAD = 64
FF = 4096
CLASSES = 1000
FREQ = 256
SEQ = 256
HALF = SEQ // 2

WEIGHTS = ((16, 3 * D), (16, D), (16, FF), (64, D))
ORDERS = ("zyx", "xzy", "yxz")
WAVES = tuple(
    tuple((weight, row, column, order) for (weight, row, column), order in zip(wave, ORDERS))
    for wave in (
        ((0, 0, 0), (0, 0, D), (0, 0, 2 * D)),
        ((1, 0, 0), (2, 0, 0), (2, 0, D)),
        ((2, 0, 2 * D), (2, 0, 3 * D), (3, 0, 0)),
        ((3, 16, 0), (3, 32, 0), (3, 48, 0)),
    )
)
UNITS = tuple(unit for wave in WAVES for unit in wave)
QUARTER = D // 4

HIGHEST = lax.Precision.HIGHEST
EPSILON = 1e-06
MESH = pl.DeviceIdType.MESH
BF16 = jnp.bfloat16
F32 = jnp.float32
NT = (((1,), (1,)), ((), ()))
TN = (((0,), (0,)), ((), ()))


class Place:
    def __init__(self):
        shard = lax.axis_index("fsdp")
        self.z_hi = lax.axis_index("ctx")
        self.core = lax.rem(shard, 2)
        self.z_lo = lax.div(shard, 32)
        self.at = {
            "x": lax.rem(lax.div(shard, 8), 4),
            "y": lax.rem(lax.div(shard, 2), 4),
            "z": 2 * self.z_hi + self.z_lo,
        }

    def step(self, axis, distance):
        return lax.rem(self.at[axis] + distance + 4, 4)

    def device(self, core=None, **moved):
        at = {**self.at, **moved}
        core = self.core if core is None else core
        shard = ((lax.rem(at["z"], 2) * 4 + at["x"]) * 4 + at["y"]) * 2 + core
        return (shard, lax.div(at["z"], 2))

    def along(self, axis, distance):
        return self.device(**{axis: self.step(axis, distance)})

    def other_core(self):
        return self.device(core=1 - self.core)

    def other_z_lo(self):
        return self.device(z=2 * self.z_hi + 1 - self.z_lo)

    def everyone(self):
        ids = [self.other_core()]
        for axis in "xyz":
            ids += [self.along(axis, distance) for distance in (1, 2, 3)]
        return ids


def greet(ids):
    barrier = pltpu.get_barrier_semaphore()
    for device in ids:
        pl.semaphore_signal(barrier, inc=1, device_id=device, device_id_type=MESH)
    pl.semaphore_wait(barrier, len(ids))


class Copies:
    def __init__(self, send_sems, recv_sems, local_sems):
        self.send_sems, self.recv_sems, self.local_sems = send_sems, recv_sems, local_sems
        self.remote, self.local = [], []

    def send(self, source, target, device):
        slot = len(self.remote)
        copy = pltpu.make_async_remote_copy(
            src_ref=source,
            dst_ref=target,
            send_sem=self.send_sems.at[slot],
            recv_sem=self.recv_sems.at[slot],
            device_id=device,
            device_id_type=MESH,
        )
        copy.start()
        self.remote.append(copy)
        return copy

    def move(self, source, target):
        slot = len(self.local)
        copy = pltpu.make_async_copy(source, target, self.local_sems.at[slot])
        copy.start()
        self.local.append(copy)
        return copy

    def drain(self):
        for copy in self.remote:
            copy.wait_send()


def copy_scratch(remote, local):
    return [
        pltpu.SemaphoreType.DMA((remote,)),
        pltpu.SemaphoreType.DMA((remote,)),
        pltpu.SemaphoreType.DMA((max(local, 1),)),
    ]


class Gather:
    def __init__(self, place, copies, source, out, unit, direct):
        self.place, self.copies, self.source, self.out = place, copies, source, out
        self.direct = direct
        _, self.row, self.column, self.order = unit
        self.done = []
        self.to_core = []

    def region(self, half_index, core, **sel):
        lead = [sel.get(axis) for axis in "xy"]
        lead = [slice(None) if index is None else index for index in lead]
        z = sel.get("z")
        start, width = self.column + half_index * 2 * QUARTER, 2 * QUARTER
        z_lo = slice(None)
        if z is not None:
            width = QUARTER
            start = start + lax.div(z, 2) * QUARTER
            z_lo = lax.rem(z, 2)
        core = slice(None) if core is None else core
        rows = pl.ds(self.row, 16)
        return self.out.at[z_lo, lead[0], lead[1], core, rows, pl.ds(pl.multiple_of(start, 128), width)]

    def begin(self):
        place = self.place
        mine = self.column + (place.core * 2 + place.z_hi) * QUARTER
        theirs = self.column + ((1 - place.core) * 2 + place.z_hi) * QUARTER
        mine, theirs = pl.multiple_of(mine, 128), pl.multiple_of(theirs, 128)
        rows = pl.ds(self.row, 16)
        self.first = self.copies.send(
            self.source.at[rows, pl.ds(theirs, QUARTER)],
            self.region(1 - place.core, place.core, **place.at),
            place.other_core(),
        )
        self.own = self.copies.move(
            self.source.at[rows, pl.ds(mine, QUARTER)], self.region(place.core, place.core, **place.at)
        )

    def ready(self):
        self.first.wait_recv()
        self.own.wait()

    def block(self, axis, index, core):
        sel = {a: self.place.at[a] for a in "xyz" if a not in self.done}
        return self.region(self.place.core, core, **{**sel, axis: index})

    def pass_on(self, phase, index, core):
        if phase == 2:
            piece = self.block(self.order[2], index, core)
            self.to_core.append(self.copies.send(piece, piece, self.place.other_core()))

    def start(self, phase):
        axis, place = self.order[phase], self.place
        self.arriving = {}
        if phase in self.direct:
            piece = self.block(axis, place.at[axis], None)
            for distance in (1, 3, 2):
                self.arriving[distance] = self.copies.send(piece, piece, place.along(axis, distance))
            return
        for way, core in ((1, 0), (-1, 1), (1, 1), (-1, 0)):
            piece = self.block(axis, place.at[axis], core)
            self.arriving[way, core] = self.copies.send(piece, piece, place.along(axis, way))
        self.pass_on(phase, place.at[axis], None)

    def forward(self, phase):
        axis, place = self.order[phase], self.place
        self.last = {}
        for way, core in ((1, 0), (-1, 1)):
            self.arriving[way, core].wait_recv()
            piece = self.block(axis, place.step(axis, -way), core)
            self.last[way, core] = self.copies.send(piece, piece, place.along(axis, way))
            self.pass_on(phase, place.step(axis, -way), core)

    def finish(self, phase):
        axis, place = self.order[phase], self.place
        self.done.append(axis)
        if phase in self.direct:
            for copy in self.arriving.values():
                copy.wait_recv()
            return
        self.done.pop()
        for way, core in ((1, 1), (-1, 0)):
            self.arriving[way, core].wait_recv()
            self.pass_on(phase, place.step(axis, -way), core)
        for way, core in ((1, 0), (-1, 1)):
            self.last[way, core].wait_recv()
            self.pass_on(phase, place.step(axis, 2), core)
        self.done.append(axis)


class SmallGather:
    def __init__(self, place, copies, whole):
        self.place, self.copies, self.whole = place, copies, whole
        self.waiting = []

    def arrive(self):
        for copy in self.waiting:
            copy.wait_recv()
        self.waiting = []

    def stage(self, which):
        self.arrive()
        place, whole, send = self.place, self.whole, self.copies.send
        at, core = place.at, place.core
        if which == 0:
            piece = whole.at[core, place.z_lo, at["x"], at["y"]]
            self.waiting = [send(piece, piece, place.along("y", d)) for d in (1, 2, 3)]
        elif which == 1:
            piece = whole.at[core, place.z_lo, at["x"]]
            self.waiting = [send(piece, piece, place.along("x", d)) for d in (1, 2, 3)]
        elif which == 2:
            piece = whole.at[core, place.z_lo]
            self.waiting = [send(piece, piece, place.other_z_lo())]
        else:
            piece = whole.at[core]
            self.waiting = [send(piece, piece, place.other_core())]


def conditioned(ids, class_table, time_weight, labels, sinus, bias):
    def body(row, _):
        core, z_lo = lax.div(row, 32), lax.rem(lax.div(row, 16), 2)
        x, y = lax.rem(lax.div(row, 4), 4), lax.rem(row, 4)
        labels[pl.ds(row, 1), :] = ids[core, z_lo, x, y, 1:2, :]
        for half in range(2):
            sinus[half, pl.ds(row, 1), :] = ids[core, z_lo, x, y, 2 + half : 3 + half, :]
        return 0

    def join(row, _):
        z_lo, x, y = lax.div(row, 16), lax.rem(lax.div(row, 4), 4), lax.rem(row, 4)
        bias[pl.ds(row, 1), :] = ids[0, z_lo, x, y, 0:1, :] + ids[1, z_lo, x, y, 0:1, :]
        return 0

    lax.fori_loop(0, 32, join, 0)

    lax.fori_loop(0, 64, body, 0)
    cond = jnp.zeros((64, 16), F32)
    lane = lax.broadcasted_iota(jnp.int32, (64, 128), 1).astype(F32)
    for start in range(0, CLASSES, 128):
        width = min(128, CLASSES - start)
        chosen = jnp.where(labels[...] == lane + float(start), 1.0, 0.0).astype(BF16)
        cond += lax.dot_general(
            chosen[:, :width], class_table[:, start : start + width], NT, preferred_element_type=F32
        )
    for half in range(2):
        cond += lax.dot_general(
            sinus[half].astype(BF16),
            time_weight[:, half * 128 : half * 128 + 128],
            NT,
            preferred_element_type=F32,
        )
    return cond


def attention_forward(projected, attended, pairs):
    low = lax.broadcasted_iota(jnp.int32, (1, 128), 1) < HEAD

    def body(pair, _):
        def columns(part):
            return pl.ds(pl.multiple_of(part * D + pair * 128, 128), 128)

        query = projected[:HALF, columns(0)] * jnp.asarray(HEAD ** (-0.5), BF16)
        key = projected[:, columns(1)]
        value = projected[:, columns(2)]
        pieces = []
        for mine in (low, jnp.logical_not(low)):
            scores = lax.dot_general(
                jnp.where(mine, query, jnp.zeros((), BF16)), key, NT, preferred_element_type=F32
            )
            terms = jnp.exp(scores - jnp.max(scores, -1, keepdims=True))
            probs = terms * (1.0 / jnp.sum(terms, -1, keepdims=True))
            pieces.append(jnp.dot(probs.astype(BF16), value, preferred_element_type=F32))
        attended[:, columns(0)] = jnp.where(low, *pieces).astype(BF16)
        return 0

    lax.fori_loop(*pairs, body, 0)


def normal_parts(values):
    centre = values - jnp.mean(values, -1, keepdims=True)
    scale = lax.rsqrt(jnp.mean(centre * centre, -1, keepdims=True) + EPSILON)
    return centre * scale, scale


def enter_kernel(
    w0, w1, w2, w3, tokens_in, class_in, time_in, modulate_in, own_ids, placed,
    o0, o1, o2, o3, modulation, labels, sinus, bias, cond, first_in, projected, attended,
    ids, other_tokens, w_attend,
    partial_mod, got_core, sum_core, got_z, slabs, sum_z, got_x, sum_x, got_y, both_first,
    tokens, class_table, time_weight, modulate_weight,
    send_sems, recv_sems, local_sems,
):
    place = Place()
    copies = Copies(send_sems, recv_sems, local_sems)
    sources, wholes = (w0, w1, w2, w3), (o0, o1, o2, o3)
    waves = [
        [
            Gather(place, copies, sources[unit[0]], wholes[unit[0]], unit, (0, 1) if index == 0 else (0,))
            for unit in wave
        ]
        for index, wave in enumerate(WAVES)
    ]
    gathers = [gather for wave in waves for gather in wave]

    def start(wave, phase):
        for gather in waves[wave]:
            gather.start(phase)

    def forward(wave, phase):
        for gather in waves[wave]:
            gather.forward(phase)

    def finish(wave, phase):
        for gather in waves[wave]:
            gather.finish(phase)

    operands = [
        copies.move(source, target)
        for source, target in (
            (class_in, class_table),
            (time_in, time_weight),
            (modulate_in, modulate_weight),
            (tokens_in, tokens),
        )
    ]
    ids[place.core, place.z_lo, place.at["x"], place.at["y"]] = own_ids[...]
    greet(place.everyone())
    id_gather = SmallGather(place, copies, ids)
    id_gather.stage(0)
    for gather in gathers:
        gather.begin()
    tokens_copy = copies.send(tokens_in, other_tokens, place.along("z", 2))
    id_gather.stage(1)
    for gather in gathers:
        gather.ready()
        gather.start(0)
    id_gather.stage(2)
    for wave in range(2):
        finish(wave, 0)
        start(wave, 1)
    id_gather.stage(3)
    for wave in range(2, 4):
        finish(wave, 0)
        start(wave, 1)
    id_gather.arrive()
    finish(0, 1)
    start(0, 2)

    for copy in operands:
        copy.wait()
    cond[...] = conditioned(ids, class_table, time_weight, labels, sinus, bias)
    act = (cond[...] / (1.0 + jnp.exp(-cond[...]))).astype(BF16)
    for column in range(0, 6 * D, D):
        columns = slice(column, column + D)
        partial_mod[:, columns] = (
            jnp.dot(act, modulate_weight[:, columns], preferred_element_type=F32) + placed[:, columns]
        ).astype(BF16)

    def share(index, count):
        return pl.ds(pl.multiple_of(index * count, count), count)

    mod_core = copies.send(partial_mod.at[share(1 - place.core, 32)], got_core, place.other_core())
    for wave in (1, 2, 3):
        forward(wave, 1)
    mod_core.wait_recv()
    sum_core[...] = (
        partial_mod[share(place.core, 32)].astype(F32) + got_core[...].astype(F32)
    ).astype(BF16)
    mod_z = copies.send(sum_core.at[share(1 - place.z_lo, 16)], got_z, place.other_z_lo())
    finish(1, 1)
    start(1, 2)
    mod_z.wait_recv()
    for row in range(48):
        columns = slice(row * 128, row * 128 + 128)
        slabs[:, row, :] = sum_core[share(place.z_lo, 16), columns].astype(F32) + got_z[
            :, columns
        ].astype(F32)
    sum_z[...] = slabs[...].astype(BF16).reshape(4, 4, 48, 128)
    mod_x = [
        copies.send(sum_z.at[place.step("x", distance)], got_x.at[distance - 1], place.along("x", distance))
        for distance in (1, 2, 3)
    ]
    finish(2, 1)
    forward(0, 2)
    start(2, 2)
    for copy in mod_x:
        copy.wait_recv()
    for y in range(4):
        total = sum_z[place.at["x"], y].astype(F32)
        for slot in range(3):
            total += got_x[slot, y].astype(F32)
        sum_x[y] = total.astype(BF16)
    mod_y = [
        copies.send(sum_x.at[place.step("y", distance)], got_y.at[distance - 1], place.along("y", distance))
        for distance in (1, 2, 3)
    ]
    finish(3, 1)
    finish(0, 2)
    for gather in waves[0]:
        for copy in gather.to_core:
            copy.wait_recv()
    weight_copy = copies.move(o0, w_attend)
    forward(1, 2)
    start(3, 2)
    for copy in mod_y:
        copy.wait_recv()
    total = sum_x[place.at["y"]].astype(F32)
    for slot in range(3):
        total += got_y[slot].astype(F32)
    for row in range(48):
        vector, lane = divmod(row, 8)
        modulation[vector : vector + 1, lane * 128 : lane * 128 + 128] = total[row : row + 1]
    tokens_copy.wait_recv()
    for row, source in enumerate((tokens, other_tokens)):
        normal, _ = normal_parts(source[...].astype(F32))
        both_first[row * HALF : row * HALF + HALF] = (
            normal * (1.0 + modulation[1:2]) + modulation[0:1]
        ).astype(BF16)
    first_in[...] = both_first[:HALF]
    forward(2, 2)
    weight_copy.wait()
    for column in range(0, 3 * D, 512):
        columns = slice(column, column + 512)
        projected[:, columns] = jnp.dot(
            both_first[...],
            w_attend[:, :, :, :, :, columns].reshape(D, 512),
            preferred_element_type=F32,
        ).astype(BF16)
    finish(1, 2)
    forward(3, 2)
    attention_forward(projected, attended, (0, HEADS // 4))
    finish(2, 2)
    attention_forward(projected, attended, (HEADS // 4, HEADS // 2))
    finish(3, 2)
    for wave in waves[1:]:
        for gather in wave:
            for copy in gather.to_core:
                copy.wait_recv()
    copies.drain()


def enter(weights, tokens, class_table, time_weight, modulate_weight, own_ids, placed):
    outside = pl.BlockSpec(memory_space=pl.ANY)
    inside = pl.BlockSpec(memory_space=pltpu.VMEM)
    slab = (48, 128)
    shapes = [jax.ShapeDtypeStruct((2, 4, 4, 2, rows, columns), BF16) for rows, columns in WEIGHTS]
    shapes += [
        jax.ShapeDtypeStruct((6, D), F32),
        jax.ShapeDtypeStruct((64, 128), F32),
        jax.ShapeDtypeStruct((2, 64, 128), F32),
        jax.ShapeDtypeStruct((32, 128), F32),
        jax.ShapeDtypeStruct((64, 16), F32),
        jax.ShapeDtypeStruct((HALF, D), BF16),
        jax.ShapeDtypeStruct((SEQ, 3 * D), BF16),
        jax.ShapeDtypeStruct((HALF, D), BF16),
    ]
    out = pl.pallas_call(
        enter_kernel,
        out_shape=shapes,
        in_specs=[outside] * 8 + [inside] * 2,
        out_specs=[outside] * 4 + [inside] * 8,
        scratch_shapes=[
            pltpu.VMEM((2, 2, 4, 4, 8, 128), F32),
            pltpu.VMEM((HALF, D), BF16),
            pltpu.VMEM((2, 4, 4, 2, 16, 3 * D), BF16),
            pltpu.VMEM((64, 6 * D), BF16),
            pltpu.VMEM((32, 6 * D), BF16),
            pltpu.VMEM((32, 6 * D), BF16),
            pltpu.VMEM((16, 6 * D), BF16),
            pltpu.VMEM((16,) + slab, F32),
            pltpu.VMEM((4, 4) + slab, BF16),
            pltpu.VMEM((3, 4) + slab, BF16),
            pltpu.VMEM((4,) + slab, BF16),
            pltpu.VMEM((3,) + slab, BF16),
            pltpu.VMEM((SEQ, D), BF16),
            pltpu.VMEM((HALF, D), BF16),
            pltpu.VMEM((16, CLASSES), BF16),
            pltpu.VMEM((16, FREQ), BF16),
            pltpu.VMEM((16, 6 * D), BF16),
        ]
        + copy_scratch(12 * 23 + 9 + 8, 17),
        compiler_params=pltpu.CompilerParams(
            collective_id=0, has_side_effects=True, vmem_limit_bytes=60 * 2**20
        ),
        name="enter",
    )(*weights, tokens, class_table, time_weight, modulate_weight, own_ids, placed)
    full = [whole.reshape(64 * rows, columns) for whole, (rows, columns) in zip(out[:4], WEIGHTS)]
    return full, out[4:]


class Pair:
    def __init__(self, place, copies, source, both, blocks=None):
        self.copies = []
        other = place.other_core()
        if blocks is None:
            self.copies.append(copies.send(source, both.at[pl.ds(HALF, HALF)], other))
            self.copies.append(copies.move(source, both.at[pl.ds(0, HALF)]))
            return
        for block in range(blocks):
            mine = pl.multiple_of(block * D + place.core * 2 * QUARTER, 128)
            theirs = pl.multiple_of(block * D + (1 - place.core) * 2 * QUARTER, 128)
            width = 2 * QUARTER
            self.copies.append(
                copies.send(source.at[:, pl.ds(theirs, width)], both.at[block, pl.ds(HALF, HALF)], other)
            )
            self.copies.append(
                copies.move(source.at[:, pl.ds(mine, width)], both.at[block, pl.ds(0, HALF)])
            )

    def wait(self):
        for index, copy in enumerate(self.copies):
            if index % 2:
                copy.wait()
            else:
                copy.wait_recv()


def make_parts(left, right, scatters):
    def body(i, _):
        z_lo, x = lax.div(i, 4), lax.rem(i, 4)
        chosen = left[:, pl.ds(pl.multiple_of(i * 128, 128), 128)]
        for scatter in scatters:
            made = lax.dot_general(
                chosen, right[scatter.column // D], TN, preferred_element_type=F32
            ).astype(BF16)
            for q in range(2):
                scatter.parts[2 * q + z_lo, x] = made[:, q * QUARTER : (q + 1) * QUARTER].reshape(
                    4, 2, 16, QUARTER
                )
        return 0

    lax.fori_loop(0, 8, body, 0)


def make_tall_parts(left, right, scatters):
    def body(i, _):
        z_lo, x = lax.div(i, 4), lax.rem(i, 4)
        chosen = left[:, pl.ds(pl.multiple_of(i * 512, 128), 512)]
        made = lax.dot_general(chosen, right[0], TN, preferred_element_type=F32).astype(BF16)
        made = made.reshape(4, 2, 64, 2 * QUARTER)
        for scatter in scatters:
            rows = made[:, :, scatter.row : scatter.row + 16]
            for q in range(2):
                scatter.parts[2 * q + z_lo, x] = rows[..., q * QUARTER : (q + 1) * QUARTER]
        return 0

    lax.fori_loop(0, 8, body, 0)


class Scatter:
    def __init__(self, place, copies, unit, parts, bufs, final, out):
        self.place, self.copies = place, copies
        _, self.row, self.column, order = unit
        self.order = order[::-1]
        self.parts, self.bufs, self.final, self.out = parts, bufs, final, out
        self.done = []

    def sel(self, axis, index):
        at = {a: self.place.at[a] if a in self.done else None for a in "xyz"}
        at[axis] = index
        return [at[a] for a in "zxy"]

    def block(self, axis, index, core):
        lead = [slice(None) if i is None else i for i in self.sel(axis, index)]
        return self.parts.at[(*lead, core)]

    def add(self, axis, index, core, bufs):
        sel = self.sel(axis, index)
        free = [i for i, s in enumerate(sel) if s is None]

        def body(step, _):
            where = [slice(None) if s is None else s for s in sel]
            inner = (slice(None),) * len(free)
            if len(free) == 2:
                where[free[0]], inner = step, (step, slice(None))
            if core is not None:
                where.append(core)
            total = self.parts[tuple(where)].astype(F32)
            for buf in bufs:
                total += buf[inner].astype(F32)
            self.parts[tuple(where)] = total.astype(BF16)
            return 0

        if len(free) == 2:
            lax.fori_loop(0, 4, body, 0)
        else:
            body(0, 0)

    def start(self, phase):
        axis, place = self.order[phase], self.place
        buf = self.bufs[phase]
        send = self.copies.send
        if phase > 0:
            self.direct = [
                send(
                    self.block(axis, place.step(axis, distance), slice(None)),
                    buf.at[distance - 1],
                    place.along(axis, distance),
                )
                for distance in (1, 3, 2)
            ]
            return
        up, down = place.along(axis, 1), place.along(axis, -1)
        far = place.step(axis, 2)
        self.far = {
            1: send(self.block(axis, far, 0), buf.at[0], up),
            -1: send(self.block(axis, far, 1), buf.at[1], down),
        }
        self.raw = {
            1: send(self.block(axis, place.step(axis, 1), 1), buf.at[3], up),
            -1: send(self.block(axis, place.step(axis, -1), 0), buf.at[2], down),
        }

    def forward(self):
        axis, place = self.order[0], self.place
        buf = self.bufs[0]
        self.near = {}
        for way, core in ((1, 0), (-1, 1)):
            self.far[way].wait_recv()
            index = place.step(axis, way)
            self.add(axis, index, core, [buf.at[core]])
            self.near[way] = self.copies.send(
                self.block(axis, index, core), buf.at[4 + core], place.along(axis, way)
            )

    def finish(self, phase):
        axis, place = self.order[phase], self.place
        buf = self.bufs[phase]
        if phase > 0:
            for copy in self.direct:
                copy.wait_recv()
            self.add(axis, place.at[axis], None, [buf.at[slot] for slot in range(3)])
        else:
            for way, core in ((1, 0), (-1, 1)):
                self.raw[-way].wait_recv()
                self.near[way].wait_recv()
                self.add(axis, place.at[axis], core, [buf.at[2 + core], buf.at[4 + core]])
        self.done.append(axis)

    def share(self):
        place, at = self.place, self.place.at
        slot = place.core * 2 + place.z_hi
        mine = self.parts.at[at["z"], at["x"], at["y"], place.core]
        theirs = self.parts.at[at["z"], at["x"], at["y"], 1 - place.core]
        far = place.step("z", 2)
        target = self.final.at[slot]
        self.shared = [
            self.copies.send(theirs, target, place.other_core()),
            self.copies.send(mine, target, place.device(z=far)),
            self.copies.send(theirs, target, place.device(z=far, core=1 - place.core)),
        ]
        self.kept = self.copies.move(mine, target)

    def store(self):
        for copy in self.shared:
            copy.wait_recv()
        self.kept.wait()
        for slot in range(4):
            start = self.column + slot * QUARTER
            self.out[self.row : self.row + 16, start : start + QUARTER] = self.final[slot].astype(F32)


LEFTS = (D, D, D, FF)
BLOCKS = (3, 1, 4, 1)


def attention_back(projected, grad_att, grad_proj, pairs):
    low = lax.broadcasted_iota(jnp.int32, (1, 128), 1) < HEAD

    def body(pair, _):
        def columns(part):
            return pl.ds(pl.multiple_of(part * D + pair * 128, 128), 128)

        query = projected[:, columns(0)] * jnp.asarray(HEAD ** (-0.5), BF16)
        key = projected[:, columns(1)]
        value = projected[:, columns(2)]
        grad = grad_att[:, columns(0)]
        zero = jnp.zeros((), BF16)
        pieces = []
        for mine in (low, jnp.logical_not(low)):
            scores = lax.dot_general(
                jnp.where(mine, query, zero), key, NT, preferred_element_type=F32
            )
            terms = jnp.exp(scores - jnp.max(scores, -1, keepdims=True))
            probs = terms * (1.0 / jnp.sum(terms, -1, keepdims=True))
            grad_probs = lax.dot_general(
                jnp.where(mine, grad, zero), value, NT, preferred_element_type=F32
            )
            inner = jnp.sum(probs * grad_probs, -1, keepdims=True)
            grad_scores = (probs * (grad_probs - inner)).astype(BF16)
            rounded = probs.astype(BF16)
            pieces.append(
                (
                    jnp.dot(grad_scores[:HALF], key, preferred_element_type=F32) * HEAD ** (-0.5),
                    lax.dot_general(grad_scores[:, :HALF], query, TN, preferred_element_type=F32),
                    lax.dot_general(rounded[:, :HALF], grad, TN, preferred_element_type=F32),
                )
            )
        for part in range(3):
            both = jnp.where(low, pieces[0][part], pieces[1][part])
            grad_proj[:, columns(part)] = both.astype(BF16)
        return 0

    lax.fori_loop(*pairs, body, 0)


LEAVE_STEPS = (
    "M3", "S30", "M2", "S20", "A0", "F3", "A1", "F2", "M1", "S10",
    "M0", "S00", "F1", "L", "N30", "S31", "F0", "N20", "S21", "N10",
    "S11", "G0", "N00", "S01", "N31", "S32", "N21", "S22", "N11", "S12",
    "G1", "N01", "S02", "N32", "H3", "N22", "H2", "G2", "N12", "H1",
    "N02", "H0", "G3", "T3", "T2", "T1", "G4", "T0",
)


def leave_kernel(*refs):
    refs = list(refs)

    def take(count):
        taken, refs[:count] = refs[:count], []
        return taken

    lefts_in, rights_in = take(4), take(3)
    w_attend, projected, own_att, tokens, grad_middle, scale_one, sums = take(7)
    outs = take(4)
    whole, tokens_grad = take(2)
    lefts, rights, parts = take(4), take(4), take(12)
    bufs = [take(3) for _ in range(12)]
    finals = take(12)
    weight, both_att, grad_proj, vector, vector_sent, vector_got = take(6)
    send_sems, recv_sems, local_sems = refs
    place = Place()
    copies = Copies(send_sems, recv_sems, local_sems)
    far = place.step("z", 2)
    rights_in = [grad_proj] + rights_in
    greet(place.everyone() + [place.device(z=far, core=1 - place.core)])
    scatters = [
        Scatter(place, copies, UNITS[i], parts[i], bufs[i], finals[i], outs[UNITS[i][0]]) for i in range(12)
    ]

    def of(weight_index, wave=None):
        return [
            scatters[i]
            for i in range(12)
            if UNITS[i][0] == weight_index and wave in (None, i // 3)
        ]

    def start(wave, phase):
        for scatter in scatters[3 * wave : 3 * wave + 3]:
            scatter.start(phase)

    def forward(wave):
        for scatter in scatters[3 * wave : 3 * wave + 3]:
            scatter.forward()

    def finish(wave, phase):
        for scatter in scatters[3 * wave : 3 * wave + 3]:
            scatter.finish(phase)

    def share(wave):
        for scatter in scatters[3 * wave : 3 * wave + 3]:
            scatter.share()

    def store(wave):
        for scatter in scatters[3 * wave : 3 * wave + 3]:
            scatter.store()

    pairs, late, later = {}, [], []

    def begin_pairs(which):
        for i in which:
            pairs[i] = [
                Pair(place, copies, lefts_in[i], lefts[i]),
                Pair(place, copies, rights_in[i], rights[i], BLOCKS[i]),
            ]

    begin_pairs((3,))
    att_copy = copies.send(own_att, both_att.at[pl.ds(HALF, HALF)], place.along("z", 2))
    both_att[:HALF] = own_att[...]

    def meet(pair):
        for half in pair:
            half.wait()

    def make(which):
        if which == 0:
            meet(late)
            make_parts(lefts[0], rights[0], of(0))
        elif which == 3:
            meet(pairs[3])
            begin_pairs((2, 1))
            late.append(Pair(place, copies, lefts_in[0], lefts[0]))
            make_tall_parts(lefts[3], rights[3], of(3))
        elif which == 2:
            meet(pairs[2])
            later.append(copies.move(w_attend, weight))
            make_parts(lefts[2], rights[2], of(2, 2))
        else:
            meet(pairs[1])
            make_parts(lefts[2], rights[2], of(2, 1))
            make_parts(lefts[1], rights[1], of(1))

    def attention(which):
        if which == 0:
            att_copy.wait_recv()
            attention_back(projected, both_att, grad_proj, (0, HEADS // 4))
        else:
            attention_back(projected, both_att, grad_proj, (HEADS // 4, HEADS // 2))
            late.append(Pair(place, copies, grad_proj, rights[0], BLOCKS[0]))

    def input_gradient():
        later[0].wait()
        normal, scale = normal_parts(tokens[...].astype(F32))
        grad_first = jnp.concatenate(
            [
                lax.dot_general(
                    grad_proj[...], weight[start : start + 256], NT, preferred_element_type=F32
                )
                for start in range(0, D, 256)
            ],
            1,
        )
        back = grad_first * (1.0 + scale_one[...])
        tokens_grad[...] = grad_middle[...] + scale * (
            back
            - jnp.mean(back, -1, keepdims=True)
            - normal * jnp.mean(back * normal, -1, keepdims=True)
        )
        vector[...] = sums[...]
        for place_of, total in ((0, grad_first), (8, grad_first * normal)):
            total = jnp.sum(total, 0, keepdims=True)
            for row in range(8):
                vector[place_of + row : place_of + row + 1, :] = total[:, row * 128 : (row + 1) * 128]
        vector_sent[...] = vector[...].astype(BF16)
        later.append(copies.send(vector_sent, vector_got, place.along("z", 2)))

    gather = SmallGather(place, copies, whole)

    def vectors(which):
        if which == 0:
            later[1].wait_recv()
            whole[place.core, place.z_lo, place.at["x"], place.at["y"]] = (
                vector_sent[...].astype(F32) + vector_got[...].astype(F32)
            ).astype(BF16)
        if which < 4:
            gather.stage(which)
        else:
            gather.arrive()

    steps = {
        "M": make,
        "A": attention,
        "L": input_gradient,
        "G": vectors,
        "S": start,
        "F": forward,
        "N": finish,
        "H": share,
        "T": store,
    }
    for step in LEAVE_STEPS:
        steps[step[0]](*(int(number) for number in step[1:]))
    copies.drain()


def buffer_shapes():
    shapes = [(6, 4, 4, 16, QUARTER), (3, 4, 2, 16, QUARTER), (3, 2, 16, QUARTER)]
    return [pltpu.VMEM(shape, BF16) for shape in shapes]


def leave(lefts, rights, w_attend, projected, grad_att, tokens, grad_middle, scale_one, sums):
    outside = pl.BlockSpec(memory_space=pl.ANY)
    inside = pl.BlockSpec(memory_space=pltpu.VMEM)
    scratch = [pltpu.VMEM((SEQ, width), BF16) for width in LEFTS]
    scratch += [pltpu.VMEM((blocks, SEQ, 2 * QUARTER), BF16) for blocks in BLOCKS]
    scratch += [pltpu.VMEM((4, 4, 4, 2, 16, QUARTER), BF16)] * 12
    scratch += buffer_shapes() * 12
    scratch += [pltpu.VMEM((4, 16, QUARTER), BF16)] * 12
    scratch += [
        pltpu.VMEM((D, 3 * D), BF16),
        pltpu.VMEM((SEQ, D), BF16),
        pltpu.VMEM((HALF, 3 * D), BF16),
        pltpu.VMEM(sums.shape, F32),
        pltpu.VMEM(sums.shape, BF16),
        pltpu.VMEM(sums.shape, BF16),
    ]
    scratch += copy_scratch(12 * 15 + 4 + 9 + 10, 4 + 9 + 1 + 12)
    return pl.pallas_call(
        leave_kernel,
        out_shape=[jax.ShapeDtypeStruct((rows, columns), F32) for rows, columns in WEIGHTS]
        + [jax.ShapeDtypeStruct((2, 2, 4, 4) + sums.shape, BF16), jax.ShapeDtypeStruct((HALF, D), F32)],
        in_specs=[outside] * 8 + [inside] * 6,
        out_specs=[inside] * 6,
        scratch_shapes=scratch,
        compiler_params=pltpu.CompilerParams(
            collective_id=3, has_side_effects=True, vmem_limit_bytes=60 * 2**20
        ),
        name="leave",
    )(*lefts, *rights, w_attend, projected, grad_att, tokens, grad_middle, scale_one, sums)


def normalize(values):
    centre = values - jnp.mean(values, -1, keepdims=True)
    spread = jnp.mean(centre * centre, -1, keepdims=True)
    return centre * lax.rsqrt(spread + EPSILON)


def modulated(values, shift_vec, scale_vec):
    return normalize(values) * (1.0 + scale_vec) + shift_vec


def gelu_tanh(values):
    return jax.nn.gelu(values, approximate=True)


def sinusoid(step_ids):
    half_width = FREQ // 2
    freq_rates = jnp.exp(
        -math.log(10000.0) * jnp.arange(half_width, dtype=jnp.float32) / half_width
    )
    angles = step_ids.astype(jnp.float32)[:, None] * freq_rates[None, :]
    return jnp.concatenate([jnp.cos(angles), jnp.sin(angles)], axis=-1)


def per_device(
    tokens,
    labels,
    timesteps,
    cotangent,
    class_table,
    time_weight,
    modulate_weight,
    modulate_offset,
    attend_weight,
    output_weight,
    expand_weight,
    hidden_offset,
    contract_weight,
):
    shard_index = lax.axis_index("fsdp")
    offset_width = modulate_offset.shape[1]
    placed = lax.dynamic_update_slice(
        jnp.zeros((1, 6 * D), F32),
        modulate_offset.astype(F32),
        (jnp.int32(0), shard_index * offset_width),
    )
    lane = lax.broadcasted_iota(jnp.int32, (1, 128), 1)
    own_bias = jnp.where(
        lax.div(lane, 64) == lax.rem(shard_index, 2), jnp.tile(hidden_offset.astype(F32), (1, 2)), 0.0
    )
    own_ids = jnp.concatenate(
        [
            own_bias,
            jnp.broadcast_to(labels[0].astype(F32), (1, 128)),
            sinusoid(timesteps).astype(BF16).astype(F32).reshape(2, 128),
            jnp.zeros((4, 128), F32),
        ],
        0,
    )
    full, (modulation, labels, sinus, bias, cond_cols, first_in, projected, attended) = enter(
        (attend_weight[0], output_weight[0], expand_weight[0], contract_weight[0]),
        tokens[0],
        class_table.T,
        time_weight.T,
        modulate_weight[0],
        own_ids,
        placed,
    )
    w_attend, w_output, w_expand, w_contract = full
    b_hidden = bias.reshape(FF)
    onehot = labels[:, :1].astype(jnp.int32) == jnp.arange(CLASSES, dtype=jnp.int32)[None, :]
    sinus_rows = jnp.concatenate([sinus[0], sinus[1]], 1)
    act_cols = jax.nn.silu(cond_cols).astype(BF16)
    _, scale_one, gate_one, shift_two, scale_two, gate_two = [modulation[i] for i in range(6)]

    hidden = tokens[0].astype(F32)
    branch_one = jnp.dot(attended, w_output, preferred_element_type=F32)
    middle = hidden + gate_one * branch_one
    second_in = modulated(middle, shift_two, scale_two).astype(BF16)
    pre_act = jnp.dot(second_in, w_expand, preferred_element_type=F32) + b_hidden
    activated = gelu_tanh(pre_act).astype(BF16)
    branch_two = jnp.dot(activated, w_contract, preferred_element_type=F32)
    result = (middle + gate_two * branch_two).astype(BF16)[None]

    grad_hidden = cotangent[0].astype(F32)
    grad_two = (grad_hidden * gate_two).astype(BF16)
    gate_two_grad = jnp.sum(grad_hidden * branch_two, 0)
    grad_act = jnp.einsum("td,fd->tf", grad_two, w_contract, preferred_element_type=F32)
    _, gelu_pull = jax.vjp(gelu_tanh, pre_act)
    grad_pre = gelu_pull(grad_act)[0].astype(BF16)
    hidden_term = jnp.sum(grad_pre.astype(F32), 0)
    grad_second = jnp.einsum("tf,df->td", grad_pre, w_expand, preferred_element_type=F32)
    _, second_pull = jax.vjp(modulated, middle, shift_two, scale_two)
    grad_middle, shift_two_grad, scale_two_grad = second_pull(grad_second)
    grad_middle = grad_hidden + grad_middle
    grad_one = (grad_middle * gate_one).astype(BF16)
    gate_one_grad = jnp.sum(grad_middle * branch_one, 0)
    grad_att = jnp.einsum("te,de->td", grad_one, w_output, preferred_element_type=F32).astype(BF16)
    sums = jnp.concatenate(
        [
            jnp.zeros((2 * D,), F32),
            gate_one_grad,
            shift_two_grad,
            scale_two_grad,
            gate_two_grad,
            hidden_term,
        ]
    ).reshape(80, 128)
    attend_grad, output_grad, expand_grad, contract_grad, all_vectors, tokens_grad = leave(
        (first_in, attended, second_in, activated),
        (grad_one, grad_pre, grad_two),
        w_attend,
        projected,
        grad_att,
        tokens[0],
        grad_middle,
        scale_one[None],
        sums,
    )
    all_vectors = all_vectors.reshape(64, 80 * 128)
    all_mod = all_vectors[:, : 6 * D]
    own_hidden = lax.dynamic_slice_in_dim(all_vectors, 6 * D + shard_index * (FF // 64), FF // 64, 1)
    hidden_grad = jnp.sum(own_hidden.astype(F32), 0)
    grad_act_cols = jnp.einsum("bk,dk->bd", all_mod, modulate_weight[0], preferred_element_type=F32)
    modulate_grad = jnp.einsum("bd,bk->dk", act_cols, all_mod, preferred_element_type=F32)
    own_cols = lax.dynamic_slice_in_dim(all_mod, shard_index * offset_width, offset_width, 1)
    offset_grad = jnp.sum(own_cols.astype(F32), 0)
    _, silu_pull = jax.vjp(jax.nn.silu, cond_cols)
    grad_cond = silu_pull(grad_act_cols)[0]
    table_grad = jnp.einsum("bc,bd->cd", onehot.astype(F32), grad_cond, precision=HIGHEST)
    time_grad = jnp.einsum("bf,bd->fd", sinus_rows, grad_cond, precision=HIGHEST)
    return (
        result,
        tokens_grad[None],
        table_grad,
        time_grad,
        modulate_grad[None],
        offset_grad[None],
        attend_grad[None],
        output_grad[None],
        expand_grad[None],
        hidden_grad[None],
        contract_grad[None],
    )


def solution(mesh):
    rows = P(None, "fsdp", None)
    columns = P(None, "fsdp")
    halves = P("fsdp", "ctx", None)
    each = P("fsdp")
    in_specs = (
        halves, each, each, halves, columns, columns, rows, columns, rows, rows, rows, columns, rows,
    )
    out_specs = (
        halves, halves, columns, columns, rows, columns, rows, rows, rows, columns, rows,
    )
    return jax.shard_map(
        per_device, mesh=mesh, in_specs=in_specs, out_specs=out_specs, check_vma=False
    )
```

```python
import functools
import math

import jax
import jax.numpy as jnp
from jax import lax
from jax.experimental import pallas as pl
from jax.experimental.pallas import tpu as pltpu
from jax.sharding import PartitionSpec as P

D = 1024
HEADS = 16
HEAD = 64
FF = 4096
CLASSES = 1000
FREQ = 256
SEQ = 256
HALF = SEQ // 2

WEIGHTS = ((16, 3 * D), (16, D), (16, FF), (64, D))
ORDERS = ("zyx", "xzy", "yxz")
WAVES = tuple(
    tuple((weight, row, column, order) for (weight, row, column), order in zip(wave, ORDERS))
    for wave in (
        ((0, 0, 0), (0, 0, D), (0, 0, 2 * D)),
        ((1, 0, 0), (2, 0, 0), (2, 0, D)),
        ((2, 0, 2 * D), (2, 0, 3 * D), (3, 0, 0)),
        ((3, 16, 0), (3, 32, 0), (3, 48, 0)),
    )
)
UNITS = tuple(unit for wave in WAVES for unit in wave)
QUARTER = D // 4

HIGHEST = lax.Precision.HIGHEST
EPSILON = 1e-06
MESH = pl.DeviceIdType.MESH
BF16 = jnp.bfloat16
F32 = jnp.float32
NT = (((1,), (1,)), ((), ()))
TN = (((0,), (0,)), ((), ()))


class Place:
    def __init__(self):
        shard = lax.axis_index("fsdp")
        self.z_hi = lax.axis_index("ctx")
        self.core = lax.rem(shard, 2)
        self.z_lo = lax.div(shard, 32)
        self.at = {
            "x": lax.rem(lax.div(shard, 8), 4),
            "y": lax.rem(lax.div(shard, 2), 4),
            "z": 2 * self.z_hi + self.z_lo,
        }

    def step(self, axis, distance):
        return lax.rem(self.at[axis] + distance + 4, 4)

    def device(self, core=None, **moved):
        at = {**self.at, **moved}
        core = self.core if core is None else core
        shard = ((lax.rem(at["z"], 2) * 4 + at["x"]) * 4 + at["y"]) * 2 + core
        return (shard, lax.div(at["z"], 2))

    def along(self, axis, distance):
        return self.device(**{axis: self.step(axis, distance)})

    def other_core(self):
        return self.device(core=1 - self.core)

    def other_z_lo(self):
        return self.device(z=2 * self.z_hi + 1 - self.z_lo)

    def everyone(self):
        ids = [self.other_core()]
        for axis in "xyz":
            ids += [self.along(axis, distance) for distance in (1, 2, 3)]
        return ids


def greet(ids):
    barrier = pltpu.get_barrier_semaphore()
    for device in ids:
        pl.semaphore_signal(barrier, inc=1, device_id=device, device_id_type=MESH)
    pl.semaphore_wait(barrier, len(ids))


class Copies:
    def __init__(self, send_sems, recv_sems, local_sems):
        self.send_sems, self.recv_sems, self.local_sems = send_sems, recv_sems, local_sems
        self.remote, self.local = [], []

    def send(self, source, target, device):
        slot = len(self.remote)
        copy = pltpu.make_async_remote_copy(
            src_ref=source,
            dst_ref=target,
            send_sem=self.send_sems.at[slot],
            recv_sem=self.recv_sems.at[slot],
            device_id=device,
            device_id_type=MESH,
        )
        copy.start()
        self.remote.append(copy)
        return copy

    def move(self, source, target):
        slot = len(self.local)
        copy = pltpu.make_async_copy(source, target, self.local_sems.at[slot])
        copy.start()
        self.local.append(copy)
        return copy

    def drain(self):
        for copy in self.remote:
            copy.wait_send()


def copy_scratch(remote, local):
    return [
        pltpu.SemaphoreType.DMA((remote,)),
        pltpu.SemaphoreType.DMA((remote,)),
        pltpu.SemaphoreType.DMA((max(local, 1),)),
    ]


class Gather:
    def __init__(self, place, copies, source, out, unit, direct):
        self.place, self.copies, self.source, self.out = place, copies, source, out
        self.direct = direct
        _, self.row, self.column, self.order = unit
        self.done = []
        self.to_core = []

    def region(self, half_index, core, **sel):
        lead = [sel.get(axis) for axis in "xy"]
        lead = [slice(None) if index is None else index for index in lead]
        z = sel.get("z")
        start, width = self.column + half_index * 2 * QUARTER, 2 * QUARTER
        z_lo = slice(None)
        if z is not None:
            width = QUARTER
            start = start + lax.div(z, 2) * QUARTER
            z_lo = lax.rem(z, 2)
        core = slice(None) if core is None else core
        rows = pl.ds(self.row, 16)
        return self.out.at[z_lo, lead[0], lead[1], core, rows, pl.ds(pl.multiple_of(start, 128), width)]

    def begin(self):
        place = self.place
        mine = self.column + (place.core * 2 + place.z_hi) * QUARTER
        theirs = self.column + ((1 - place.core) * 2 + place.z_hi) * QUARTER
        mine, theirs = pl.multiple_of(mine, 128), pl.multiple_of(theirs, 128)
        rows = pl.ds(self.row, 16)
        self.first = self.copies.send(
            self.source.at[rows, pl.ds(theirs, QUARTER)],
            self.region(1 - place.core, place.core, **place.at),
            place.other_core(),
        )
        self.own = self.copies.move(
            self.source.at[rows, pl.ds(mine, QUARTER)], self.region(place.core, place.core, **place.at)
        )

    def ready(self):
        self.first.wait_recv()
        self.own.wait()

    def block(self, axis, index, core):
        sel = {a: self.place.at[a] for a in "xyz" if a not in self.done}
        return self.region(self.place.core, core, **{**sel, axis: index})

    def pass_on(self, phase, index, core):
        if phase == 2:
            piece = self.block(self.order[2], index, core)
            self.to_core.append(self.copies.send(piece, piece, self.place.other_core()))

    def start(self, phase):
        axis, place = self.order[phase], self.place
        self.arriving = {}
        if phase in self.direct:
            piece = self.block(axis, place.at[axis], None)
            for distance in (1, 3, 2):
                self.arriving[distance] = self.copies.send(piece, piece, place.along(axis, distance))
            return
        for way, core in ((1, 0), (-1, 1), (1, 1), (-1, 0)):
            piece = self.block(axis, place.at[axis], core)
            self.arriving[way, core] = self.copies.send(piece, piece, place.along(axis, way))
        self.pass_on(phase, place.at[axis], None)

    def forward(self, phase):
        axis, place = self.order[phase], self.place
        self.last = {}
        for way, core in ((1, 0), (-1, 1)):
            self.arriving[way, core].wait_recv()
            piece = self.block(axis, place.step(axis, -way), core)
            self.last[way, core] = self.copies.send(piece, piece, place.along(axis, way))
            self.pass_on(phase, place.step(axis, -way), core)

    def finish(self, phase):
        axis, place = self.order[phase], self.place
        self.done.append(axis)
        if phase in self.direct:
            for copy in self.arriving.values():
                copy.wait_recv()
            return
        self.done.pop()
        for way, core in ((1, 1), (-1, 0)):
            self.arriving[way, core].wait_recv()
            self.pass_on(phase, place.step(axis, -way), core)
        for way, core in ((1, 0), (-1, 1)):
            self.last[way, core].wait_recv()
            self.pass_on(phase, place.step(axis, 2), core)
        self.done.append(axis)


class SmallGather:
    def __init__(self, place, copies, whole):
        self.place, self.copies, self.whole = place, copies, whole
        self.waiting = []

    def arrive(self):
        for copy in self.waiting:
            copy.wait_recv()
        self.waiting = []

    def stage(self, which):
        self.arrive()
        place, whole, send = self.place, self.whole, self.copies.send
        at, core = place.at, place.core
        if which == 0:
            piece = whole.at[core, place.z_lo, at["x"], at["y"]]
            self.waiting = [send(piece, piece, place.along("y", d)) for d in (1, 2, 3)]
        elif which == 1:
            piece = whole.at[core, place.z_lo, at["x"]]
            self.waiting = [send(piece, piece, place.along("x", d)) for d in (1, 2, 3)]
        elif which == 2:
            piece = whole.at[core, place.z_lo]
            self.waiting = [send(piece, piece, place.other_z_lo())]
        else:
            piece = whole.at[core]
            self.waiting = [send(piece, piece, place.other_core())]


def conditioned(ids, class_table, time_weight, labels, sinus, bias):
    def body(row, _):
        core, z_lo = lax.div(row, 32), lax.rem(lax.div(row, 16), 2)
        x, y = lax.rem(lax.div(row, 4), 4), lax.rem(row, 4)
        labels[pl.ds(row, 1), :] = ids[core, z_lo, x, y, 1:2, :]
        for half in range(2):
            sinus[half, pl.ds(row, 1), :] = ids[core, z_lo, x, y, 2 + half : 3 + half, :]
        return 0

    def join(row, _):
        z_lo, x, y = lax.div(row, 16), lax.rem(lax.div(row, 4), 4), lax.rem(row, 4)
        bias[pl.ds(row, 1), :] = ids[0, z_lo, x, y, 0:1, :] + ids[1, z_lo, x, y, 0:1, :]
        return 0

    lax.fori_loop(0, 32, join, 0)

    lax.fori_loop(0, 64, body, 0)
    cond = jnp.zeros((64, 16), F32)
    lane = lax.broadcasted_iota(jnp.int32, (64, 128), 1).astype(F32)
    for start in range(0, CLASSES, 128):
        width = min(128, CLASSES - start)
        chosen = jnp.where(labels[...] == lane + float(start), 1.0, 0.0).astype(BF16)
        cond += lax.dot_general(
            chosen[:, :width], class_table[:, start : start + width], NT, preferred_element_type=F32
        )
    for half in range(2):
        cond += lax.dot_general(
            sinus[half].astype(BF16),
            time_weight[:, half * 128 : half * 128 + 128],
            NT,
            preferred_element_type=F32,
        )
    return cond


def attention_forward(projected, attended, pairs):
    low = lax.broadcasted_iota(jnp.int32, (1, 128), 1) < HEAD

    def body(pair, _):
        def columns(part):
            return pl.ds(pl.multiple_of(part * D + pair * 128, 128), 128)

        query = projected[:HALF, columns(0)] * jnp.asarray(HEAD ** (-0.5), BF16)
        key = projected[:, columns(1)]
        value = projected[:, columns(2)]
        pieces = []
        for mine in (low, jnp.logical_not(low)):
            scores = lax.dot_general(
                jnp.where(mine, query, jnp.zeros((), BF16)), key, NT, preferred_element_type=F32
            )
            terms = jnp.exp(scores - jnp.max(scores, -1, keepdims=True))
            probs = terms * (1.0 / jnp.sum(terms, -1, keepdims=True))
            pieces.append(jnp.dot(probs.astype(BF16), value, preferred_element_type=F32))
        attended[:, columns(0)] = jnp.where(low, *pieces).astype(BF16)
        return 0

    lax.fori_loop(*pairs, body, 0)


def normal_parts(values):
    centre = values - jnp.mean(values, -1, keepdims=True)
    scale = lax.rsqrt(jnp.mean(centre * centre, -1, keepdims=True) + EPSILON)
    return centre * scale, scale


def enter_kernel(
    w0, w1, w2, w3, tokens_in, class_in, time_in, modulate_in, own_ids, placed,
    o0, o1, o2, o3, modulation, labels, sinus, bias, cond, first_in, projected, attended,
    ids, other_tokens, w_attend,
    partial_mod, got_core, sum_core, got_z, slabs, sum_z, got_x, sum_x, got_y, both_first,
    tokens, class_table, time_weight, modulate_weight,
    send_sems, recv_sems, local_sems,
):
    place = Place()
    copies = Copies(send_sems, recv_sems, local_sems)
    sources, wholes = (w0, w1, w2, w3), (o0, o1, o2, o3)
    waves = [
        [
            Gather(place, copies, sources[unit[0]], wholes[unit[0]], unit, (0, 1) if index == 0 else (0,))
            for unit in wave
        ]
        for index, wave in enumerate(WAVES)
    ]
    gathers = [gather for wave in waves for gather in wave]

    def start(wave, phase):
        for gather in waves[wave]:
            gather.start(phase)

    def forward(wave, phase):
        for gather in waves[wave]:
            gather.forward(phase)

    def finish(wave, phase):
        for gather in waves[wave]:
            gather.finish(phase)

    operands = [
        copies.move(source, target)
        for source, target in (
            (class_in, class_table),
            (time_in, time_weight),
            (modulate_in, modulate_weight),
            (tokens_in, tokens),
        )
    ]
    ids[place.core, place.z_lo, place.at["x"], place.at["y"]] = own_ids[...]
    greet(place.everyone())
    id_gather = SmallGather(place, copies, ids)
    id_gather.stage(0)
    for gather in gathers:
        gather.begin()
    tokens_copy = copies.send(tokens_in, other_tokens, place.along("z", 2))
    id_gather.stage(1)
    for gather in gathers:
        gather.ready()
        gather.start(0)
    id_gather.stage(2)
    for wave in range(2):
        finish(wave, 0)
        start(wave, 1)
    id_gather.stage(3)
    for wave in range(2, 4):
        finish(wave, 0)
        start(wave, 1)
    id_gather.arrive()
    finish(0, 1)
    start(0, 2)

    for copy in operands:
        copy.wait()
    cond[...] = conditioned(ids, class_table, time_weight, labels, sinus, bias)
    act = (cond[...] / (1.0 + jnp.exp(-cond[...]))).astype(BF16)
    for column in range(0, 6 * D, D):
        columns = slice(column, column + D)
        partial_mod[:, columns] = (
            jnp.dot(act, modulate_weight[:, columns], preferred_element_type=F32) + placed[:, columns]
        ).astype(BF16)

    def share(index, count):
        return pl.ds(pl.multiple_of(index * count, count), count)

    mod_core = copies.send(partial_mod.at[share(1 - place.core, 32)], got_core, place.other_core())
    for wave in (1, 2, 3):
        forward(wave, 1)
    mod_core.wait_recv()
    sum_core[...] = (
        partial_mod[share(place.core, 32)].astype(F32) + got_core[...].astype(F32)
    ).astype(BF16)
    mod_z = copies.send(sum_core.at[share(1 - place.z_lo, 16)], got_z, place.other_z_lo())
    finish(1, 1)
    start(1, 2)
    mod_z.wait_recv()
    for row in range(48):
        columns = slice(row * 128, row * 128 + 128)
        slabs[:, row, :] = sum_core[share(place.z_lo, 16), columns].astype(F32) + got_z[
            :, columns
        ].astype(F32)
    sum_z[...] = slabs[...].astype(BF16).reshape(4, 4, 48, 128)
    mod_x = [
        copies.send(sum_z.at[place.step("x", distance)], got_x.at[distance - 1], place.along("x", distance))
        for distance in (1, 2, 3)
    ]
    finish(2, 1)
    forward(0, 2)
    start(2, 2)
    for copy in mod_x:
        copy.wait_recv()
    for y in range(4):
        total = sum_z[place.at["x"], y].astype(F32)
        for slot in range(3):
            total += got_x[slot, y].astype(F32)
        sum_x[y] = total.astype(BF16)
    mod_y = [
        copies.send(sum_x.at[place.step("y", distance)], got_y.at[distance - 1], place.along("y", distance))
        for distance in (1, 2, 3)
    ]
    finish(3, 1)
    finish(0, 2)
    for gather in waves[0]:
        for copy in gather.to_core:
            copy.wait_recv()
    weight_copy = copies.move(o0, w_attend)
    forward(1, 2)
    start(3, 2)
    for copy in mod_y:
        copy.wait_recv()
    total = sum_x[place.at["y"]].astype(F32)
    for slot in range(3):
        total += got_y[slot].astype(F32)
    for row in range(48):
        vector, lane = divmod(row, 8)
        modulation[vector : vector + 1, lane * 128 : lane * 128 + 128] = total[row : row + 1]
    tokens_copy.wait_recv()
    for row, source in enumerate((tokens, other_tokens)):
        normal, _ = normal_parts(source[...].astype(F32))
        both_first[row * HALF : row * HALF + HALF] = (
            normal * (1.0 + modulation[1:2]) + modulation[0:1]
        ).astype(BF16)
    first_in[...] = both_first[:HALF]
    forward(2, 2)
    weight_copy.wait()
    for column in range(0, 3 * D, 512):
        columns = slice(column, column + 512)
        projected[:, columns] = jnp.dot(
            both_first[...],
            w_attend[:, :, :, :, :, columns].reshape(D, 512),
            preferred_element_type=F32,
        ).astype(BF16)
    finish(1, 2)
    forward(3, 2)
    attention_forward(projected, attended, (0, HEADS // 4))
    finish(2, 2)
    attention_forward(projected, attended, (HEADS // 4, HEADS // 2))
    finish(3, 2)
    for wave in waves[1:]:
        for gather in wave:
            for copy in gather.to_core:
                copy.wait_recv()
    copies.drain()


def enter(weights, tokens, class_table, time_weight, modulate_weight, own_ids, placed):
    outside = pl.BlockSpec(memory_space=pl.ANY)
    inside = pl.BlockSpec(memory_space=pltpu.VMEM)
    slab = (48, 128)
    shapes = [jax.ShapeDtypeStruct((2, 4, 4, 2, rows, columns), BF16) for rows, columns in WEIGHTS]
    shapes += [
        jax.ShapeDtypeStruct((6, D), F32),
        jax.ShapeDtypeStruct((64, 128), F32),
        jax.ShapeDtypeStruct((2, 64, 128), F32),
        jax.ShapeDtypeStruct((32, 128), F32),
        jax.ShapeDtypeStruct((64, 16), F32),
        jax.ShapeDtypeStruct((HALF, D), BF16),
        jax.ShapeDtypeStruct((SEQ, 3 * D), BF16),
        jax.ShapeDtypeStruct((HALF, D), BF16),
    ]
    out = pl.pallas_call(
        enter_kernel,
        out_shape=shapes,
        in_specs=[outside] * 8 + [inside] * 2,
        out_specs=[outside] * 4 + [inside] * 8,
        scratch_shapes=[
            pltpu.VMEM((2, 2, 4, 4, 8, 128), F32),
            pltpu.VMEM((HALF, D), BF16),
            pltpu.VMEM((2, 4, 4, 2, 16, 3 * D), BF16),
            pltpu.VMEM((64, 6 * D), BF16),
            pltpu.VMEM((32, 6 * D), BF16),
            pltpu.VMEM((32, 6 * D), BF16),
            pltpu.VMEM((16, 6 * D), BF16),
            pltpu.VMEM((16,) + slab, F32),
            pltpu.VMEM((4, 4) + slab, BF16),
            pltpu.VMEM((3, 4) + slab, BF16),
            pltpu.VMEM((4,) + slab, BF16),
            pltpu.VMEM((3,) + slab, BF16),
            pltpu.VMEM((SEQ, D), BF16),
            pltpu.VMEM((HALF, D), BF16),
            pltpu.VMEM((16, CLASSES), BF16),
            pltpu.VMEM((16, FREQ), BF16),
            pltpu.VMEM((16, 6 * D), BF16),
        ]
        + copy_scratch(12 * 23 + 9 + 8, 17),
        compiler_params=pltpu.CompilerParams(
            collective_id=0, has_side_effects=True, vmem_limit_bytes=60 * 2**20
        ),
        name="enter",
    )(*weights, tokens, class_table, time_weight, modulate_weight, own_ids, placed)
    full = [whole.reshape(64 * rows, columns) for whole, (rows, columns) in zip(out[:4], WEIGHTS)]
    return full, out[4:]


class Pair:
    def __init__(self, place, copies, source, both, blocks=None):
        self.copies = []
        other = place.other_core()
        if blocks is None:
            self.copies.append(copies.send(source, both.at[pl.ds(HALF, HALF)], other))
            self.copies.append(copies.move(source, both.at[pl.ds(0, HALF)]))
            return
        for block in range(blocks):
            mine = pl.multiple_of(block * D + place.core * 2 * QUARTER, 128)
            theirs = pl.multiple_of(block * D + (1 - place.core) * 2 * QUARTER, 128)
            width = 2 * QUARTER
            self.copies.append(
                copies.send(source.at[:, pl.ds(theirs, width)], both.at[block, pl.ds(HALF, HALF)], other)
            )
            self.copies.append(
                copies.move(source.at[:, pl.ds(mine, width)], both.at[block, pl.ds(0, HALF)])
            )

    def wait(self):
        for index, copy in enumerate(self.copies):
            if index % 2:
                copy.wait()
            else:
                copy.wait_recv()


def make_parts(left, right, scatters):
    def body(i, _):
        z_lo, x = lax.div(i, 4), lax.rem(i, 4)
        chosen = left[:, pl.ds(pl.multiple_of(i * 128, 128), 128)]
        for scatter in scatters:
            made = lax.dot_general(
                chosen, right[scatter.column // D], TN, preferred_element_type=F32
            ).astype(BF16)
            for q in range(2):
                scatter.parts[2 * q + z_lo, x] = made[:, q * QUARTER : (q + 1) * QUARTER].reshape(
                    4, 2, 16, QUARTER
                )
        return 0

    lax.fori_loop(0, 8, body, 0)


def make_tall_parts(left, right, scatters):
    def body(i, _):
        z_lo, x = lax.div(i, 4), lax.rem(i, 4)
        chosen = left[:, pl.ds(pl.multiple_of(i * 512, 128), 512)]
        made = lax.dot_general(chosen, right[0], TN, preferred_element_type=F32).astype(BF16)
        made = made.reshape(4, 2, 64, 2 * QUARTER)
        for scatter in scatters:
            rows = made[:, :, scatter.row : scatter.row + 16]
            for q in range(2):
                scatter.parts[2 * q + z_lo, x] = rows[..., q * QUARTER : (q + 1) * QUARTER]
        return 0

    lax.fori_loop(0, 8, body, 0)


class Scatter:
    def __init__(self, place, copies, unit, parts, bufs, final, out):
        self.place, self.copies = place, copies
        _, self.row, self.column, order = unit
        self.order = order[::-1]
        self.parts, self.bufs, self.final, self.out = parts, bufs, final, out
        self.done = []

    def sel(self, axis, index):
        at = {a: self.place.at[a] if a in self.done else None for a in "xyz"}
        at[axis] = index
        return [at[a] for a in "zxy"]

    def block(self, axis, index, core):
        lead = [slice(None) if i is None else i for i in self.sel(axis, index)]
        return self.parts.at[(*lead, core)]

    def add(self, axis, index, core, bufs):
        sel = self.sel(axis, index)
        free = [i for i, s in enumerate(sel) if s is None]

        def body(step, _):
            where = [slice(None) if s is None else s for s in sel]
            inner = (slice(None),) * len(free)
            if len(free) == 2:
                where[free[0]], inner = step, (step, slice(None))
            if core is not None:
                where.append(core)
            total = self.parts[tuple(where)].astype(F32)
            for buf in bufs:
                total += buf[inner].astype(F32)
            self.parts[tuple(where)] = total.astype(BF16)
            return 0

        if len(free) == 2:
            lax.fori_loop(0, 4, body, 0)
        else:
            body(0, 0)

    def start(self, phase):
        axis, place = self.order[phase], self.place
        buf = self.bufs[phase]
        send = self.copies.send
        if phase > 0:
            self.direct = [
                send(
                    self.block(axis, place.step(axis, distance), slice(None)),
                    buf.at[distance - 1],
                    place.along(axis, distance),
                )
                for distance in (1, 3, 2)
            ]
            return
        up, down = place.along(axis, 1), place.along(axis, -1)
        far = place.step(axis, 2)
        self.far = {
            1: send(self.block(axis, far, 0), buf.at[0], up),
            -1: send(self.block(axis, far, 1), buf.at[1], down),
        }
        self.raw = {
            1: send(self.block(axis, place.step(axis, 1), 1), buf.at[3], up),
            -1: send(self.block(axis, place.step(axis, -1), 0), buf.at[2], down),
        }

    def forward(self):
        axis, place = self.order[0], self.place
        buf = self.bufs[0]
        self.near = {}
        for way, core in ((1, 0), (-1, 1)):
            self.far[way].wait_recv()
            index = place.step(axis, way)
            self.add(axis, index, core, [buf.at[core]])
            self.near[way] = self.copies.send(
                self.block(axis, index, core), buf.at[4 + core], place.along(axis, way)
            )

    def finish(self, phase):
        axis, place = self.order[phase], self.place
        buf = self.bufs[phase]
        if phase > 0:
            for copy in self.direct:
                copy.wait_recv()
            self.add(axis, place.at[axis], None, [buf.at[slot] for slot in range(3)])
        else:
            for way, core in ((1, 0), (-1, 1)):
                self.raw[-way].wait_recv()
                self.near[way].wait_recv()
                self.add(axis, place.at[axis], core, [buf.at[2 + core], buf.at[4 + core]])
        self.done.append(axis)

    def share(self):
        place, at = self.place, self.place.at
        slot = place.core * 2 + place.z_hi
        mine = self.parts.at[at["z"], at["x"], at["y"], place.core]
        theirs = self.parts.at[at["z"], at["x"], at["y"], 1 - place.core]
        far = place.step("z", 2)
        target = self.final.at[slot]
        self.shared = [
            self.copies.send(theirs, target, place.other_core()),
            self.copies.send(mine, target, place.device(z=far)),
            self.copies.send(theirs, target, place.device(z=far, core=1 - place.core)),
        ]
        self.kept = self.copies.move(mine, target)

    def store(self):
        for copy in self.shared:
            copy.wait_recv()
        self.kept.wait()
        for slot in range(4):
            start = self.column + slot * QUARTER
            self.out[self.row : self.row + 16, start : start + QUARTER] = self.final[slot]


LEFTS = (D, D, D, FF)
BLOCKS = (3, 1, 4, 1)


def attention_back(projected, grad_att, grad_proj, pairs):
    low = lax.broadcasted_iota(jnp.int32, (1, 128), 1) < HEAD

    def body(pair, _):
        def columns(part):
            return pl.ds(pl.multiple_of(part * D + pair * 128, 128), 128)

        query = projected[:, columns(0)] * jnp.asarray(HEAD ** (-0.5), BF16)
        key = projected[:, columns(1)]
        value = projected[:, columns(2)]
        grad = grad_att[:, columns(0)]
        zero = jnp.zeros((), BF16)
        pieces = []
        for mine in (low, jnp.logical_not(low)):
            scores = lax.dot_general(
                jnp.where(mine, query, zero), key, NT, preferred_element_type=F32
            )
            terms = jnp.exp(scores - jnp.max(scores, -1, keepdims=True))
            probs = terms * (1.0 / jnp.sum(terms, -1, keepdims=True))
            grad_probs = lax.dot_general(
                jnp.where(mine, grad, zero), value, NT, preferred_element_type=F32
            )
            inner = jnp.sum(probs * grad_probs, -1, keepdims=True)
            grad_scores = (probs * (grad_probs - inner)).astype(BF16)
            rounded = probs.astype(BF16)
            pieces.append(
                (
                    jnp.dot(grad_scores[:HALF], key, preferred_element_type=F32) * HEAD ** (-0.5),
                    lax.dot_general(grad_scores[:, :HALF], query, TN, preferred_element_type=F32),
                    lax.dot_general(rounded[:, :HALF], grad, TN, preferred_element_type=F32),
                )
            )
        for part in range(3):
            both = jnp.where(low, pieces[0][part], pieces[1][part])
            grad_proj[:, columns(part)] = both.astype(BF16)
        return 0

    lax.fori_loop(*pairs, body, 0)


LEAVE_STEPS = (
    "M3", "S30", "M2", "S20", "A0", "F3", "A1", "F2", "M1", "S10",
    "M0", "S00", "F1", "L", "N30", "S31", "F0", "N20", "S21", "N10",
    "S11", "G0", "N00", "S01", "N31", "S32", "N21", "S22", "N11", "S12",
    "G1", "N01", "S02", "N32", "H3", "N22", "H2", "G2", "N12", "H1",
    "N02", "H0", "G3", "T3", "T2", "T1", "G4", "T0",
)


def leave_kernel(*refs):
    refs = list(refs)

    def take(count):
        taken, refs[:count] = refs[:count], []
        return taken

    lefts_in, rights_in = take(4), take(3)
    w_attend, projected, own_att, tokens, grad_middle, scale_one, sums = take(7)
    outs = take(4)
    whole, tokens_grad = take(2)
    lefts, rights, parts = take(4), take(4), take(12)
    bufs = [take(3) for _ in range(12)]
    finals = take(12)
    weight, both_att, grad_proj, vector, vector_sent, vector_got = take(6)
    send_sems, recv_sems, local_sems = refs
    place = Place()
    copies = Copies(send_sems, recv_sems, local_sems)
    far = place.step("z", 2)
    rights_in = [grad_proj] + rights_in
    greet(place.everyone() + [place.device(z=far, core=1 - place.core)])
    scatters = [
        Scatter(place, copies, UNITS[i], parts[i], bufs[i], finals[i], outs[UNITS[i][0]]) for i in range(12)
    ]

    def of(weight_index, wave=None):
        return [
            scatters[i]
            for i in range(12)
            if UNITS[i][0] == weight_index and wave in (None, i // 3)
        ]

    def start(wave, phase):
        for scatter in scatters[3 * wave : 3 * wave + 3]:
            scatter.start(phase)

    def forward(wave):
        for scatter in scatters[3 * wave : 3 * wave + 3]:
            scatter.forward()

    def finish(wave, phase):
        for scatter in scatters[3 * wave : 3 * wave + 3]:
            scatter.finish(phase)

    def share(wave):
        for scatter in scatters[3 * wave : 3 * wave + 3]:
            scatter.share()

    def store(wave):
        for scatter in scatters[3 * wave : 3 * wave + 3]:
            scatter.store()

    pairs, late, later = {}, [], []

    def begin_pairs(which):
        for i in which:
            pairs[i] = [
                Pair(place, copies, lefts_in[i], lefts[i]),
                Pair(place, copies, rights_in[i], rights[i], BLOCKS[i]),
            ]

    begin_pairs((3,))
    att_copy = copies.send(own_att, both_att.at[pl.ds(HALF, HALF)], place.along("z", 2))
    both_att[:HALF] = own_att[...]

    def meet(pair):
        for half in pair:
            half.wait()

    def make(which):
        if which == 0:
            meet(late)
            make_parts(lefts[0], rights[0], of(0))
        elif which == 3:
            meet(pairs[3])
            begin_pairs((2, 1))
            late.append(Pair(place, copies, lefts_in[0], lefts[0]))
            make_tall_parts(lefts[3], rights[3], of(3))
        elif which == 2:
            meet(pairs[2])
            later.append(copies.move(w_attend, weight))
            make_parts(lefts[2], rights[2], of(2, 2))
        else:
            meet(pairs[1])
            make_parts(lefts[2], rights[2], of(2, 1))
            make_parts(lefts[1], rights[1], of(1))

    def attention(which):
        if which == 0:
            att_copy.wait_recv()
            attention_back(projected, both_att, grad_proj, (0, HEADS // 4))
        else:
            attention_back(projected, both_att, grad_proj, (HEADS // 4, HEADS // 2))
            late.append(Pair(place, copies, grad_proj, rights[0], BLOCKS[0]))

    def input_gradient():
        later[0].wait()
        normal, scale = normal_parts(tokens[...].astype(F32))
        grad_first = jnp.concatenate(
            [
                lax.dot_general(
                    grad_proj[...], weight[start : start + 256], NT, preferred_element_type=F32
                )
                for start in range(0, D, 256)
            ],
            1,
        )
        back = grad_first * (1.0 + scale_one[...])
        tokens_grad[...] = grad_middle[...] + scale * (
            back
            - jnp.mean(back, -1, keepdims=True)
            - normal * jnp.mean(back * normal, -1, keepdims=True)
        )
        vector[...] = sums[...]
        for place_of, total in ((0, grad_first), (8, grad_first * normal)):
            total = jnp.sum(total, 0, keepdims=True)
            for row in range(8):
                vector[place_of + row : place_of + row + 1, :] = total[:, row * 128 : (row + 1) * 128]
        vector_sent[...] = vector[...].astype(BF16)
        later.append(copies.send(vector_sent, vector_got, place.along("z", 2)))

    gather = SmallGather(place, copies, whole)

    def vectors(which):
        if which == 0:
            later[1].wait_recv()
            whole[place.core, place.z_lo, place.at["x"], place.at["y"]] = (
                vector_sent[...].astype(F32) + vector_got[...].astype(F32)
            ).astype(BF16)
        if which < 4:
            gather.stage(which)
        else:
            gather.arrive()

    steps = {
        "M": make,
        "A": attention,
        "L": input_gradient,
        "G": vectors,
        "S": start,
        "F": forward,
        "N": finish,
        "H": share,
        "T": store,
    }
    for step in LEAVE_STEPS:
        steps[step[0]](*(int(number) for number in step[1:]))
    copies.drain()


def buffer_shapes():
    shapes = [(6, 4, 4, 16, QUARTER), (3, 4, 2, 16, QUARTER), (3, 2, 16, QUARTER)]
    return [pltpu.VMEM(shape, BF16) for shape in shapes]


def leave(lefts, rights, w_attend, projected, grad_att, tokens, grad_middle, scale_one, sums):
    outside = pl.BlockSpec(memory_space=pl.ANY)
    inside = pl.BlockSpec(memory_space=pltpu.VMEM)
    scratch = [pltpu.VMEM((SEQ, width), BF16) for width in LEFTS]
    scratch += [pltpu.VMEM((blocks, SEQ, 2 * QUARTER), BF16) for blocks in BLOCKS]
    scratch += [pltpu.VMEM((4, 4, 4, 2, 16, QUARTER), BF16)] * 12
    scratch += buffer_shapes() * 12
    scratch += [pltpu.VMEM((4, 16, QUARTER), BF16)] * 12
    scratch += [
        pltpu.VMEM((D, 3 * D), BF16),
        pltpu.VMEM((SEQ, D), BF16),
        pltpu.VMEM((HALF, 3 * D), BF16),
        pltpu.VMEM(sums.shape, F32),
        pltpu.VMEM(sums.shape, BF16),
        pltpu.VMEM(sums.shape, BF16),
    ]
    scratch += copy_scratch(12 * 15 + 4 + 9 + 10, 4 + 9 + 1 + 12)
    return pl.pallas_call(
        leave_kernel,
        out_shape=[jax.ShapeDtypeStruct((rows, columns), BF16) for rows, columns in WEIGHTS]
        + [jax.ShapeDtypeStruct((2, 2, 4, 4) + sums.shape, BF16), jax.ShapeDtypeStruct((HALF, D), F32)],
        in_specs=[outside] * 8 + [inside] * 6,
        out_specs=[inside] * 6,
        scratch_shapes=scratch,
        compiler_params=pltpu.CompilerParams(
            collective_id=3, has_side_effects=True, vmem_limit_bytes=60 * 2**20
        ),
        name="leave",
    )(*lefts, *rights, w_attend, projected, grad_att, tokens, grad_middle, scale_one, sums)


def normalize(values):
    centre = values - jnp.mean(values, -1, keepdims=True)
    spread = jnp.mean(centre * centre, -1, keepdims=True)
    return centre * lax.rsqrt(spread + EPSILON)


def modulated(values, shift_vec, scale_vec):
    return normalize(values) * (1.0 + scale_vec) + shift_vec


def gelu_tanh(values):
    return jax.nn.gelu(values, approximate=True)


def sinusoid(step_ids):
    half_width = FREQ // 2
    freq_rates = jnp.exp(
        -math.log(10000.0) * jnp.arange(half_width, dtype=jnp.float32) / half_width
    )
    angles = step_ids.astype(jnp.float32)[:, None] * freq_rates[None, :]
    return jnp.concatenate([jnp.cos(angles), jnp.sin(angles)], axis=-1)


def per_device(
    tokens,
    labels,
    timesteps,
    cotangent,
    class_table,
    time_weight,
    modulate_weight,
    modulate_offset,
    attend_weight,
    output_weight,
    expand_weight,
    hidden_offset,
    contract_weight,
):
    shard_index = lax.axis_index("fsdp")
    offset_width = modulate_offset.shape[1]
    placed = lax.dynamic_update_slice(
        jnp.zeros((1, 6 * D), F32),
        modulate_offset.astype(F32),
        (jnp.int32(0), shard_index * offset_width),
    )
    lane = lax.broadcasted_iota(jnp.int32, (1, 128), 1)
    own_bias = jnp.where(
        lax.div(lane, 64) == lax.rem(shard_index, 2), jnp.tile(hidden_offset.astype(F32), (1, 2)), 0.0
    )
    own_ids = jnp.concatenate(
        [
            own_bias,
            jnp.broadcast_to(labels[0].astype(F32), (1, 128)),
            sinusoid(timesteps).astype(BF16).astype(F32).reshape(2, 128),
            jnp.zeros((4, 128), F32),
        ],
        0,
    )
    full, (modulation, labels, sinus, bias, cond_cols, first_in, projected, attended) = enter(
        (attend_weight[0], output_weight[0], expand_weight[0], contract_weight[0]),
        tokens[0],
        class_table.T,
        time_weight.T,
        modulate_weight[0],
        own_ids,
        placed,
    )
    w_attend, w_output, w_expand, w_contract = full
    b_hidden = bias.reshape(FF)
    onehot = labels[:, :1].astype(jnp.int32) == jnp.arange(CLASSES, dtype=jnp.int32)[None, :]
    sinus_rows = jnp.concatenate([sinus[0], sinus[1]], 1)
    act_cols = jax.nn.silu(cond_cols).astype(BF16)
    _, scale_one, gate_one, shift_two, scale_two, gate_two = [modulation[i] for i in range(6)]

    hidden = tokens[0].astype(F32)
    branch_one = jnp.dot(attended, w_output, preferred_element_type=F32)
    middle = hidden + gate_one * branch_one
    second_in = modulated(middle, shift_two, scale_two).astype(BF16)
    pre_act = jnp.dot(second_in, w_expand, preferred_element_type=F32) + b_hidden
    activated = gelu_tanh(pre_act).astype(BF16)
    branch_two = jnp.dot(activated, w_contract, preferred_element_type=F32)
    result = (middle + gate_two * branch_two).astype(BF16)[None]

    grad_hidden = cotangent[0].astype(F32)
    grad_two = (grad_hidden * gate_two).astype(BF16)
    gate_two_grad = jnp.sum(grad_hidden * branch_two, 0)
    grad_act = jnp.einsum("td,fd->tf", grad_two, w_contract, preferred_element_type=F32)
    _, gelu_pull = jax.vjp(gelu_tanh, pre_act)
    grad_pre = gelu_pull(grad_act)[0].astype(BF16)
    hidden_term = jnp.sum(grad_pre.astype(F32), 0)
    grad_second = jnp.einsum("tf,df->td", grad_pre, w_expand, preferred_element_type=F32)
    _, second_pull = jax.vjp(modulated, middle, shift_two, scale_two)
    grad_middle, shift_two_grad, scale_two_grad = second_pull(grad_second)
    grad_middle = grad_hidden + grad_middle
    grad_one = (grad_middle * gate_one).astype(BF16)
    gate_one_grad = jnp.sum(grad_middle * branch_one, 0)
    grad_att = jnp.einsum("te,de->td", grad_one, w_output, preferred_element_type=F32).astype(BF16)
    sums = jnp.concatenate(
        [
            jnp.zeros((2 * D,), F32),
            gate_one_grad,
            shift_two_grad,
            scale_two_grad,
            gate_two_grad,
            hidden_term,
        ]
    ).reshape(80, 128)
    attend_grad, output_grad, expand_grad, contract_grad, all_vectors, tokens_grad = leave(
        (first_in, attended, second_in, activated),
        (grad_one, grad_pre, grad_two),
        w_attend,
        projected,
        grad_att,
        tokens[0],
        grad_middle,
        scale_one[None],
        sums,
    )
    all_vectors = all_vectors.reshape(64, 80 * 128)
    all_mod = all_vectors[:, : 6 * D]
    own_hidden = lax.dynamic_slice_in_dim(all_vectors, 6 * D + shard_index * (FF // 64), FF // 64, 1)
    hidden_grad = jnp.sum(own_hidden.astype(F32), 0)
    grad_act_cols = jnp.einsum("bk,dk->bd", all_mod, modulate_weight[0], preferred_element_type=F32)
    modulate_grad = jnp.einsum("bd,bk->dk", act_cols, all_mod, preferred_element_type=F32)
    own_cols = lax.dynamic_slice_in_dim(all_mod, shard_index * offset_width, offset_width, 1)
    offset_grad = jnp.sum(own_cols.astype(F32), 0)
    _, silu_pull = jax.vjp(jax.nn.silu, cond_cols)
    grad_cond = silu_pull(grad_act_cols)[0]
    table_grad = jnp.einsum("bc,bd->cd", onehot.astype(F32), grad_cond, precision=HIGHEST)
    time_grad = jnp.einsum("bf,bd->fd", sinus_rows, grad_cond, precision=HIGHEST)
    return (
        result,
        tokens_grad[None],
        table_grad,
        time_grad,
        modulate_grad[None],
        offset_grad[None],
        attend_grad.astype(F32)[None],
        output_grad.astype(F32)[None],
        expand_grad.astype(F32)[None],
        hidden_grad[None],
        contract_grad.astype(F32)[None],
    )


def solution(mesh):
    rows = P(None, "fsdp", None)
    columns = P(None, "fsdp")
    halves = P("fsdp", "ctx", None)
    each = P("fsdp")
    in_specs = (
        halves, each, each, halves, columns, columns, rows, columns, rows, rows, rows, columns, rows,
    )
    out_specs = (
        halves, halves, columns, columns, rows, columns, rows, rows, rows, columns, rows,
    )
    return jax.shard_map(
        per_device, mesh=mesh, in_specs=in_specs, out_specs=out_specs, check_vma=False
    )
```
